256 devices in a mesh: fact: 8 (over z), dim: 32 (over y, x, core).
Axes of the slice: x: 4, y: 4, z: 8, core: 2. Of those that a mesh axis runs over, the one named last changes fastest.
Arguments:
- facts: bfloat16 [32768, 512], P(('fact', 'dim')), may hold values from -6 to 6
- dims: bfloat16 [32768, 512], P(('fact', 'dim')), may hold values from -6 to 6
- tiles: bfloat16 [8192, 128, 128], P(('fact', 'dim')), may hold values from -0.125 to 0.125
- links: int32 [8192, 2], P(('fact', 'dim')), may hold values from 0 to 255, as said below
- link_count: int32 [256], P(('fact', 'dim')), may hold values from 8 to 32, as said below
- block_table: int32 [256], replicated, may hold values from 0 to 2
- w_self: bfloat16 [512, 512], replicated, may hold values from -0.25 to 0.25
- w_tables: bfloat16 [3, 512, 512], replicated, may hold values from -0.25 to 0.25
- cot: bfloat16 [32768, 512], P(('fact', 'dim')), may hold values from -6 to 6
Outputs:
- fact_out: bfloat16 [32768, 512], P(('fact', 'dim'))
- grad_dims: float32 [32768, 512], P(('fact', 'dim'))
- grad_w_self: float32 [512, 512], replicated
- grad_w_tables: float32 [3, 512, 512], replicated
The draws below stay inside these ranges and needn't reach their ends.
Inputs may be any that keep to these rules, and one draw needn't show every extreme that they name: On device k = f * 32 + d (f, d its fact and dim indices), links[l,0] is a fact block among those of rows f * 128 * 32 to (f + 1) * 128 * 32 - 1, and links[l,1] is a dimension block held by a device with dim index d, i.e. links[l,1] % 32 == d. Slots beyond the device's count hold such indices too and are padding. `link_count`: some device has all 32 slots live and some device exactly 8.
All inputs are finite; a program needn't handle non-finite values.
Results may differ from the reference program's by a relative error of at most 0.017.
Values may be sent and summed in bfloat16 or wider, within the bound.
No kernel may reach another device: no remote copies, remote signals or barrier semaphores. Data moves between devices by JAX's collectives and lax.ppermute only.
A program may use at most 64 MiB of HBM per device.

```python
import jax
import jax.numpy as jnp
from jax import lax

D = 512
TABLES = 3
BLOCK = 128
FACT_DEV = 128
DIM_DEV = 128
LINKS_DEV = 32
NF = 32768
ND = 32768
LINKS = 8192
DBLOCKS = 256
N_FACT = 8
N_DIM = 32


def draw_links(key, part):
    devices = N_FACT * N_DIM
    first, second, third = jax.random.split(key, 3)
    device = jnp.arange(devices, dtype=jnp.int32)
    fact_index = device // N_DIM
    dim_index = device % N_DIM
    fact_blocks = FACT_DEV * N_DIM // BLOCK
    per_owner = DIM_DEV // BLOCK
    fact_off = jax.random.randint(first, (devices, LINKS_DEV), 0, fact_blocks)
    holder = jax.random.randint(second, (devices, LINKS_DEV), 0, N_FACT)
    within = jax.random.randint(third, (devices, LINKS_DEV), 0, per_owner)
    slot = jnp.arange(LINKS_DEV, dtype=jnp.int32)
    first_dev = (device[:, None] == 0) & (slot[None, :] == 0)
    last_dev = (device[:, None] == devices - 1) & (slot[None, :] == 0)
    fact_off = jnp.where(first_dev, 0, jnp.where(last_dev, fact_blocks - 1, fact_off))
    holder = jnp.where(first_dev, 0, jnp.where(last_dev, N_FACT - 1, holder))
    within = jnp.where(first_dev, 0, jnp.where(last_dev, per_owner - 1, within))
    fact_blk = fact_index[:, None] * fact_blocks + fact_off
    dim_blk = (holder * N_DIM + dim_index[:, None]) * per_owner + within
    return jnp.stack([fact_blk, dim_blk], axis=-1).reshape(devices * LINKS_DEV, 2).astype(jnp.int32)


def draw_link_count(key, part):
    devices = N_FACT * N_DIM
    first, second, third = jax.random.split(key, 3)
    lowest = LINKS_DEV // 4
    counts = jax.random.randint(first, (devices,), lowest, LINKS_DEV + 1)
    busiest = jax.random.randint(second, (), 0, devices)
    lightest = (busiest + 1 + jax.random.randint(third, (), 0, devices - 1)) % devices
    device = jnp.arange(devices, dtype=jnp.int32)
    counts = jnp.where(device == busiest, LINKS_DEV, counts)
    counts = jnp.where(device == lightest, lowest, counts)
    return counts.astype(jnp.int32)


def place_ends(values, key, least, largest):
    shape = values.shape
    index_at = [jax.random.randint(jax.random.fold_in(key, axis), (), 0, shape[axis]) for axis in range(len(shape))]
    values = values.at[tuple(index_at)].set(least)
    longest = shape.index(max(shape))
    index_at[longest] = (index_at[longest] + 1) % shape[longest]
    return values.at[tuple(index_at)].set(largest)


def level_of(rng, shape, cuts, low, top_value):
    loudness, own = 1.0, jax.random.fold_in(rng, 6)
    for position, blocks in cuts:
        heights = jnp.exp(jax.random.uniform(jax.random.fold_in(own, position), (blocks,), jnp.float32, low / len(cuts), top_value / len(cuts)))
        loudness = loudness * jnp.repeat(heights, shape[position] // blocks).reshape([-1 if axis == position else 1 for axis in range(len(shape))])
    return loudness


def centred(rng, shape, spread, most, cuts=(), held_as=jnp.bfloat16):
    loudness = level_of(rng, shape, cuts, -0.22, 0.18) if cuts else 1.0
    entries = jax.random.normal(rng, shape, jnp.float32) * spread * loudness
    return jnp.minimum(jnp.maximum(entries, -most), most).astype(held_as)


def setup_inputs(seed: int = 0) -> dict:
    streams_of = jax.random.split(jax.random.key(seed), 10)
    facts = centred(streams_of[0], (NF, D), 1.0, 6.0, ((0, 256),))
    dims = centred(streams_of[1], (ND, D), 1.0, 6.0, ((0, 256),))
    tiles = centred(streams_of[2], (LINKS, BLOCK, BLOCK), (5 * LINKS_DEV * BLOCK * BLOCK // (8 * FACT_DEV)) ** -0.5, 0.125, ((0, 256),))
    links = draw_links(jax.random.fold_in(streams_of[9], 71), 0)
    link_count = draw_link_count(jax.random.fold_in(streams_of[9], 71), 0)
    block_table = place_ends(jax.random.randint(streams_of[5], (DBLOCKS,), 0, TABLES), jax.random.fold_in(streams_of[5], 1), 0, TABLES - 1).astype(jnp.int32)
    w_self = centred(streams_of[6], (D, D), D ** -0.5, 0.25)
    w_tables = centred(streams_of[7], (TABLES, D, D), D ** -0.5, 0.25)
    cot = centred(streams_of[8], (NF, D), 1.0, 6.0, ((0, 256),))
    return dict(facts=facts, dims=dims, tiles=tiles, links=links, link_count=link_count, block_table=block_table, w_self=w_self, w_tables=w_tables, cot=cot)


def project_rows(rows, row_table, w_tables):
    acc = jnp.zeros((rows.shape[0], w_tables.shape[2]), jnp.float32)
    for table in range(TABLES):
        term = jnp.dot(rows, w_tables[table], preferred_element_type=jnp.float32)
        acc = acc + jnp.where(row_table[:, None] == table, term, jnp.float32(0.0))
    return acc


def reference(facts, dims, tiles, links, link_count, block_table, w_self, w_tables, cot):
    devices = N_FACT * N_DIM
    row_table = jnp.repeat(block_table, BLOCK)
    projected = project_rows(dims, row_table, w_tables).astype(jnp.bfloat16)
    slot = jnp.arange(LINKS, dtype=jnp.int32) % LINKS_DEV
    owner = jnp.arange(LINKS, dtype=jnp.int32) // LINKS_DEV
    live = (slot < link_count[owner]).astype(jnp.float32).reshape(devices, LINKS_DEV)
    tile_dev = tiles.reshape(devices, LINKS_DEV, BLOCK, BLOCK)
    link_dev = links.reshape(devices, LINKS_DEV, 2)
    proj_blocks = projected.reshape(ND // BLOCK, BLOCK, D)

    def forward_step(acc, xs):
        tile, link, alive = xs
        blocks = proj_blocks[link[:, 1]].astype(jnp.float32)
        contrib = jnp.einsum('lij,ljd->lid', tile.astype(jnp.float32), blocks) * alive[:, None, None]
        return acc.at[link[:, 0]].add(contrib), None

    agg, _ = lax.scan(forward_step, jnp.zeros((NF // BLOCK, BLOCK, D), jnp.float32), (tile_dev, link_dev, live))
    pre = jnp.dot(facts, w_self, preferred_element_type=jnp.float32) + agg.reshape(NF, D)
    fact_out = jax.nn.silu(pre).astype(jnp.bfloat16)
    sig = jax.nn.sigmoid(pre)
    grad_pre = (cot.astype(jnp.float32) * sig * (1.0 + pre * (1.0 - sig))).astype(jnp.bfloat16)
    grad_w_self = lax.dot_general(facts, grad_pre, (((0,), (0,)), ((), ())), preferred_element_type=jnp.float32) * (NF ** -0.5)
    grad_blocks = grad_pre.reshape(NF // BLOCK, BLOCK, D)

    def backward_step(acc, xs):
        tile, link, alive = xs
        blocks = grad_blocks[link[:, 0]].astype(jnp.float32)
        contrib = jnp.einsum('lji,ljd->lid', tile.astype(jnp.float32), blocks) * alive[:, None, None]
        return acc.at[link[:, 1]].add(contrib), None

    gsum, _ = lax.scan(backward_step, jnp.zeros((ND // BLOCK, BLOCK, D), jnp.float32), (tile_dev, link_dev, live))
    gsum_b = gsum.reshape(ND, D).astype(jnp.bfloat16)
    grad_dims = jnp.zeros((ND, D), jnp.float32)
    grads = []
    for table in range(TABLES):
        term = lax.dot_general(gsum_b, w_tables[table], (((1,), (1,)), ((), ())), preferred_element_type=jnp.float32)
        grad_dims = grad_dims + jnp.where(row_table[:, None] == table, term, jnp.float32(0.0))
        masked = jnp.where(row_table[:, None] == table, dims, jnp.zeros_like(dims))
        grads.append(lax.dot_general(masked, gsum_b, (((0,), (0,)), ((), ())), preferred_element_type=jnp.float32) * (ND ** -0.5))
    grad_w_tables = jnp.stack(grads)
    return (fact_out, grad_dims, grad_w_self, grad_w_tables)
```

```python
import jax
import jax.numpy as jnp
from jax import lax
from jax.experimental import pallas as pl
from jax.experimental.pallas import tpu as pltpu
from jax.sharding import PartitionSpec as P

F32 = jnp.float32
BF16 = jnp.bfloat16
VMEM = pl.BlockSpec(memory_space=pltpu.VMEM)
SMEM = pl.BlockSpec(memory_space=pltpu.SMEM)
PARAMS = pltpu.CompilerParams(vmem_limit_bytes=48 * 1024 * 1024)


def call(kernel, out_shape, in_specs, scratch=(), flops=0, moved=0):
    return pl.pallas_call(
        kernel,
        out_shape=out_shape,
        in_specs=in_specs,
        out_specs=jax.tree.map(lambda _: VMEM, out_shape),
        scratch_shapes=list(scratch),
        compiler_params=PARAMS,
        cost_estimate=pl.CostEstimate(flops=flops, bytes_accessed=moved, transcendentals=0),
    )


def forward_kernel(place, links_own, links_sib, table, dims_own, dims_sib, w, tiles_own, tiles_sib, out, proj, acc):
    dim_pos, core = place[1], place[2]
    holders, n_dim = dims_own.shape[0], table.shape[0] // dims_own.shape[0]
    sides = ((dims_own, links_own, tiles_own, dim_pos), (dims_sib, links_sib, tiles_sib, dim_pos + 1 - 2 * core))
    for side, (dims, _, _, column) in enumerate(sides):
        for h in range(holders):
            kind = table[h * n_dim + column]
            proj[side * holders + h] = jnp.dot(dims[h], w[kind], preferred_element_type=F32).astype(BF16)
    acc[...] = jnp.zeros_like(acc)
    for side, (_, links, tiles, _) in enumerate(sides):

        def step(slot, carry, side=side, links=links, tiles=tiles):
            target, holder = links[2 * slot], links[2 * slot + 1]

            @pl.when(lax.rem(target, 2) == core)
            def _():
                chip = lax.div(target, 2)
                acc[chip] += jnp.dot(tiles[slot], proj[side * holders + holder], preferred_element_type=F32)

            return carry

        lax.fori_loop(0, tiles.shape[0], step, 0)
    out[...] = acc[...].astype(BF16)


def middle_kernel(parts, facts, w, cot, fact_out, spread):
    pre = jnp.dot(facts[...], w[...], preferred_element_type=F32)
    agg = parts[0].astype(F32)
    for chip in range(1, parts.shape[0]):
        agg = agg + parts[chip].astype(F32)
    pre = pre + agg
    sig = jax.nn.sigmoid(pre)
    fact_out[...] = (pre * sig).astype(BF16)
    grad = cot[...].astype(F32) * sig * (1.0 + pre * (1.0 - sig))
    turned = grad.T.astype(BF16)
    for chip in range(spread.shape[0]):
        spread[chip] = turned


def backward_kernel(place, links_own, links_sib, grads, facts, tiles_own, tiles_sib, own, sib, acc, weight):
    core, chip_pos = place[2], place[3]
    holders = acc.shape[0] // 2
    acc[...] = jnp.zeros_like(acc)
    for side, (links, tiles) in enumerate(((links_own, tiles_own), (links_sib, tiles_sib))):

        def step(slot, carry, side=side, links=links, tiles=tiles):
            target, holder = links[2 * slot], links[2 * slot + 1]

            @pl.when(lax.rem(target, 2) == core)
            def _():
                at = side * holders + holder
                acc[at] += jnp.dot(grads[lax.div(target, 2)], tiles[slot], preferred_element_type=F32)

            return carry

        lax.fori_loop(0, tiles.shape[0], step, 0)
    chips = grads.shape[0]
    piece = weight.shape[0]
    half = piece // 2
    first = pl.multiple_of(chip_pos * piece, piece)
    total = jnp.zeros(weight.shape, F32)
    for chip in range(chips):
        total = total + jnp.dot(grads[chip, pl.ds(first, piece), :], facts[chip], preferred_element_type=F32)
    weight[...] = total
    for out, base, row, kind in ((own, 0, core * half, F32), (sib, holders, (1 - core) * half, BF16)):
        for z in range(8):
            for h in range(holders):
                out[z, h * 64 : (h + 1) * 64, :] = acc[base + h, z * 64 : (z + 1) * 64, :].astype(kind)
            rows = pl.ds(pl.multiple_of(row + (z % 2) * 8, 8), 8)
            mine = weight[rows, (z // 2) * 128 : (z // 2 + 1) * 128]
            out[z, 512:528, :] = jnp.concatenate([mine, jnp.zeros_like(mine)], axis=0).astype(kind)


def slice_kernel(place, table, parts, dims, tab, gsum, self_piece, tacc):
    dim_pos = place[1]
    holders = dims.shape[0]
    n_dim = table.shape[0] // holders
    total = parts[0].astype(F32)
    for z in range(1, parts.shape[0]):
        total = total + parts[z].astype(F32)
    self_piece[...] = total[512:520]
    tacc[...] = jnp.zeros_like(tacc)
    for h in range(holders):
        rounded = total[h * 64 : (h + 1) * 64].astype(BF16)
        gsum[h] = rounded
        kind = table[h * n_dim + dim_pos]
        tacc[kind] += jnp.dot(rounded, dims[h], preferred_element_type=F32)
    for q in range(4):
        for t in range(3):
            at = q * 192 + t * 64
            tab[at : at + 64, :] = tacc[t, :, q * 128 : (q + 1) * 128].astype(BF16)


def pack_kernel(parts, gsum, self_piece, out):
    total = jnp.sum(parts[...].astype(F32), axis=0)
    piece = jnp.concatenate([total, self_piece[...]], axis=0).astype(BF16)
    for z in range(out.shape[0]):
        out[z, 0:64, :] = gsum[z]
        out[z, 64:96, :] = piece


def final_kernel(place, own, sib, grad_self, grad_tab):
    even = place[2] == 0
    scale = F32(32768.0**-0.5)

    def block(d, z):
        mine, other = own[d // 2, z].astype(F32), sib[d // 2, z].astype(F32)
        return jnp.where(even, mine, other) if d % 2 == 0 else jnp.where(even, other, mine)

    for q in range(4):
        rows = []
        for pair in range(4):
            halves = []
            for z in (2 * pair, 2 * pair + 1):
                parts = [block(d, z)[0:24] for d in range(8 * q, 8 * q + 8)]
                halves.append(jnp.concatenate(parts, axis=0))
            for t in range(3):
                both = jnp.concatenate([x[t * 64 : (t + 1) * 64] for x in halves], axis=0)
                grad_tab[t, q * 128 : (q + 1) * 128, pair * 128 : (pair + 1) * 128] = both.T * scale
        for d in range(32):
            rows += [block(d, 2 * q)[24:32], block(d, 2 * q + 1)[24:32]]
        for part in range(4):
            both = jnp.concatenate(rows[part * 16 : (part + 1) * 16], axis=0)
            grad_self[q * 128 : (q + 1) * 128, part * 128 : (part + 1) * 128] = both.T * scale


def body(facts, dims, tiles, links, link_count, block_table, w_self, w_tables, cot):
    n_fact = lax.axis_size("fact")
    n_dim = lax.axis_size("dim")
    fact_pos = lax.axis_index("fact")
    dim_pos = lax.axis_index("dim")
    chips = n_dim // 2
    same = [[2 * m + core for m in range(chips)] for core in range(2)]
    pair = [(d, d ^ 1) for d in range(n_dim)]
    rows, width = dims.shape
    slots, block, _ = tiles.shape
    place = jnp.stack([fact_pos, dim_pos, dim_pos % 2, dim_pos // 2]).astype(jnp.int32)

    def swap(x):
        return lax.ppermute(x, "dim", pair)

    def by_chip(x):
        return lax.all_to_all(x, "dim", 0, 0, tiled=True, axis_index_groups=same)

    def by_fact(x):
        return lax.all_to_all(x, "fact", 0, 0, tiled=True)

    live = jnp.arange(slots, dtype=jnp.int32) < link_count[0]
    target = jnp.where(live, links[:, 0] - fact_pos * n_dim, -1)
    links_own = jnp.stack([target, links[:, 1] // n_dim], axis=1).reshape(-1)
    links_sib = swap(links_own)
    tiles_sib = swap(tiles)
    facts_all = lax.all_gather(facts, "dim", axis=0, axis_index_groups=same)
    dims_own = by_fact(jnp.broadcast_to(dims[None], (n_fact, rows, width)))
    dims_sib = swap(dims_own)

    partial = call(
        forward_kernel,
        jax.ShapeDtypeStruct((chips, block, width), BF16),
        [SMEM] * 4 + [VMEM] * 5,
        [pltpu.VMEM((2 * n_fact, rows, width), BF16), pltpu.VMEM((chips, block, width), F32)],
        flops=2 * slots * block * block * width + 4 * n_fact * rows * width * width,
        moved=8 << 20,
    )(place, links_own, links_sib, block_table, dims_own, dims_sib, w_tables, tiles, tiles_sib)
    parts = by_chip(partial)

    fact_out, spread = call(
        middle_kernel,
        (jax.ShapeDtypeStruct((block, width), BF16), jax.ShapeDtypeStruct((chips, width, block), BF16)),
        [VMEM] * 4,
        flops=2 * block * width * width,
        moved=5 << 20,
    )(parts, facts, w_self, cot)
    grads = by_chip(spread)

    own, sib = call(
        backward_kernel,
        (jax.ShapeDtypeStruct((n_fact, 528, 128), F32), jax.ShapeDtypeStruct((n_fact, 528, 128), BF16)),
        [SMEM] * 3 + [VMEM] * 4,
        [pltpu.VMEM((2 * n_fact, width, block), F32), pltpu.VMEM((width // chips, width), F32)],
        flops=2 * slots * block * block * width,
        moved=9 << 20,
    )(place, links_own, links_sib, grads, facts_all, tiles, tiles_sib)
    slices = by_fact((own + swap(sib).astype(F32)).astype(BF16))

    tab, gsum, self_piece = call(
        slice_kernel,
        (
            jax.ShapeDtypeStruct((768, 128), BF16),
            jax.ShapeDtypeStruct((n_fact, 64, 128), BF16),
            jax.ShapeDtypeStruct((8, 128), F32),
        ),
        [SMEM] * 2 + [VMEM] * 2,
        [pltpu.VMEM((3, 64, width), F32)],
        flops=2 * n_fact * 64 * 128 * width,
        moved=3 << 20,
    )(place, block_table, slices, dims_own)
    tab = lax.all_to_all(tab.reshape(n_dim, 24, 128), "dim", 0, 0, tiled=True)
    packed = call(
        pack_kernel, jax.ShapeDtypeStruct((n_fact, 96, 128), BF16), [VMEM] * 3, moved=1 << 19
    )(tab, gsum, self_piece)
    packed = by_fact(packed)
    pieces_own = by_chip(jnp.broadcast_to(packed[None, :, 64:, :], (chips, n_fact, 32, 128)))
    pieces_sib = swap(pieces_own)

    turned = packed[:, :64, :].reshape(width, rows)
    kind = lax.dynamic_index_in_dim(block_table, fact_pos * n_dim + dim_pos, keepdims=False)
    weight = lax.dynamic_index_in_dim(w_tables, kind, keepdims=False)
    grad_dims = lax.dot_general(turned, weight, (((0,), (1,)), ((), ())), preferred_element_type=F32)

    grad_self, grad_tab = call(
        final_kernel,
        (jax.ShapeDtypeStruct((width, width), F32), jax.ShapeDtypeStruct((3, width, width), F32)),
        [SMEM] + [VMEM] * 2,
        moved=6 << 20,
    )(place, pieces_own, pieces_sib)
    return (fact_out, grad_dims, grad_self, grad_tab)


def solution(mesh):
    split = P(("fact", "dim"), None)
    return jax.shard_map(
        body,
        mesh=mesh,
        in_specs=(split, split, P(("fact", "dim"), None, None), split, P(("fact", "dim")), P(), P(), P(), split),
        out_specs=(split, split, P(), P()),
        check_vma=False,
    )
```

```python
import jax
import jax.numpy as jnp
from jax import lax
from jax.experimental import pallas as pl
from jax.experimental.pallas import tpu as pltpu
from jax.sharding import PartitionSpec as P

F32 = jnp.float32
BF16 = jnp.bfloat16
VMEM = pl.BlockSpec(memory_space=pltpu.VMEM)
SMEM = pl.BlockSpec(memory_space=pltpu.SMEM)
PARAMS = pltpu.CompilerParams(vmem_limit_bytes=24 * 1024 * 1024)
UNROLL = 2


def call(kernel, out_shape, in_specs, scratch=(), flops=0, moved=0):
    return pl.pallas_call(
        kernel,
        out_shape=out_shape,
        in_specs=in_specs,
        out_specs=jax.tree.map(lambda _: VMEM, out_shape),
        scratch_shapes=list(scratch),
        compiler_params=PARAMS,
        cost_estimate=pl.CostEstimate(flops=flops, bytes_accessed=moved, transcendentals=0),
    )


def project_kernel(place, table, dims, w, out):
    out[...] = jnp.dot(dims[...], w[0], preferred_element_type=F32).astype(BF16)


def project(place, table, dims, w):
    rows, width = dims.shape
    n_dim = table.shape[0] // 8
    return pl.pallas_call(
        project_kernel,
        out_shape=jax.ShapeDtypeStruct((rows, width), BF16),
        grid_spec=pltpu.PrefetchScalarGridSpec(
            num_scalar_prefetch=2,
            grid=(1,),
            in_specs=[
                pl.BlockSpec((rows, width), lambda i, place, table: (0, 0)),
                pl.BlockSpec((1, width, width), lambda i, place, table: (table[place[0] * n_dim + place[1]], 0, 0)),
            ],
            out_specs=pl.BlockSpec((rows, width), lambda i, place, table: (0, 0)),
        ),
        compiler_params=PARAMS,
        cost_estimate=pl.CostEstimate(flops=2 * rows * width * width, bytes_accessed=1 << 20, transcendentals=0),
    )(place, table, dims, w)


def decode(code):
    return code & 31, (code >> 5) & 7, code >> 8


def forward_kernel(place, lists, counts, *refs):
    panels, (facts_t, tiles_own, tiles_sib, out, panel, acc) = (refs[:9], refs[9:18]), refs[18:]
    fact_pos = place[0]
    half = panels[0][7].shape[0]
    for side in range(2):
        for at, shift in enumerate((0, -1, 1, -2, 2, -3, 3)):
            panel[side * 8 + ((fact_pos + shift) & 7)] = panels[side][at][...]
        far = side * 8 + ((fact_pos + 4) & 7)
        panel[far, 0:half, :] = panels[side][7][...]
        panel[far, half : 2 * half, :] = panels[side][8][...]
    acc[...] = jnp.zeros_like(acc)
    for side, tiles in enumerate((tiles_own, tiles_sib)):

        def step(i, carry, side=side, tiles=tiles):
            found = []
            for u in range(UNROLL):
                slot, holder, chip = decode(lists[side * 32 + i * UNROLL + u])
                found.append((chip, jnp.dot(tiles[slot], panel[side * 8 + holder], preferred_element_type=F32)))
            for chip, value in found:
                acc[chip] += value
            return carry

        lax.fori_loop(0, (counts[side] + UNROLL - 1) // UNROLL, step, 0)
    for chip in range(out.shape[0]):
        for q in range(4):
            out[chip, q * 128 : (q + 1) * 128, :] = acc[chip, :, q * 128 : (q + 1) * 128].astype(BF16)
        out[chip, 512:544, :] = facts_t[chip]


def middle_kernel(parts, facts, w, cot, fact_out, spread, facts_t):
    pre = jnp.dot(facts[...], w[...], preferred_element_type=F32)
    aggs = []
    for q in range(4):
        agg = parts[0, q * 128 : (q + 1) * 128, :].astype(F32)
        for chip in range(1, parts.shape[0]):
            agg = agg + parts[chip, q * 128 : (q + 1) * 128, :].astype(F32)
        aggs.append(agg)
    pre = pre + jnp.concatenate(aggs, axis=1)
    sig = jax.nn.sigmoid(pre)
    fact_out[...] = (pre * sig).astype(BF16)
    grad = cot[...].astype(F32) * sig * (1.0 + pre * (1.0 - sig))
    turned = grad.T.astype(BF16)
    for chip in range(spread.shape[0]):
        spread[chip] = turned
        facts_t[chip] = parts[chip, 512:544, :]


def backward_kernel(place, lists, counts, grads, facts_t, tiles_own, tiles_sib, own, sib, acc, weight):
    core = place[2]
    holders = 8
    acc[...] = jnp.zeros_like(acc)
    for side, tiles in enumerate((tiles_own, tiles_sib)):

        def step(i, carry, side=side, tiles=tiles):
            found = []
            for u in range(UNROLL):
                slot, holder, chip = decode(lists[side * 32 + i * UNROLL + u])
                at = jnp.where(chip == 16, 16, side * holders + holder)
                value = jnp.dot(grads[jnp.minimum(chip, 15)], tiles[slot], preferred_element_type=F32)
                found.append((at, value))
            for at, value in found:
                acc[at] += value
            return carry

        lax.fori_loop(0, (counts[side] + UNROLL - 1) // UNROLL, step, 0)
    half = weight.shape[0] // 2
    total = jnp.zeros(weight.shape, F32)
    for chip in range(grads.shape[0]):
        total = total + lax.dot_general(
            facts_t[chip], grads[chip], (((1,), (1,)), ((), ())), preferred_element_type=F32
        )
    weight[...] = total
    for out, base, row, kind in ((own, 0, core * half, F32), (sib, holders, (1 - core) * half, BF16)):
        for z in range(8):
            for h in range(holders):
                out[z, h * 64 : (h + 1) * 64, :] = acc[base + h, z * 64 : (z + 1) * 64, :].astype(kind)
            rows = pl.ds(pl.multiple_of(row + (z % 2) * 8, 8), 8)
            mine = weight[rows, (z // 2) * 128 : (z // 2 + 1) * 128]
            out[z, 512:528, :] = jnp.concatenate([mine, jnp.zeros_like(mine)], axis=0).astype(kind)


def slice_kernel(place, table, parts, dims, tab, gsum, self_piece, tacc):
    dim_pos = place[1]
    holders = dims.shape[0]
    n_dim = table.shape[0] // holders
    total = parts[0].astype(F32)
    for z in range(1, parts.shape[0]):
        total = total + parts[z].astype(F32)
    self_piece[...] = total[512:520]
    tacc[...] = jnp.zeros_like(tacc)
    for h in range(holders):
        rounded = total[h * 64 : (h + 1) * 64].astype(BF16)
        gsum[h] = rounded
        kind = table[h * n_dim + dim_pos]
        tacc[kind] += jnp.dot(rounded, dims[h], preferred_element_type=F32)
    for q in range(4):
        for t in range(3):
            at = q * 192 + t * 64
            tab[at : at + 64, :] = tacc[t, :, q * 128 : (q + 1) * 128].astype(BF16)


def pack_kernel(parts, gsum, self_piece, out):
    total = jnp.sum(parts[...].astype(F32), axis=0)
    piece = jnp.concatenate([total, self_piece[...]], axis=0).astype(BF16)
    for z in range(out.shape[0]):
        out[z, 0:64, :] = gsum[z]
        out[z, 64:96, :] = piece


def final_kernel(place, table, own, sib, packed, w, grad_dims, grad_self, grad_tab):
    even = place[2] == 0
    scale = F32(32768.0**-0.5)
    kind = table[place[0] * 32 + place[1]]
    turned = packed[:, 0:64, :].astype(F32).reshape(512, 128)
    grad_dims[...] = lax.dot_general(
        turned.T.astype(BF16), w[kind], (((1,), (1,)), ((), ())), preferred_element_type=F32
    )

    def block(d, z):
        mine, other = own[d // 2, z].astype(F32), sib[d // 2, z].astype(F32)
        return (jnp.where(even, mine, other) if d % 2 == 0 else jnp.where(even, other, mine)) * scale

    for q in range(4):
        for pair in range(4):
            halves = []
            for z in (2 * pair, 2 * pair + 1):
                every = [block(d, z) for d in range(8 * q, 8 * q + 8)]
                halves.append(jnp.concatenate([x[0:24] for x in every], axis=0))
                for at, x in enumerate(every):
                    row = (8 * q + at) * 16 + (z % 2) * 8
                    grad_self[row : row + 8, pair * 128 : (pair + 1) * 128] = x[24:32]
            for t in range(3):
                both = jnp.concatenate([x[t * 64 : (t + 1) * 64] for x in halves], axis=0)
                grad_tab[t, q * 128 : (q + 1) * 128, pair * 128 : (pair + 1) * 128] = both.T


def compact(codes, active):
    at = jnp.arange(codes.shape[0], dtype=jnp.int32)
    place_of = jnp.sum(jnp.where(active[None, :] & (at[None, :] < at[:, None]), 1, 0), axis=1)
    hit = active[:, None] & (place_of[:, None] == at[None, :])
    listed = jnp.sum(jnp.where(hit, codes[:, None] - (16 << 8), 0), axis=0) + (16 << 8)
    return listed, jnp.sum(active.astype(jnp.int32))


def body(facts, dims, tiles, links, link_count, block_table, w_self, w_tables, cot):
    n_fact = lax.axis_size("fact")
    n_dim = lax.axis_size("dim")
    fact_pos = lax.axis_index("fact")
    dim_pos = lax.axis_index("dim")
    chips = n_dim // 2
    same = [[2 * m + core for m in range(chips)] for core in range(2)]
    pair = [(d, d ^ 1) for d in range(n_dim)]
    rows, width = dims.shape
    slots, block, _ = tiles.shape
    core = dim_pos & 1
    place = jnp.stack([fact_pos, dim_pos, core, dim_pos >> 1]).astype(jnp.int32)

    def swap(x):
        return lax.ppermute(x, "dim", pair)

    def shift(x, by):
        return lax.ppermute(x, "fact", [(i, (i + by) % n_fact) for i in range(n_fact)])

    def by_chip(x):
        return lax.all_to_all(x, "dim", 0, 0, tiled=True, axis_index_groups=same)

    def by_fact(x):
        return lax.all_to_all(x, "fact", 0, 0, tiled=True)

    mine = project(place, block_table, dims, w_tables)
    pieces, up, down = [mine], mine, mine
    for _ in range(3):
        up, down = shift(up, 1), shift(down, -1)
        pieces += [up, down]
    pieces += [shift(up[: rows // 2], 1), shift(down[rows // 2 :], -1)]
    pieces_sib = [swap(x) for x in pieces]

    live = jnp.arange(slots, dtype=jnp.int32) < link_count[0]
    target = links[:, 0] - fact_pos * n_dim
    codes_own = jnp.arange(slots, dtype=jnp.int32) + ((links[:, 1] // n_dim) << 5) + ((target >> 1) << 8)
    keys_own = jnp.where(live, 2 * codes_own + (target & 1), -1)
    keys_sib = swap(keys_own)
    tiles_sib = swap(tiles)
    found = [compact(x >> 1, (x >= 0) & ((x & 1) == core)) for x in (keys_own, keys_sib)]
    lists = jnp.concatenate([x[0] for x in found])
    counts = jnp.stack([x[1] for x in found])
    facts_t = facts.T.reshape(chips, width // chips, block)

    partial = call(
        forward_kernel,
        jax.ShapeDtypeStruct((chips, 544, 128), BF16),
        [SMEM] * 3 + [VMEM] * 21,
        [pltpu.VMEM((2 * n_fact, rows, width), BF16), pltpu.VMEM((chips + 1, block, width), F32)],
        flops=2 * slots * block * block * width,
        moved=8 << 20,
    )(place, lists, counts, *pieces, *pieces_sib, facts_t, tiles, tiles_sib)
    late_dims, partial = lax.optimization_barrier((dims, partial))
    dims_all = lax.all_gather(late_dims, "fact", axis=0)
    parts = by_chip(partial)

    fact_out, spread, facts_t = call(
        middle_kernel,
        (
            jax.ShapeDtypeStruct((block, width), BF16),
            jax.ShapeDtypeStruct((chips, width, block), BF16),
            jax.ShapeDtypeStruct((chips, width // chips, block), BF16),
        ),
        [VMEM] * 4,
        flops=2 * block * width * width,
        moved=5 << 20,
    )(parts, facts, w_self, cot)
    grads, dims_all = lax.optimization_barrier((by_chip(spread), dims_all))

    own, sib = call(
        backward_kernel,
        (jax.ShapeDtypeStruct((n_fact, 528, 128), F32), jax.ShapeDtypeStruct((n_fact, 528, 128), BF16)),
        [SMEM] * 3 + [VMEM] * 4,
        [pltpu.VMEM((2 * n_fact + 1, width, block), F32), pltpu.VMEM((width // chips, width), F32)],
        flops=2 * slots * block * block * width,
        moved=9 << 20,
    )(place, lists, counts, grads, facts_t, tiles, tiles_sib)
    slices = by_fact((own + swap(sib).astype(F32)).astype(BF16))

    tab, gsum, self_piece = call(
        slice_kernel,
        (
            jax.ShapeDtypeStruct((768, 128), BF16),
            jax.ShapeDtypeStruct((n_fact, 64, 128), BF16),
            jax.ShapeDtypeStruct((8, 128), F32),
        ),
        [SMEM] * 2 + [VMEM] * 2,
        [pltpu.VMEM((3, 64, width), F32)],
        flops=2 * n_fact * 64 * 128 * width,
        moved=3 << 20,
    )(place, block_table, slices, dims_all)
    tab = lax.all_to_all(tab.reshape(n_dim, 24, 128), "dim", 0, 0, tiled=True)
    packed = call(
        pack_kernel, jax.ShapeDtypeStruct((n_fact, 96, 128), BF16), [VMEM] * 3, moved=1 << 19
    )(tab, gsum, self_piece)
    packed = by_fact(packed)
    pieces_own = by_chip(jnp.broadcast_to(packed[None, :, 64:, :], (chips, n_fact, 32, 128)))
    pieces_sib = swap(pieces_own)

    grad_dims, grad_self, grad_tab = call(
        final_kernel,
        (
            jax.ShapeDtypeStruct((rows, width), F32),
            jax.ShapeDtypeStruct((width, width), F32),
            jax.ShapeDtypeStruct((3, width, width), F32),
        ),
        [SMEM] * 2 + [VMEM] * 4,
        moved=8 << 20,
    )(place, block_table, pieces_own, pieces_sib, packed, w_tables)
    return (fact_out, grad_dims, grad_self, grad_tab)


def solution(mesh):
    split = P(("fact", "dim"), None)
    return jax.shard_map(
        body,
        mesh=mesh,
        in_specs=(split, split, P(("fact", "dim"), None, None), split, P(("fact", "dim")), P(), P(), P(), split),
        out_specs=(split, split, P(), P()),
        check_vma=False,
    )
```

```python
import jax
import jax.numpy as jnp
from jax import lax
from jax.experimental import pallas as pl
from jax.experimental.pallas import tpu as pltpu
from jax.sharding import PartitionSpec as P

F32 = jnp.float32
BF16 = jnp.bfloat16
VMEM = pl.BlockSpec(memory_space=pltpu.VMEM)
SMEM = pl.BlockSpec(memory_space=pltpu.SMEM)
PARAMS = pltpu.CompilerParams(vmem_limit_bytes=24 * 1024 * 1024)
UNROLL = 2


ORDER = (0, -1, 1, -2, 2, -3, 3)
EARLY = 5
LIST = 40


def call(kernel, out_shape, in_specs, scratch=(), flops=0, moved=0, out_specs=None):
    return pl.pallas_call(
        kernel,
        out_shape=out_shape,
        in_specs=in_specs,
        out_specs=jax.tree.map(lambda _: VMEM, out_shape) if out_specs is None else out_specs,
        scratch_shapes=list(scratch),
        compiler_params=PARAMS,
        cost_estimate=pl.CostEstimate(flops=flops, bytes_accessed=moved, transcendentals=0),
    )


def decode(code):
    return code & 31, (code >> 5) & 7, code >> 8


def column_kind(place, table, side, h):
    dim_pos = place[1]
    return table[h * 32 + (dim_pos if side == 0 else dim_pos + 1 - 2 * place[2])]


def prepare_kernel(place, table, links_own, links_sib, count_own, count_sib, facts, w, *refs):
    early, (lists, counts, proj, facts_t) = refs[: 2 * EARLY], refs[2 * EARLY :]
    fact_pos, core = place[0], place[2]
    for side, (links, count) in enumerate(((links_own, count_own), (links_sib, count_sib))):
        n = jnp.int32(0)
        for slot in range(32):
            target = links[slot, 0] - fact_pos * 32
            lists[side * LIST + n] = slot + ((links[slot, 1] >> 5) << 5) + ((target >> 1) << 8)
            n = n + jnp.where((slot < count[0]) & ((target & 1) == core), 1, 0)
        lists[side * LIST + n] = 16 << 8
        counts[side] = n
    for side in range(2):
        for at, shift in enumerate(ORDER[:EARLY]):
            kind = column_kind(place, table, side, (fact_pos + shift) & 7)
            value = jnp.dot(early[side * EARLY + at][...], w[kind], preferred_element_type=F32)
            proj[side * EARLY + at] = value.astype(BF16)
    facts_t[...] = facts[...].astype(F32).T.astype(BF16)


def forward_kernel(place, table, lists, counts, proj, *refs):
    late = 9 - EARLY
    sides, (w, facts_t, tiles_own, tiles_sib, out, panel, acc) = (refs[:late], refs[late : 2 * late]), refs[2 * late :]
    fact_pos = place[0]
    for side, pieces in enumerate(sides):
        for at, shift in enumerate(ORDER[:EARLY]):
            panel[side * 8 + ((fact_pos + shift) & 7)] = proj[side * EARLY + at]
        blocks = [x[...] for x in pieces[:-2]] + [jnp.concatenate([pieces[-2][...], pieces[-1][...]], axis=0)]
        for shift, rows in zip(ORDER[EARLY:] + (4,), blocks):
            h = (fact_pos + shift) & 7
            value = jnp.dot(rows, w[column_kind(place, table, side, h)], preferred_element_type=F32)
            panel[side * 8 + h] = value.astype(BF16)
    acc[...] = jnp.zeros_like(acc)
    for side, tiles in enumerate((tiles_own, tiles_sib)):

        def step(i, carry, side=side, tiles=tiles):
            found = []
            for u in range(UNROLL):
                slot, holder, chip = decode(lists[side * LIST + i * UNROLL + u])
                found.append((chip, jnp.dot(tiles[slot], panel[side * 8 + holder], preferred_element_type=F32)))
            for chip, value in found:
                acc[chip] += value
            return carry

        lax.fori_loop(0, (counts[side] + UNROLL - 1) // UNROLL, step, 0)
    for chip in range(out.shape[0]):
        for q in range(4):
            out[chip, q * 128 : (q + 1) * 128, :] = acc[chip, :, q * 128 : (q + 1) * 128].astype(BF16)
        out[chip, 512:544, :] = facts_t[chip * 32 : (chip + 1) * 32, :]


def middle_kernel(parts, facts, w, cot, fact_out, spread, facts_t):
    pre = jnp.dot(facts[...], w[...], preferred_element_type=F32)
    aggs = []
    for q in range(4):
        agg = parts[0, q * 128 : (q + 1) * 128, :].astype(F32)
        for chip in range(1, parts.shape[0]):
            agg = agg + parts[chip, q * 128 : (q + 1) * 128, :].astype(F32)
        aggs.append(agg)
    pre = pre + jnp.concatenate(aggs, axis=1)
    sig = jax.nn.sigmoid(pre)
    fact_out[...] = (pre * sig).astype(BF16)
    grad = cot[...].astype(F32) * sig * (1.0 + pre * (1.0 - sig))
    turned = grad.T.astype(BF16)
    for chip in range(spread.shape[0]):
        spread[chip] = turned
        facts_t[chip] = parts[chip, 512:544, :]


def backward_kernel(place, lists, counts, grads, facts_t, tiles_own, tiles_sib, keep, give, acc, weight):
    core = place[2]
    acc[...] = jnp.zeros_like(acc)
    for side, tiles in enumerate((tiles_own, tiles_sib)):
        base = 8 * (core if side == 0 else 1 - core)

        def step(i, carry, side=side, tiles=tiles, base=base):
            found = []
            for u in range(UNROLL):
                slot, holder, chip = decode(lists[side * LIST + i * UNROLL + u])
                at = jnp.where(chip == 16, 16, base + holder)
                value = jnp.dot(grads[jnp.minimum(chip, 15)], tiles[slot], preferred_element_type=F32)
                found.append((at, value))
            for at, value in found:
                acc[at] += value
            return carry

        lax.fori_loop(0, (counts[side] + UNROLL - 1) // UNROLL, step, 0)
    half = weight.shape[0] // 2
    total = jnp.zeros(weight.shape, F32)
    for chip in range(grads.shape[0]):
        total = total + lax.dot_general(
            facts_t[chip], grads[chip], (((1,), (1,)), ((), ())), preferred_element_type=F32
        )
    weight[...] = total
    for out, who, kind in ((keep, core, F32), (give, 1 - core, BF16)):
        for z in range(8):
            features = pl.ds(pl.multiple_of(who * 256 + z * 32, 32), 32)
            for at in range(16):
                out[z, at * 32 : (at + 1) * 32, :] = acc[at, features, :].astype(kind)
            rows = pl.ds(pl.multiple_of(who * half + (z % 2) * 8, 8), 8)
            mine = weight[rows, (z // 2) * 128 : (z // 2 + 1) * 128]
            out[z, 512:528, :] = jnp.concatenate([mine, jnp.zeros_like(mine)], axis=0).astype(kind)


def slice_kernel(place, table, parts, *refs):
    pieces, (tab, gsum, self_piece, tacc) = refs[:18], refs[18:]
    fact_pos, core = place[0], place[2]
    total = parts[0].astype(F32)
    for z in range(1, parts.shape[0]):
        total = total + parts[z].astype(F32)
    self_piece[...] = total[512:520]
    for at in range(16):
        gsum[at] = total[at * 32 : (at + 1) * 32].astype(BF16)
    tacc[...] = jnp.zeros_like(tacc)
    for side in range(2):
        column = 8 * (core if side == 0 else 1 - core)
        for at, shift in enumerate(ORDER + (4,)):
            h = (fact_pos + shift) & 7
            kind = column_kind(place, table, side, h)
            grad = gsum[column + h]
            if shift == 4:
                low, high = pieces[side * 9 + 7], pieces[side * 9 + 8]
                rows = jnp.concatenate([low[...], high[...]], axis=0)
            else:
                rows = pieces[side * 9 + at][...]
            tacc[kind] += jnp.dot(grad, rows, preferred_element_type=F32)
    for q in range(4):
        for t in range(3):
            at = q * 96 + t * 32
            tab[at : at + 32, :] = tacc[t, :, q * 128 : (q + 1) * 128].astype(BF16)


def pack_kernel(place, parts, gsum, self_piece, out):
    core = place[2]
    total = jnp.sum(parts[...].astype(F32), axis=0)
    piece = jnp.concatenate([total, self_piece[...]], axis=0).astype(BF16)
    for z in range(out.shape[0]):
        out[z, 0:32, :] = gsum[core * 8 + z]
        out[z, 32:64, :] = gsum[(1 - core) * 8 + z]
        out[z, 64:96, :] = piece


def final_kernel(place, table, own, sib, kept, given, w, grad_dims, grad_self, grad_tab):
    even = place[2] == 0
    scale = F32(32768.0**-0.5)
    kind = table[place[0] * 32 + place[1]]
    mine, other = kept[...].astype(F32).reshape(256, 128), given[...].astype(F32).reshape(256, 128)
    turned = jnp.concatenate([jnp.where(even, mine, other), jnp.where(even, other, mine)], axis=0)
    grad_dims[...] = lax.dot_general(
        turned.T.astype(BF16), w[kind], (((1,), (1,)), ((), ())), preferred_element_type=F32
    )
    for q in range(4):
        for group in range(2):
            tables = [[[], [], []], [[], [], []]]
            for z in range(4 * group, 4 * group + 4):
                for chip in range(16):
                    mine, other = own[chip, z].astype(F32) * scale, sib[chip, z].astype(F32) * scale
                    pair = (jnp.where(even, mine, other), jnp.where(even, other, mine))
                    for core in range(2):
                        if z // 2 == q:
                            row = (2 * chip + core) * 16 + (z % 2) * 8
                            grad_self[row : row + 8, q * 128 : (q + 1) * 128] = pair[core][24:32]
                        if chip // 4 == q:
                            first = (chip % 4) * 24
                            for t in range(3):
                                lo, hi = max(first, t * 32), min(first + 24, t * 32 + 32)
                                if lo < hi:
                                    tables[core][t].append(pair[core][lo - first : hi - first])
            for core in range(2):
                for t in range(3):
                    column = core * 256 + group * 128
                    both = jnp.concatenate(tables[core][t], axis=0)
                    grad_tab[t, q * 128 : (q + 1) * 128, column : column + 128] = both.T


def body(facts, dims, tiles, links, link_count, block_table, w_self, w_tables, cot):
    n_fact = lax.axis_size("fact")
    n_dim = lax.axis_size("dim")
    fact_pos = lax.axis_index("fact")
    dim_pos = lax.axis_index("dim")
    chips = n_dim // 2
    same = [[2 * m + core for m in range(chips)] for core in range(2)]
    pair = [(d, d ^ 1) for d in range(n_dim)]
    rows, width = dims.shape
    slots, block, _ = tiles.shape
    place = jnp.stack([fact_pos, dim_pos, dim_pos & 1, dim_pos >> 1]).astype(jnp.int32)

    def swap(x):
        return lax.ppermute(x, "dim", pair)

    def shift(x, by):
        return lax.ppermute(x, "fact", [(i, (i + by) % n_fact) for i in range(n_fact)])

    def by_chip(x):
        return lax.all_to_all(x, "dim", 0, 0, tiled=True, axis_index_groups=same)

    def by_fact(x):
        return lax.all_to_all(x, "fact", 0, 0, tiled=True)

    pieces, up, down = [dims], dims, dims
    for _ in range(3):
        up, down = shift(up, 1), shift(down, -1)
        pieces += [up, down]
    pieces_sib = [swap(x) for x in pieces]
    far = [shift(up[: rows // 2], 1), shift(down[rows // 2 :], -1)]
    tiles_sib = swap(tiles)

    lists, counts, proj, facts_t = call(
        prepare_kernel,
        (
            jax.ShapeDtypeStruct((2 * LIST,), jnp.int32),
            jax.ShapeDtypeStruct((2,), jnp.int32),
            jax.ShapeDtypeStruct((2 * EARLY, rows, width), BF16),
            jax.ShapeDtypeStruct((width, block), BF16),
        ),
        [SMEM] * 6 + [VMEM] * (2 + 2 * EARLY),
        flops=4 * EARLY * rows * width * width,
        moved=6 << 20,
        out_specs=(SMEM, SMEM, VMEM, VMEM),
    )(
        place, block_table, links, swap(links), link_count, swap(link_count), facts, w_tables,
        *pieces[:EARLY], *pieces_sib[:EARLY],
    )
    *far, proj = lax.optimization_barrier((*far, proj))
    pieces, pieces_sib = pieces + far, pieces_sib + [swap(x) for x in far]
    partial = call(
        forward_kernel,
        jax.ShapeDtypeStruct((chips, 544, 128), BF16),
        [SMEM] * 4 + [VMEM] * (5 + 2 * (9 - EARLY)),
        [pltpu.VMEM((2 * n_fact, rows, width), BF16), pltpu.VMEM((chips + 1, block, width), F32)],
        flops=2 * slots * block * block * width,
        moved=8 << 20,
    )(place, block_table, lists, counts, proj, *pieces[EARLY:], *pieces_sib[EARLY:], w_tables, facts_t, tiles, tiles_sib)
    parts = by_chip(partial)

    fact_out, spread, facts_t = call(
        middle_kernel,
        (
            jax.ShapeDtypeStruct((block, width), BF16),
            jax.ShapeDtypeStruct((chips, width, block), BF16),
            jax.ShapeDtypeStruct((chips, width // chips, block), BF16),
        ),
        [VMEM] * 4,
        flops=2 * block * width * width,
        moved=5 << 20,
    )(parts, facts, w_self, cot)
    grads = by_chip(spread)

    keep, give = call(
        backward_kernel,
        (jax.ShapeDtypeStruct((n_fact, 528, 128), F32), jax.ShapeDtypeStruct((n_fact, 528, 128), BF16)),
        [SMEM] * 3 + [VMEM] * 4,
        [pltpu.VMEM((2 * n_fact + 1, width, block), F32), pltpu.VMEM((width // chips, width), F32)],
        flops=2 * slots * block * block * width,
        moved=9 << 20,
    )(place, lists, counts, grads, facts_t, tiles, tiles_sib)
    slices = by_fact((keep + swap(give).astype(F32)).astype(BF16))

    tab, gsum, self_piece = call(
        slice_kernel,
        (
            jax.ShapeDtypeStruct((384, 128), BF16),
            jax.ShapeDtypeStruct((2 * n_fact, 32, 128), BF16),
            jax.ShapeDtypeStruct((8, 128), F32),
        ),
        [SMEM] * 2 + [VMEM] * 19,
        [pltpu.VMEM((3, 32, width), F32)],
        flops=4 * n_fact * 32 * 128 * width,
        moved=3 << 20,
    )(place, block_table, slices, *pieces, *pieces_sib)
    tab = by_chip(tab.reshape(chips, 24, 128))
    packed = call(
        pack_kernel, jax.ShapeDtypeStruct((n_fact, 96, 128), BF16), [SMEM] + [VMEM] * 3, moved=1 << 19
    )(place, tab, gsum, self_piece)
    packed = by_fact(packed)
    pieces_own = by_chip(jnp.broadcast_to(packed[None, :, 64:, :], (chips, n_fact, 32, 128)))
    given = swap(packed[:, 32:64, :])

    grad_dims, grad_self, grad_tab = call(
        final_kernel,
        (
            jax.ShapeDtypeStruct((rows, width), F32),
            jax.ShapeDtypeStruct((width, width), F32),
            jax.ShapeDtypeStruct((3, width, width), F32),
        ),
        [SMEM] * 2 + [VMEM] * 5,
        moved=8 << 20,
    )(place, block_table, pieces_own, swap(pieces_own), packed[:, :32, :], given, w_tables)
    return (fact_out, grad_dims, grad_self, grad_tab)


def solution(mesh):
    split = P(("fact", "dim"), None)
    return jax.shard_map(
        body,
        mesh=mesh,
        in_specs=(split, split, P(("fact", "dim"), None, None), split, P(("fact", "dim")), P(), P(), P(), split),
        out_specs=(split, split, P(), P()),
        check_vma=False,
    )
```

```python
import jax
import jax.numpy as jnp
from jax import lax
from jax.experimental import pallas as pl
from jax.experimental.pallas import tpu as pltpu
from jax.sharding import PartitionSpec as P

F32 = jnp.float32
BF16 = jnp.bfloat16
VMEM = pl.BlockSpec(memory_space=pltpu.VMEM)
SMEM = pl.BlockSpec(memory_space=pltpu.SMEM)
PARAMS = pltpu.CompilerParams(vmem_limit_bytes=24 * 1024 * 1024)
UNROLL = 4


ORDER = (0, -1, 1, -2, 2, -3, 3)
EARLY = 5
LIST = 40


def call(kernel, out_shape, in_specs, scratch=(), flops=0, moved=0, out_specs=None):
    return pl.pallas_call(
        kernel,
        out_shape=out_shape,
        in_specs=in_specs,
        out_specs=jax.tree.map(lambda _: VMEM, out_shape) if out_specs is None else out_specs,
        scratch_shapes=list(scratch),
        compiler_params=PARAMS,
        cost_estimate=pl.CostEstimate(flops=flops, bytes_accessed=moved, transcendentals=0),
    )


def decode(code):
    return code & 31, (code >> 5) & 7, code >> 8


def column_kind(place, table, side, h):
    dim_pos = place[1]
    return table[h * 32 + (dim_pos if side == 0 else dim_pos + 1 - 2 * place[2])]


def prepare_kernel(place, table, links_own, links_sib, facts, dims, w, lists, counts, facts_t, proj):
    fact_pos, core = place[0], place[2]
    for side, links in enumerate((links_own, links_sib)):
        n = jnp.int32(0)
        for slot in range(32):
            target = links[0, slot] - fact_pos * 32
            lists[side * LIST + n] = slot + ((links[1, slot] >> 5) << 5) + ((target >> 1) << 8)
            n = n + jnp.where((slot < links[0, 32]) & ((target & 1) == core), 1, 0)
        for spare in range(UNROLL - 1):
            lists[side * LIST + n + spare] = 16 << 8
        counts[side] = n
    kind = column_kind(place, table, 0, fact_pos)
    proj[...] = jnp.dot(dims[...], w[kind], preferred_element_type=F32).astype(BF16)
    facts_t[...] = facts[...].astype(F32).T.astype(BF16)


def project_kernel(place, table, w, *refs):
    early, proj = refs[:-1], refs[-1]
    at = 0
    for side in range(2):
        for shift in ORDER[1 - side : EARLY]:
            kind = column_kind(place, table, side, (place[0] + shift) & 7)
            proj[at] = jnp.dot(early[at][...], w[kind], preferred_element_type=F32).astype(BF16)
            at += 1


def forward_kernel(place, table, lists, counts, proj_own, proj, *refs):
    late = 9 - EARLY
    sides, (w, facts_t, tiles_own, tiles_sib, out, panel, acc) = (refs[:late], refs[late : 2 * late]), refs[2 * late :]
    fact_pos = place[0]
    for side, pieces in enumerate(sides):
        for at, shift in enumerate(ORDER[:EARLY]):
            value = proj_own[...] if side + at == 0 else proj[side * EARLY + at - 1]
            panel[side * 8 + ((fact_pos + shift) & 7)] = value
        blocks = [x[...] for x in pieces[:-2]] + [jnp.concatenate([pieces[-2][...], pieces[-1][...]], axis=0)]
        for shift, rows in zip(ORDER[EARLY:] + (4,), blocks):
            h = (fact_pos + shift) & 7
            value = jnp.dot(rows, w[column_kind(place, table, side, h)], preferred_element_type=F32)
            panel[side * 8 + h] = value.astype(BF16)
    acc[...] = jnp.zeros_like(acc)
    for side, tiles in enumerate((tiles_own, tiles_sib)):

        def step(i, carry, side=side, tiles=tiles):
            found = []
            for u in range(UNROLL):
                slot, holder, chip = decode(lists[side * LIST + i * UNROLL + u])
                found.append((chip, jnp.dot(tiles[slot], panel[side * 8 + holder], preferred_element_type=F32)))
            for chip, value in found:
                acc[chip] += value
            return carry

        lax.fori_loop(0, (counts[side] + UNROLL - 1) // UNROLL, step, 0)
    for chip in range(out.shape[0]):
        for q in range(4):
            out[chip, q * 128 : (q + 1) * 128, :] = acc[chip, :, q * 128 : (q + 1) * 128].astype(BF16)
        out[chip, 512:544, :] = facts_t[chip * 32 : (chip + 1) * 32, :]


def middle_kernel(parts, facts, w, cot, fact_out, spread, facts_t):
    pre = jnp.dot(facts[...], w[...], preferred_element_type=F32)
    aggs = []
    for q in range(4):
        agg = parts[0, q * 128 : (q + 1) * 128, :].astype(F32)
        for chip in range(1, parts.shape[0]):
            agg = agg + parts[chip, q * 128 : (q + 1) * 128, :].astype(F32)
        aggs.append(agg)
    pre = pre + jnp.concatenate(aggs, axis=1)
    sig = jax.nn.sigmoid(pre)
    fact_out[...] = (pre * sig).astype(BF16)
    grad = cot[...].astype(F32) * sig * (1.0 + pre * (1.0 - sig))
    turned = grad.T.astype(BF16)
    for chip in range(spread.shape[0]):
        spread[chip] = turned
        facts_t[chip] = parts[chip, 512:544, :]


def backward_kernel(place, lists, counts, grads, facts_t, tiles_own, tiles_sib, keep, give, acc, weight):
    core = place[2]
    acc[...] = jnp.zeros_like(acc)
    for side, tiles in enumerate((tiles_own, tiles_sib)):
        base = 8 * (core if side == 0 else 1 - core)

        def step(i, carry, side=side, tiles=tiles, base=base):
            found = []
            for u in range(UNROLL):
                slot, holder, chip = decode(lists[side * LIST + i * UNROLL + u])
                at = jnp.where(chip == 16, 16, base + holder)
                value = jnp.dot(grads[jnp.minimum(chip, 15)], tiles[slot], preferred_element_type=F32)
                found.append((at, value))
            for at, value in found:
                acc[at] += value
            return carry

        lax.fori_loop(0, (counts[side] + UNROLL - 1) // UNROLL, step, 0)
    half = weight.shape[0] // 2
    total = jnp.zeros(weight.shape, F32)
    for chip in range(grads.shape[0]):
        total = total + lax.dot_general(
            facts_t[chip], grads[chip], (((1,), (1,)), ((), ())), preferred_element_type=F32
        )
    weight[...] = total
    for out, who, kind in ((keep, core, F32), (give, 1 - core, BF16)):
        for z in range(8):
            features = pl.ds(pl.multiple_of(who * 256 + z * 32, 32), 32)
            for at in range(16):
                out[z, at * 32 : (at + 1) * 32, :] = acc[at, features, :].astype(kind)
            rows = pl.ds(pl.multiple_of(who * half + (z % 2) * 8, 8), 8)
            mine = weight[rows, (z // 2) * 128 : (z // 2 + 1) * 128]
            out[z, 512:528, :] = jnp.concatenate([mine, jnp.zeros_like(mine)], axis=0).astype(kind)


def slice_kernel(place, table, parts, *refs):
    pieces, (tab, gsum, self_piece, tacc) = refs[:18], refs[18:]
    fact_pos, core = place[0], place[2]
    total = parts[0].astype(F32)
    for z in range(1, parts.shape[0]):
        total = total + parts[z].astype(F32)
    self_piece[...] = total[512:520]
    for at in range(16):
        gsum[at] = total[at * 32 : (at + 1) * 32].astype(BF16)
    tacc[...] = jnp.zeros_like(tacc)
    for side in range(2):
        column = 8 * (core if side == 0 else 1 - core)
        for at, shift in enumerate(ORDER + (4,)):
            h = (fact_pos + shift) & 7
            kind = column_kind(place, table, side, h)
            grad = gsum[column + h]
            if shift == 4:
                low, high = pieces[side * 9 + 7], pieces[side * 9 + 8]
                rows = jnp.concatenate([low[...], high[...]], axis=0)
            else:
                rows = pieces[side * 9 + at][...]
            tacc[kind] += jnp.dot(grad, rows, preferred_element_type=F32)
    for q in range(4):
        for t in range(3):
            at = q * 96 + t * 32
            tab[at : at + 32, :] = tacc[t, :, q * 128 : (q + 1) * 128].astype(BF16)


def pack_kernel(place, parts, gsum, self_piece, out):
    core = place[2]
    total = jnp.sum(parts[...].astype(F32), axis=0)
    piece = jnp.concatenate([total, self_piece[...]], axis=0).astype(BF16)
    for z in range(out.shape[0]):
        out[z, 0:32, :] = gsum[core * 8 + z]
        out[z, 32:64, :] = gsum[(1 - core) * 8 + z]
        out[z, 64:96, :] = piece


def rows_kernel(place, table, kept, given, w, grad_dims):
    even = place[2] == 0
    kind = table[place[0] * 32 + place[1]]
    mine, other = kept[...].astype(F32).reshape(256, 128), given[...].astype(F32).reshape(256, 128)
    turned = jnp.concatenate([jnp.where(even, mine, other), jnp.where(even, other, mine)], axis=0)
    grad_dims[...] = lax.dot_general(
        turned.T.astype(BF16), w[kind], (((1,), (1,)), ((), ())), preferred_element_type=F32
    )


def final_kernel(place, own, sib, grad_self, grad_tab):
    even = place[2] == 0
    scale = F32(32768.0**-0.5)
    for q in range(4):
        for group in range(2):
            tables = [[[], [], []], [[], [], []]]
            for z in range(4 * group, 4 * group + 4):
                for chip in range(16):
                    mine, other = own[chip, z].astype(F32) * scale, sib[chip, z].astype(F32) * scale
                    pair = (jnp.where(even, mine, other), jnp.where(even, other, mine))
                    for core in range(2):
                        if z // 2 == q:
                            row = (2 * chip + core) * 16 + (z % 2) * 8
                            grad_self[row : row + 8, q * 128 : (q + 1) * 128] = pair[core][24:32]
                        if chip // 4 == q:
                            first = (chip % 4) * 24
                            for t in range(3):
                                lo, hi = max(first, t * 32), min(first + 24, t * 32 + 32)
                                if lo < hi:
                                    tables[core][t].append(pair[core][lo - first : hi - first])
            for core in range(2):
                for t in range(3):
                    column = core * 256 + group * 128
                    both = jnp.concatenate(tables[core][t], axis=0)
                    grad_tab[t, q * 128 : (q + 1) * 128, column : column + 128] = both.T


def body(facts, dims, tiles, links, link_count, block_table, w_self, w_tables, cot):
    n_fact = lax.axis_size("fact")
    n_dim = lax.axis_size("dim")
    fact_pos = lax.axis_index("fact")
    dim_pos = lax.axis_index("dim")
    chips = n_dim // 2
    same = [[2 * m + core for m in range(chips)] for core in range(2)]
    pair = [(d, d ^ 1) for d in range(n_dim)]
    rows, width = dims.shape
    slots, block, _ = tiles.shape
    place = jnp.stack([fact_pos, dim_pos, dim_pos & 1, dim_pos >> 1]).astype(jnp.int32)

    def swap(x):
        return lax.ppermute(x, "dim", pair)

    def shift(x, by):
        return lax.ppermute(x, "fact", [(i, (i + by) % n_fact) for i in range(n_fact)])

    def by_chip(x):
        return lax.all_to_all(x, "dim", 0, 0, tiled=True, axis_index_groups=same)

    def by_fact(x):
        return lax.all_to_all(x, "fact", 0, 0, tiled=True)

    count = jnp.broadcast_to(link_count[None, :], (2, 1))
    links_own = jnp.concatenate([links.T, count], axis=1)
    links_sib = swap(links_own)
    lists, counts, facts_t, proj_own = call(
        prepare_kernel,
        (
            jax.ShapeDtypeStruct((2 * LIST,), jnp.int32),
            jax.ShapeDtypeStruct((2,), jnp.int32),
            jax.ShapeDtypeStruct((width, block), BF16),
            jax.ShapeDtypeStruct((rows, width), BF16),
        ),
        [SMEM] * 4 + [VMEM] * 3,
        flops=2 * rows * width * width,
        moved=3 << 20,
        out_specs=(SMEM, SMEM, VMEM, VMEM),
    )(place, block_table, links_own, links_sib, facts, dims, w_tables)
    tiles_sib = swap(tiles)

    pieces, up, down = [dims], dims, dims
    for step in range(3):
        if step == 2:
            up, down, proj_own = lax.optimization_barrier((up, down, proj_own))
        up, down = shift(up, 1), shift(down, -1)
        pieces += [up, down]
    pieces_sib = [swap(x) for x in pieces]
    far = [shift(up[: rows // 2], 1), shift(down[rows // 2 :], -1)]
    early = pieces[1:EARLY] + pieces_sib[:EARLY]
    proj = call(
        project_kernel,
        jax.ShapeDtypeStruct((len(early), rows, width), BF16),
        [SMEM] * 2 + [VMEM] * (1 + len(early)),
        flops=2 * len(early) * rows * width * width,
        moved=4 << 20,
    )(place, block_table, w_tables, *early)
    *far, proj = lax.optimization_barrier((*far, proj))
    pieces, pieces_sib = pieces + far, pieces_sib + [swap(x) for x in far]
    partial = call(
        forward_kernel,
        jax.ShapeDtypeStruct((chips, 544, 128), BF16),
        [SMEM] * 4 + [VMEM] * (6 + 2 * (9 - EARLY)),
        [pltpu.VMEM((2 * n_fact, rows, width), BF16), pltpu.VMEM((chips + 1, block, width), F32)],
        flops=2 * slots * block * block * width,
        moved=8 << 20,
    )(place, block_table, lists, counts, proj_own, proj, *pieces[EARLY:], *pieces_sib[EARLY:], w_tables, facts_t, tiles, tiles_sib)
    parts = by_chip(partial)

    fact_out, spread, facts_t = call(
        middle_kernel,
        (
            jax.ShapeDtypeStruct((block, width), BF16),
            jax.ShapeDtypeStruct((chips, width, block), BF16),
            jax.ShapeDtypeStruct((chips, width // chips, block), BF16),
        ),
        [VMEM] * 4,
        flops=2 * block * width * width,
        moved=5 << 20,
    )(parts, facts, w_self, cot)
    grads = by_chip(spread)

    keep, give = call(
        backward_kernel,
        (jax.ShapeDtypeStruct((n_fact, 528, 128), F32), jax.ShapeDtypeStruct((n_fact, 528, 128), BF16)),
        [SMEM] * 3 + [VMEM] * 4,
        [pltpu.VMEM((2 * n_fact + 1, width, block), F32), pltpu.VMEM((width // chips, width), F32)],
        flops=2 * slots * block * block * width,
        moved=9 << 20,
    )(place, lists, counts, grads, facts_t, tiles, tiles_sib)
    slices = by_fact((keep + swap(give).astype(F32)).astype(BF16))

    tab, gsum, self_piece = call(
        slice_kernel,
        (
            jax.ShapeDtypeStruct((384, 128), BF16),
            jax.ShapeDtypeStruct((2 * n_fact, 32, 128), BF16),
            jax.ShapeDtypeStruct((8, 128), F32),
        ),
        [SMEM] * 2 + [VMEM] * 19,
        [pltpu.VMEM((3, 32, width), F32)],
        flops=4 * n_fact * 32 * 128 * width,
        moved=3 << 20,
    )(place, block_table, slices, *pieces, *pieces_sib)
    tab = by_chip(tab.reshape(chips, 24, 128))
    packed = call(
        pack_kernel, jax.ShapeDtypeStruct((n_fact, 96, 128), BF16), [SMEM] + [VMEM] * 3, moved=1 << 19
    )(place, tab, gsum, self_piece)
    packed = by_fact(packed)
    pieces_own = by_chip(jnp.broadcast_to(packed[None, :, 64:, :], (chips, n_fact, 32, 128)))
    given = swap(packed[:, 32:64, :])

    grad_dims = call(
        rows_kernel,
        jax.ShapeDtypeStruct((rows, width), F32),
        [SMEM] * 2 + [VMEM] * 3,
        flops=2 * rows * width * width,
        moved=2 << 20,
    )(place, block_table, packed[:, :32, :], given, w_tables)
    grad_self, grad_tab = call(
        final_kernel,
        (jax.ShapeDtypeStruct((width, width), F32), jax.ShapeDtypeStruct((3, width, width), F32)),
        [SMEM] + [VMEM] * 2,
        moved=8 << 20,
    )(place, pieces_own, swap(pieces_own))
    return (fact_out, grad_dims, grad_self, grad_tab)


def solution(mesh):
    split = P(("fact", "dim"), None)
    return jax.shard_map(
        body,
        mesh=mesh,
        in_specs=(split, split, P(("fact", "dim"), None, None), split, P(("fact", "dim")), P(), P(), P(), split),
        out_specs=(split, split, P(), P()),
        check_vma=False,
    )
```

```python
import jax
import jax.numpy as jnp
from jax import lax
from jax.experimental import pallas as pl
from jax.experimental.pallas import tpu as pltpu
from jax.sharding import PartitionSpec as P

F32 = jnp.float32
BF16 = jnp.bfloat16
VMEM = pl.BlockSpec(memory_space=pltpu.VMEM)
SMEM = pl.BlockSpec(memory_space=pltpu.SMEM)
PARAMS = pltpu.CompilerParams(vmem_limit_bytes=24 * 1024 * 1024)
UNROLL = 4


ORDER = (0, -1, 1, -2, 2, -3, 3)
EARLY = 5
LIST = 40
COUNT, KIND, PLACE, INFO = 80, 96, 112, 128


def call(kernel, out_shape, in_specs, scratch=(), flops=0, moved=0, out_specs=None):
    return pl.pallas_call(
        kernel,
        out_shape=out_shape,
        in_specs=in_specs,
        out_specs=jax.tree.map(lambda _: VMEM, out_shape) if out_specs is None else out_specs,
        scratch_shapes=list(scratch),
        compiler_params=PARAMS,
        cost_estimate=pl.CostEstimate(flops=flops, bytes_accessed=moved, transcendentals=0),
    )


def decode(code):
    return code & 31, (code >> 5) & 7, code >> 8


def prepare_kernel(place, links_own, links_sib, table, info):
    fact_pos, dim_pos, core = place[0], place[1], place[2]
    for side, links in enumerate((links_own, links_sib)):
        n = jnp.int32(0)
        for slot in range(32):
            target = links[0, slot] - fact_pos * 32
            info[side * LIST + n] = slot + ((links[1, slot] >> 5) << 5) + ((target >> 1) << 8)
            n = n + jnp.where((slot < links[0, 32]) & ((target & 1) == core), 1, 0)
        for spare in range(UNROLL - 1):
            info[side * LIST + n + spare] = 16 << 8
        info[COUNT + side] = n
    for i in range(4):
        info[PLACE + i] = place[i]
    for h in range(8):
        info[KIND + h] = table[h * 32 + dim_pos]
        info[KIND + 8 + h] = table[h * 32 + dim_pos + 1 - 2 * core]


def project_kernel(info, w, facts, *refs):
    early, (proj, facts_t) = refs[:-2], refs[-2:]
    at = 0
    for side in range(2):
        for shift in ORDER[:EARLY]:
            kind = info[KIND + side * 8 + ((info[PLACE] + shift) & 7)]
            proj[at] = jnp.dot(early[at][...], w[kind], preferred_element_type=F32).astype(BF16)
            at += 1
    facts_t[...] = facts[...].astype(F32).T.astype(BF16)


def forward_kernel(info, proj, *refs):
    late = 9 - EARLY
    sides, (w, facts_t, tiles_own, tiles_sib, out, panel, acc) = (refs[:late], refs[late : 2 * late]), refs[2 * late :]
    fact_pos = info[PLACE]
    for side, pieces in enumerate(sides):
        for at, shift in enumerate(ORDER[:EARLY]):
            panel[side * 8 + ((fact_pos + shift) & 7)] = proj[side * EARLY + at]
        blocks = [x[...] for x in pieces[:-2]] + [jnp.concatenate([pieces[-2][...], pieces[-1][...]], axis=0)]
        for shift, rows in zip(ORDER[EARLY:] + (4,), blocks):
            h = (fact_pos + shift) & 7
            value = jnp.dot(rows, w[info[KIND + side * 8 + h]], preferred_element_type=F32)
            panel[side * 8 + h] = value.astype(BF16)
    acc[...] = jnp.zeros_like(acc)
    for side, tiles in enumerate((tiles_own, tiles_sib)):

        def step(i, carry, side=side, tiles=tiles):
            found = []
            for u in range(UNROLL):
                slot, holder, chip = decode(info[side * LIST + i * UNROLL + u])
                found.append((chip, jnp.dot(tiles[slot], panel[side * 8 + holder], preferred_element_type=F32)))
            for chip, value in found:
                acc[chip] += value
            return carry

        lax.fori_loop(0, (info[COUNT + side] + UNROLL - 1) // UNROLL, step, 0)
    for chip in range(out.shape[0]):
        for q in range(4):
            out[chip, q * 128 : (q + 1) * 128, :] = acc[chip, :, q * 128 : (q + 1) * 128].astype(BF16)
        out[chip, 512:544, :] = facts_t[chip * 32 : (chip + 1) * 32, :]


def middle_kernel(parts, facts, w, cot, fact_out, spread, facts_t):
    pre = jnp.dot(facts[...], w[...], preferred_element_type=F32)
    aggs = []
    for q in range(4):
        agg = parts[0, q * 128 : (q + 1) * 128, :].astype(F32)
        for chip in range(1, parts.shape[0]):
            agg = agg + parts[chip, q * 128 : (q + 1) * 128, :].astype(F32)
        aggs.append(agg)
    pre = pre + jnp.concatenate(aggs, axis=1)
    sig = jax.nn.sigmoid(pre)
    fact_out[...] = (pre * sig).astype(BF16)
    grad = cot[...].astype(F32) * sig * (1.0 + pre * (1.0 - sig))
    turned = grad.T.astype(BF16)
    for chip in range(spread.shape[0]):
        spread[chip] = turned
        facts_t[chip] = parts[chip, 512:544, :]


def backward_kernel(info, grads, facts_t, tiles_own, tiles_sib, keep, give, acc, weight):
    fact_pos, core = info[PLACE], info[PLACE + 2]
    acc[...] = jnp.zeros_like(acc)
    for side, tiles in enumerate((tiles_own, tiles_sib)):
        base = 8 * (core if side == 0 else 1 - core)

        def step(i, carry, side=side, tiles=tiles, base=base):
            found = []
            for u in range(UNROLL):
                slot, holder, chip = decode(info[side * LIST + i * UNROLL + u])
                at = jnp.where(chip == 16, 16, base + holder)
                value = jnp.dot(grads[jnp.minimum(chip, 15)], tiles[slot], preferred_element_type=F32)
                found.append((at, value))
            for at, value in found:
                acc[at] += value
            return carry

        lax.fori_loop(0, (info[COUNT + side] + UNROLL - 1) // UNROLL, step, 0)
    piece, width = facts_t.shape[1], grads.shape[1]
    half = piece // 2
    total = jnp.zeros((piece, width), F32)
    for chip in range(grads.shape[0]):
        total = total + lax.dot_general(
            facts_t[chip], grads[chip], (((1,), (1,)), ((), ())), preferred_element_type=F32
        )
    for q in range(4):
        weight[q] = total[:, q * 128 : (q + 1) * 128]
    for out, who, kind in ((keep, core, F32), (give, 1 - core, BF16)):
        for k in range(8):
            z = (fact_pos + k) & 7
            features = pl.ds(pl.multiple_of(who * 256 + z * 32, 32), 32)
            for at in range(16):
                out[k, at * 32 : (at + 1) * 32, :] = acc[at, features, :].astype(kind)
            rows = pl.ds(pl.multiple_of(who * half + (z & 1) * 8, 8), 8)
            mine = weight[z >> 1, rows, :]
            out[k, 512:528, :] = jnp.concatenate([mine, jnp.zeros_like(mine)], axis=0).astype(kind)


def slice_kernel(info, kept, given, from_below, from_above, *refs):
    pieces, (tab, gsum, self_piece, tacc) = refs[:18], refs[18:]
    fact_pos, core = info[PLACE], info[PLACE + 2]
    total = kept[...] + given[...].astype(F32) + from_below[...].astype(F32) + from_above[...].astype(F32)
    self_piece[...] = total[512:520]
    for at in range(16):
        gsum[at] = total[at * 32 : (at + 1) * 32].astype(BF16)
    tacc[...] = jnp.zeros_like(tacc)
    for side in range(2):
        column = 8 * (core if side == 0 else 1 - core)
        for at, shift in enumerate(ORDER + (4,)):
            h = (fact_pos + shift) & 7
            kind = info[KIND + side * 8 + h]
            grad = gsum[column + h]
            if shift == 4:
                low, high = pieces[side * 9 + 7], pieces[side * 9 + 8]
                rows = jnp.concatenate([low[...], high[...]], axis=0)
            else:
                rows = pieces[side * 9 + at][...]
            tacc[kind] += jnp.dot(grad, rows, preferred_element_type=F32)
    for q in range(4):
        for t in range(3):
            at = q * 96 + t * 32
            tab[at : at + 32, :] = tacc[t, :, q * 128 : (q + 1) * 128].astype(BF16)


def pack_kernel(info, parts, gsum, self_piece, out):
    core = info[PLACE + 2]
    total = jnp.sum(parts[...].astype(F32), axis=0)
    piece = jnp.concatenate([total, self_piece[...]], axis=0).astype(BF16)
    for z in range(out.shape[0]):
        out[z, 0:32, :] = gsum[core * 8 + z]
        out[z, 32:64, :] = gsum[(1 - core) * 8 + z]
        out[z, 64:96, :] = piece


def rows_kernel(info, kept, given, w, grad_dims):
    even = info[PLACE + 2] == 0
    kind = info[KIND + info[PLACE]]
    mine, other = kept[...].astype(F32).reshape(256, 128), given[...].astype(F32).reshape(256, 128)
    turned = jnp.concatenate([jnp.where(even, mine, other), jnp.where(even, other, mine)], axis=0)
    grad_dims[...] = lax.dot_general(
        turned.T.astype(BF16), w[kind], (((1,), (1,)), ((), ())), preferred_element_type=F32
    )


def final_kernel(info, own, sib, grad_self, grad_tab):
    even = info[PLACE + 2] == 0
    scale = F32(32768.0**-0.5)
    for q in range(4):
        for group in range(2):
            tables = [[[], [], []], [[], [], []]]
            for z in range(4 * group, 4 * group + 4):
                for chip in range(16):
                    mine, other = own[chip, z].astype(F32) * scale, sib[chip, z].astype(F32) * scale
                    pair = (jnp.where(even, mine, other), jnp.where(even, other, mine))
                    for core in range(2):
                        if z // 2 == q:
                            row = (2 * chip + core) * 16 + (z % 2) * 8
                            grad_self[row : row + 8, q * 128 : (q + 1) * 128] = pair[core][24:32]
                        if chip // 4 == q:
                            first = (chip % 4) * 24
                            for t in range(3):
                                lo, hi = max(first, t * 32), min(first + 24, t * 32 + 32)
                                if lo < hi:
                                    tables[core][t].append(pair[core][lo - first : hi - first])
            for core in range(2):
                for t in range(3):
                    column = core * 256 + group * 128
                    both = jnp.concatenate(tables[core][t], axis=0)
                    grad_tab[t, q * 128 : (q + 1) * 128, column : column + 128] = both.T


def body(facts, dims, tiles, links, link_count, block_table, w_self, w_tables, cot):
    n_fact = lax.axis_size("fact")
    n_dim = lax.axis_size("dim")
    fact_pos = lax.axis_index("fact")
    dim_pos = lax.axis_index("dim")
    chips = n_dim // 2
    same = [[2 * m + core for m in range(chips)] for core in range(2)]
    pair = [(d, d ^ 1) for d in range(n_dim)]
    rows, width = dims.shape
    slots, block, _ = tiles.shape
    place = jnp.stack([fact_pos, dim_pos, dim_pos & 1, dim_pos >> 1]).astype(jnp.int32)

    def swap(x):
        return lax.ppermute(x, "dim", pair)

    def shift(x, by):
        return lax.ppermute(x, "fact", [(i, (i + by) % n_fact) for i in range(n_fact)])

    def by_chip(x):
        return lax.all_to_all(x, "dim", 0, 0, tiled=True, axis_index_groups=same)

    def by_fact(x):
        return lax.all_to_all(x, "fact", 0, 0, tiled=True)

    count = jnp.broadcast_to(link_count[None, :], (2, 1))
    links_own = jnp.concatenate([links.T, count], axis=1)
    links_sib = swap(links_own)
    info = call(
        prepare_kernel,
        jax.ShapeDtypeStruct((INFO,), jnp.int32),
        [SMEM] * 4,
        flops=1 << 31,
        moved=4096,
        out_specs=SMEM,
    )(place, links_own, links_sib, block_table)
    tiles_sib = swap(tiles)

    pieces, up, down = [dims], dims, dims
    for step in range(3):
        if step == 2:
            up, down, info = lax.optimization_barrier((up, down, info))
        up, down = shift(up, 1), shift(down, -1)
        pieces += [up, down]
    pieces_sib = [swap(x) for x in pieces]
    far = [shift(up[: rows // 2], 1), shift(down[rows // 2 :], -1)]
    early = pieces[:EARLY] + pieces_sib[:EARLY]
    proj, facts_t = call(
        project_kernel,
        (jax.ShapeDtypeStruct((len(early), rows, width), BF16), jax.ShapeDtypeStruct((width, block), BF16)),
        [SMEM] + [VMEM] * (2 + len(early)),
        flops=2 * len(early) * rows * width * width,
        moved=4 << 20,
    )(info, w_tables, facts, *early)
    *far, proj = lax.optimization_barrier((*far, proj))
    pieces, pieces_sib = pieces + far, pieces_sib + [swap(x) for x in far]
    partial = call(
        forward_kernel,
        jax.ShapeDtypeStruct((chips, 544, 128), BF16),
        [SMEM] + [VMEM] * (5 + 2 * (9 - EARLY)),
        [pltpu.VMEM((2 * n_fact, rows, width), BF16), pltpu.VMEM((chips + 1, block, width), F32)],
        flops=2 * slots * block * block * width,
        moved=8 << 20,
    )(info, proj, *pieces[EARLY:], *pieces_sib[EARLY:], w_tables, facts_t, tiles, tiles_sib)
    parts = by_chip(partial)

    fact_out, spread, facts_t = call(
        middle_kernel,
        (
            jax.ShapeDtypeStruct((block, width), BF16),
            jax.ShapeDtypeStruct((chips, width, block), BF16),
            jax.ShapeDtypeStruct((chips, width // chips, block), BF16),
        ),
        [VMEM] * 4,
        flops=2 * block * width * width,
        moved=5 << 20,
    )(parts, facts, w_self, cot)
    grads = by_chip(spread)

    keep, give = call(
        backward_kernel,
        (jax.ShapeDtypeStruct((n_fact, 528, 128), F32), jax.ShapeDtypeStruct((n_fact, 528, 128), BF16)),
        [SMEM] + [VMEM] * 4,
        [pltpu.VMEM((2 * n_fact + 1, width, block), F32), pltpu.VMEM((4, width // chips, 128), F32)],
        flops=2 * slots * block * block * width,
        moved=9 << 20,
    )(info, grads, facts_t, tiles, tiles_sib)
    give = swap(give)

    def partial_sum(k, arrived):
        return (keep[k] + give[k].astype(F32) + arrived.astype(F32)).astype(BF16)

    up = shift((keep[4] + give[4].astype(F32)).astype(BF16), 1)
    down = shift((keep[5] + give[5].astype(F32)).astype(BF16), -1)
    for k in (3, 2):
        up, down = shift(partial_sum(k, up), 1), shift(partial_sum(9 - k, down), -1)
    up = shift(partial_sum(1, up), 1)

    tab, gsum, self_piece = call(
        slice_kernel,
        (
            jax.ShapeDtypeStruct((384, 128), BF16),
            jax.ShapeDtypeStruct((2 * n_fact, 32, 128), BF16),
            jax.ShapeDtypeStruct((8, 128), F32),
        ),
        [SMEM] + [VMEM] * 22,
        [pltpu.VMEM((3, 32, width), F32)],
        flops=4 * n_fact * 32 * 128 * width,
        moved=3 << 20,
    )(info, keep[0], give[0], up, down, *pieces, *pieces_sib)
    tab = by_chip(tab.reshape(chips, 24, 128))
    packed = call(
        pack_kernel, jax.ShapeDtypeStruct((n_fact, 96, 128), BF16), [SMEM] + [VMEM] * 3, moved=1 << 19
    )(info, tab, gsum, self_piece)
    packed = by_fact(packed)
    pieces_own = by_chip(jnp.broadcast_to(packed[None, :, 64:, :], (chips, n_fact, 32, 128)))
    given = swap(packed[:, 32:64, :])

    grad_dims = call(
        rows_kernel,
        jax.ShapeDtypeStruct((rows, width), F32),
        [SMEM] + [VMEM] * 3,
        flops=2 * rows * width * width,
        moved=2 << 20,
    )(info, packed[:, :32, :], given, w_tables)
    grad_self, grad_tab = call(
        final_kernel,
        (jax.ShapeDtypeStruct((width, width), F32), jax.ShapeDtypeStruct((3, width, width), F32)),
        [SMEM] + [VMEM] * 2,
        moved=8 << 20,
    )(info, pieces_own, swap(pieces_own))
    return (fact_out, grad_dims, grad_self, grad_tab)


def solution(mesh):
    split = P(("fact", "dim"), None)
    return jax.shard_map(
        body,
        mesh=mesh,
        in_specs=(split, split, P(("fact", "dim"), None, None), split, P(("fact", "dim")), P(), P(), P(), split),
        out_specs=(split, split, P(), P()),
        check_vma=False,
    )
```

```python
import jax
import jax.numpy as jnp
from jax import lax
from jax.experimental import pallas as pl
from jax.experimental.pallas import tpu as pltpu
from jax.sharding import PartitionSpec as P

F32 = jnp.float32
BF16 = jnp.bfloat16
VMEM = pl.BlockSpec(memory_space=pltpu.VMEM)
SMEM = pl.BlockSpec(memory_space=pltpu.SMEM)
PARAMS = pltpu.CompilerParams(vmem_limit_bytes=24 * 1024 * 1024)
UNROLL = 4


ORDER = (0, -1, 1, -2, 2, 4, -3, 3)
EARLY = 6
LIST = 40
COUNT, KIND, PLACE, INFO = 80, 96, 112, 128


def call(kernel, out_shape, in_specs, scratch=(), flops=0, moved=0, out_specs=None):
    return pl.pallas_call(
        kernel,
        out_shape=out_shape,
        in_specs=in_specs,
        out_specs=jax.tree.map(lambda _: VMEM, out_shape) if out_specs is None else out_specs,
        scratch_shapes=list(scratch),
        compiler_params=PARAMS,
        cost_estimate=pl.CostEstimate(flops=flops, bytes_accessed=moved, transcendentals=0),
    )


def decode(code):
    return code & 31, (code >> 5) & 7, code >> 8


def prepare_kernel(place, links_own, links_sib, table, info):
    fact_pos, dim_pos, core = place[0], place[1], place[2]
    for side, links in enumerate((links_own, links_sib)):
        n = jnp.int32(0)
        for slot in range(32):
            target = links[0, slot] - fact_pos * 32
            info[side * LIST + n] = slot + ((links[1, slot] >> 5) << 5) + ((target >> 1) << 8)
            n = n + jnp.where((slot < links[0, 32]) & ((target & 1) == core), 1, 0)
        for spare in range(UNROLL - 1):
            info[side * LIST + n + spare] = 16 << 8
        info[COUNT + side] = n
    for i in range(4):
        info[PLACE + i] = place[i]
    for h in range(8):
        info[KIND + h] = table[h * 32 + dim_pos]
        info[KIND + 8 + h] = table[h * 32 + dim_pos + 1 - 2 * core]


def project_kernel(info, w, facts, *refs):
    early, (proj, facts_t) = refs[:-2], refs[-2:]
    at = 0
    for side in range(2):
        for shift in ORDER[:EARLY]:
            kind = info[KIND + side * 8 + ((info[PLACE] + shift) & 7)]
            proj[at] = jnp.dot(early[at][...], w[kind], preferred_element_type=F32).astype(BF16)
            at += 1
    facts_t[...] = facts[...].astype(F32).T.astype(BF16)


def forward_kernel(info, proj, *refs):
    late = len(ORDER) - EARLY
    sides, (w, facts_t, tiles_own, tiles_sib, out, panel, acc) = (refs[:late], refs[late : 2 * late]), refs[2 * late :]
    fact_pos = info[PLACE]
    for side, pieces in enumerate(sides):
        for at, shift in enumerate(ORDER[:EARLY]):
            panel[side * 8 + ((fact_pos + shift) & 7)] = proj[side * EARLY + at]
        for shift, rows in zip(ORDER[EARLY:], pieces):
            h = (fact_pos + shift) & 7
            value = jnp.dot(rows[...], w[info[KIND + side * 8 + h]], preferred_element_type=F32)
            panel[side * 8 + h] = value.astype(BF16)
    acc[...] = jnp.zeros_like(acc)
    for side, tiles in enumerate((tiles_own, tiles_sib)):

        def step(i, carry, side=side, tiles=tiles):
            found = []
            for u in range(UNROLL):
                slot, holder, chip = decode(info[side * LIST + i * UNROLL + u])
                found.append((chip, jnp.dot(tiles[slot], panel[side * 8 + holder], preferred_element_type=F32)))
            for chip, value in found:
                acc[chip] += value
            return carry

        lax.fori_loop(0, (info[COUNT + side] + UNROLL - 1) // UNROLL, step, 0)
    for chip in range(out.shape[0]):
        for q in range(4):
            out[chip, q * 128 : (q + 1) * 128, :] = acc[chip, :, q * 128 : (q + 1) * 128].astype(BF16)
        out[chip, 512:544, :] = facts_t[chip * 32 : (chip + 1) * 32, :]


def middle_kernel(parts, facts, w, cot, fact_out, spread, facts_t):
    pre = jnp.dot(facts[...], w[...], preferred_element_type=F32)
    aggs = []
    for q in range(4):
        agg = parts[0, q * 128 : (q + 1) * 128, :].astype(F32)
        for chip in range(1, parts.shape[0]):
            agg = agg + parts[chip, q * 128 : (q + 1) * 128, :].astype(F32)
        aggs.append(agg)
    pre = pre + jnp.concatenate(aggs, axis=1)
    sig = jax.nn.sigmoid(pre)
    fact_out[...] = (pre * sig).astype(BF16)
    grad = cot[...].astype(F32) * sig * (1.0 + pre * (1.0 - sig))
    turned = grad.T.astype(BF16)
    for chip in range(spread.shape[0]):
        spread[chip] = turned
        facts_t[chip] = parts[chip, 512:544, :]


def backward_kernel(info, grads, facts_t, tiles_own, tiles_sib, keep, give, acc, weight):
    fact_pos, core = info[PLACE], info[PLACE + 2]
    acc[...] = jnp.zeros_like(acc)
    for side, tiles in enumerate((tiles_own, tiles_sib)):
        base = 8 * (core if side == 0 else 1 - core)

        def step(i, carry, side=side, tiles=tiles, base=base):
            found = []
            for u in range(UNROLL):
                slot, holder, chip = decode(info[side * LIST + i * UNROLL + u])
                at = jnp.where(chip == 16, 16, base + holder)
                value = jnp.dot(grads[jnp.minimum(chip, 15)], tiles[slot], preferred_element_type=F32)
                found.append((at, value))
            for at, value in found:
                acc[at] += value
            return carry

        lax.fori_loop(0, (info[COUNT + side] + UNROLL - 1) // UNROLL, step, 0)
    piece, width = facts_t.shape[1], grads.shape[1]
    half = piece // 2
    total = jnp.zeros((piece, width), F32)
    for chip in range(grads.shape[0]):
        total = total + lax.dot_general(
            facts_t[chip], grads[chip], (((1,), (1,)), ((), ())), preferred_element_type=F32
        )
    for q in range(4):
        weight[q] = total[:, q * 128 : (q + 1) * 128]
    for out, who, kind in ((keep, core, F32), (give, 1 - core, BF16)):
        for k in range(8):
            z = (fact_pos + k) & 7
            features = pl.ds(pl.multiple_of(who * 256 + z * 32, 32), 32)
            for at in range(16):
                out[k, at * 32 : (at + 1) * 32, :] = acc[at, features, :].astype(kind)
            rows = pl.ds(pl.multiple_of(who * half + (z & 1) * 8, 8), 8)
            mine = weight[z >> 1, rows, :]
            out[k, 512:528, :] = jnp.concatenate([mine, jnp.zeros_like(mine)], axis=0).astype(kind)


def slice_kernel(info, kept, given, from_below, from_above, from_far, *refs):
    pieces, (tab, gsum, self_piece, tacc) = refs[:16], refs[16:]
    fact_pos, core = info[PLACE], info[PLACE + 2]
    total = kept[...]
    for arrived in (given, from_below, from_above, from_far):
        total = total + arrived[...].astype(F32)
    self_piece[...] = total[512:520]
    for at in range(16):
        gsum[at] = total[at * 32 : (at + 1) * 32].astype(BF16)
    tacc[...] = jnp.zeros_like(tacc)
    for side in range(2):
        column = 8 * (core if side == 0 else 1 - core)
        for at, shift in enumerate(ORDER):
            h = (fact_pos + shift) & 7
            kind = info[KIND + side * 8 + h]
            rows = pieces[side * 8 + at][...]
            tacc[kind] += jnp.dot(gsum[column + h], rows, preferred_element_type=F32)
    for q in range(4):
        for t in range(3):
            at = q * 96 + t * 32
            tab[at : at + 32, :] = tacc[t, :, q * 128 : (q + 1) * 128].astype(BF16)


def pack_kernel(info, parts, gsum, self_piece, out):
    core = info[PLACE + 2]
    total = jnp.sum(parts[...].astype(F32), axis=0)
    piece = jnp.concatenate([total, self_piece[...]], axis=0).astype(BF16)
    for z in range(out.shape[0]):
        out[z, 0:32, :] = gsum[core * 8 + z]
        out[z, 32:64, :] = gsum[(1 - core) * 8 + z]
        out[z, 64:96, :] = piece


def rows_kernel(info, kept, given, w, grad_dims):
    even = info[PLACE + 2] == 0
    kind = info[KIND + info[PLACE]]
    mine, other = kept[...].astype(F32).reshape(256, 128), given[...].astype(F32).reshape(256, 128)
    turned = jnp.concatenate([jnp.where(even, mine, other), jnp.where(even, other, mine)], axis=0)
    grad_dims[...] = lax.dot_general(
        turned.T.astype(BF16), w[kind], (((1,), (1,)), ((), ())), preferred_element_type=F32
    )


def final_kernel(info, own, sib, grad_self, grad_tab):
    even = info[PLACE + 2] == 0
    scale = F32(32768.0**-0.5)
    for q in range(4):
        for group in range(2):
            tables = [[[], [], []], [[], [], []]]
            for z in range(4 * group, 4 * group + 4):
                for chip in range(16):
                    mine, other = own[chip, z].astype(F32) * scale, sib[chip, z].astype(F32) * scale
                    pair = (jnp.where(even, mine, other), jnp.where(even, other, mine))
                    for core in range(2):
                        if z // 2 == q:
                            row = (2 * chip + core) * 16 + (z % 2) * 8
                            grad_self[row : row + 8, q * 128 : (q + 1) * 128] = pair[core][24:32]
                        if chip // 4 == q:
                            first = (chip % 4) * 24
                            for t in range(3):
                                lo, hi = max(first, t * 32), min(first + 24, t * 32 + 32)
                                if lo < hi:
                                    tables[core][t].append(pair[core][lo - first : hi - first])
            for core in range(2):
                for t in range(3):
                    column = core * 256 + group * 128
                    both = jnp.concatenate(tables[core][t], axis=0)
                    grad_tab[t, q * 128 : (q + 1) * 128, column : column + 128] = both.T


def body(facts, dims, tiles, links, link_count, block_table, w_self, w_tables, cot):
    n_fact = lax.axis_size("fact")
    n_dim = lax.axis_size("dim")
    fact_pos = lax.axis_index("fact")
    dim_pos = lax.axis_index("dim")
    chips = n_dim // 2
    same = [[2 * m + core for m in range(chips)] for core in range(2)]
    pair = [(d, d ^ 1) for d in range(n_dim)]
    rows, width = dims.shape
    slots, block, _ = tiles.shape
    place = jnp.stack([fact_pos, dim_pos, dim_pos & 1, dim_pos >> 1]).astype(jnp.int32)

    def swap(x):
        return lax.ppermute(x, "dim", pair)

    def shift(x, by):
        return lax.ppermute(x, "fact", [(i, (i + by) % n_fact) for i in range(n_fact)])

    def by_chip(x):
        return lax.all_to_all(x, "dim", 0, 0, tiled=True, axis_index_groups=same)

    def by_fact(x):
        return lax.all_to_all(x, "fact", 0, 0, tiled=True)

    count = jnp.broadcast_to(link_count[None, :], (2, 1))
    links_own = jnp.concatenate([links.T, count], axis=1)
    links_sib = swap(links_own)
    info = call(
        prepare_kernel,
        jax.ShapeDtypeStruct((INFO,), jnp.int32),
        [SMEM] * 4,
        flops=1 << 31,
        moved=4096,
        out_specs=SMEM,
    )(place, links_own, links_sib, block_table)
    tiles_sib = swap(tiles)

    far = shift(dims, 4)
    pieces, up, down = [dims], dims, dims
    for step in range(3):
        if step == 2:
            up, down, far, info = lax.optimization_barrier((up, down, far, info))
            pieces.append(far)
        up, down = shift(up, 1), shift(down, -1)
        pieces += [up, down]
    pieces, late = pieces[:EARLY], pieces[EARLY:]
    pieces_sib = [swap(x) for x in pieces]
    early = pieces + pieces_sib
    proj, facts_t = call(
        project_kernel,
        (jax.ShapeDtypeStruct((len(early), rows, width), BF16), jax.ShapeDtypeStruct((width, block), BF16)),
        [SMEM] + [VMEM] * (2 + len(early)),
        flops=2 * len(early) * rows * width * width,
        moved=4 << 20,
    )(info, w_tables, facts, *early)
    *late, proj = lax.optimization_barrier((*late, proj))
    pieces, pieces_sib = pieces + late, pieces_sib + [swap(x) for x in late]
    partial = call(
        forward_kernel,
        jax.ShapeDtypeStruct((chips, 544, 128), BF16),
        [SMEM] + [VMEM] * (5 + 2 * len(late)),
        [pltpu.VMEM((2 * n_fact, rows, width), BF16), pltpu.VMEM((chips + 1, block, width), F32)],
        flops=2 * slots * block * block * width,
        moved=8 << 20,
    )(info, proj, *pieces[EARLY:], *pieces_sib[EARLY:], w_tables, facts_t, tiles, tiles_sib)
    parts = by_chip(partial)

    fact_out, spread, facts_t = call(
        middle_kernel,
        (
            jax.ShapeDtypeStruct((block, width), BF16),
            jax.ShapeDtypeStruct((chips, width, block), BF16),
            jax.ShapeDtypeStruct((chips, width // chips, block), BF16),
        ),
        [VMEM] * 4,
        flops=2 * block * width * width,
        moved=5 << 20,
    )(parts, facts, w_self, cot)
    grads = by_chip(spread)

    keep, give = call(
        backward_kernel,
        (jax.ShapeDtypeStruct((n_fact, 528, 128), F32), jax.ShapeDtypeStruct((n_fact, 528, 128), BF16)),
        [SMEM] + [VMEM] * 4,
        [pltpu.VMEM((2 * n_fact + 1, width, block), F32), pltpu.VMEM((4, width // chips, 128), F32)],
        flops=2 * slots * block * block * width,
        moved=9 << 20,
    )(info, grads, facts_t, tiles, tiles_sib)
    give = swap(give)

    def partial_sum(k, arrived):
        return (keep[k] + give[k].astype(F32) + arrived.astype(F32)).astype(BF16)

    far = shift((keep[4] + give[4].astype(F32)).astype(BF16), 4)
    up = shift((keep[3] + give[3].astype(F32)).astype(BF16), 1)
    down = shift((keep[5] + give[5].astype(F32)).astype(BF16), -1)
    for k in (2, 1):
        if k == 1:
            up, down, far = lax.optimization_barrier((up, down, far))
        up, down = shift(partial_sum(k, up), 1), shift(partial_sum(8 - k, down), -1)

    tab, gsum, self_piece = call(
        slice_kernel,
        (
            jax.ShapeDtypeStruct((384, 128), BF16),
            jax.ShapeDtypeStruct((2 * n_fact, 32, 128), BF16),
            jax.ShapeDtypeStruct((8, 128), F32),
        ),
        [SMEM] + [VMEM] * 21,
        [pltpu.VMEM((3, 32, width), F32)],
        flops=4 * n_fact * 32 * 128 * width,
        moved=3 << 20,
    )(info, keep[0], give[0], up, down, far, *pieces, *pieces_sib)
    tab = by_chip(tab.reshape(chips, 24, 128))
    packed = call(
        pack_kernel, jax.ShapeDtypeStruct((n_fact, 96, 128), BF16), [SMEM] + [VMEM] * 3, moved=1 << 19
    )(info, tab, gsum, self_piece)
    packed = by_fact(packed)
    pieces_own = by_chip(jnp.broadcast_to(packed[None, :, 64:, :], (chips, n_fact, 32, 128)))
    given = swap(packed[:, 32:64, :])

    grad_dims = call(
        rows_kernel,
        jax.ShapeDtypeStruct((rows, width), F32),
        [SMEM] + [VMEM] * 3,
        flops=2 * rows * width * width,
        moved=2 << 20,
    )(info, packed[:, :32, :], given, w_tables)
    grad_self, grad_tab = call(
        final_kernel,
        (jax.ShapeDtypeStruct((width, width), F32), jax.ShapeDtypeStruct((3, width, width), F32)),
        [SMEM] + [VMEM] * 2,
        moved=8 << 20,
    )(info, pieces_own, swap(pieces_own))
    return (fact_out, grad_dims, grad_self, grad_tab)


def solution(mesh):
    split = P(("fact", "dim"), None)
    return jax.shard_map(
        body,
        mesh=mesh,
        in_specs=(split, split, P(("fact", "dim"), None, None), split, P(("fact", "dim")), P(), P(), P(), split),
        out_specs=(split, split, P(), P()),
        check_vma=False,
    )
```

```python
import jax
import jax.numpy as jnp
from jax import lax
from jax.experimental import pallas as pl
from jax.experimental.pallas import tpu as pltpu
from jax.sharding import PartitionSpec as P

F32 = jnp.float32
BF16 = jnp.bfloat16
VMEM = pl.BlockSpec(memory_space=pltpu.VMEM)
SMEM = pl.BlockSpec(memory_space=pltpu.SMEM)
PARAMS = pltpu.CompilerParams(vmem_limit_bytes=24 * 1024 * 1024)
UNROLL = 4


PIECES = [(0, 0, 0, 0), (0, 1, 1, 0)]
for _step in (1, 2, 3):
    PIECES += [(2 * _step - 1, 0, 0, -_step), (2 * _step - 1, 1, 1, -_step)]
    PIECES += [(2 * _step, 0, 1, _step), (2 * _step, 1, 0, _step)]
PIECES += [(7, 0, 0, 4), (8, 0, 1, 4)]
EARLY = 10
LIST = 40
COUNT, KIND, PLACE, INFO = 80, 96, 112, 128


def call(kernel, out_shape, in_specs, scratch=(), flops=0, moved=0, out_specs=None):
    return pl.pallas_call(
        kernel,
        out_shape=out_shape,
        in_specs=in_specs,
        out_specs=jax.tree.map(lambda _: VMEM, out_shape) if out_specs is None else out_specs,
        scratch_shapes=list(scratch),
        compiler_params=PARAMS,
        cost_estimate=pl.CostEstimate(flops=flops, bytes_accessed=moved, transcendentals=0),
    )


def decode(code):
    return code & 31, (code >> 5) & 7, code >> 8


def prepare_kernel(place, links_own, links_sib, table, info):
    fact_pos, dim_pos, core = place[0], place[1], place[2]
    for side, links in enumerate((links_own, links_sib)):
        n = jnp.int32(0)
        for slot in range(32):
            target = links[0, slot] - fact_pos * 32
            info[side * LIST + n] = slot + ((links[1, slot] >> 5) << 5) + ((target >> 1) << 8)
            n = n + jnp.where((slot < links[0, 32]) & ((target & 1) == core), 1, 0)
        for spare in range(UNROLL - 1):
            info[side * LIST + n + spare] = 16 << 8
        info[COUNT + side] = n
    for i in range(4):
        info[PLACE + i] = place[i]
    for h in range(8):
        info[KIND + h] = table[h * 32 + dim_pos]
        info[KIND + 8 + h] = table[h * 32 + dim_pos + 1 - 2 * core]


def holder_of(info, shift):
    return (info[PLACE] + shift * (1 - 2 * info[PLACE + 2])) & 7


def project_kernel(info, w, facts, *refs):
    early, (proj, facts_t) = refs[:-2], refs[-2:]
    for at, (array, row, side, shift) in enumerate(PIECES[:EARLY]):
        kind = info[KIND + side * 8 + holder_of(info, shift)]
        proj[at] = jnp.dot(early[array][row], w[kind], preferred_element_type=F32).astype(BF16)
    facts_t[...] = facts[...].astype(F32).T.astype(BF16)


def forward_kernel(info, proj, *refs):
    late, (w, facts_t, tiles_own, tiles_sib, out, panel, acc) = refs[:4], refs[4:]
    for at, (array, row, side, shift) in enumerate(PIECES):
        h = holder_of(info, shift)
        if at < EARLY:
            panel[side * 8 + h] = proj[at]
        else:
            kind = info[KIND + side * 8 + h]
            value = jnp.dot(late[array - 5][row], w[kind], preferred_element_type=F32)
            panel[side * 8 + h] = value.astype(BF16)
    acc[...] = jnp.zeros_like(acc)
    for side, tiles in enumerate((tiles_own, tiles_sib)):

        def step(i, carry, side=side, tiles=tiles):
            found = []
            for u in range(UNROLL):
                slot, holder, chip = decode(info[side * LIST + i * UNROLL + u])
                found.append((chip, jnp.dot(tiles[slot], panel[side * 8 + holder], preferred_element_type=F32)))
            for chip, value in found:
                acc[chip] += value
            return carry

        lax.fori_loop(0, (info[COUNT + side] + UNROLL - 1) // UNROLL, step, 0)
    for chip in range(out.shape[0]):
        for q in range(4):
            out[chip, q * 128 : (q + 1) * 128, :] = acc[chip, :, q * 128 : (q + 1) * 128].astype(BF16)
        out[chip, 512:544, :] = facts_t[chip * 32 : (chip + 1) * 32, :]


def middle_kernel(parts, facts, w, cot, fact_out, spread, facts_t):
    pre = jnp.dot(facts[...], w[...], preferred_element_type=F32)
    aggs = []
    for q in range(4):
        agg = parts[0, q * 128 : (q + 1) * 128, :].astype(F32)
        for chip in range(1, parts.shape[0]):
            agg = agg + parts[chip, q * 128 : (q + 1) * 128, :].astype(F32)
        aggs.append(agg)
    pre = pre + jnp.concatenate(aggs, axis=1)
    sig = jax.nn.sigmoid(pre)
    fact_out[...] = (pre * sig).astype(BF16)
    grad = cot[...].astype(F32) * sig * (1.0 + pre * (1.0 - sig))
    turned = grad.T.astype(BF16)
    for chip in range(spread.shape[0]):
        spread[chip] = turned
        facts_t[chip] = parts[chip, 512:544, :]


def backward_kernel(info, grads, facts_t, tiles_own, tiles_sib, keep, give, acc, weight):
    fact_pos, core = info[PLACE], info[PLACE + 2]
    acc[...] = jnp.zeros_like(acc)
    for side, tiles in enumerate((tiles_own, tiles_sib)):
        base = 8 * (core if side == 0 else 1 - core)

        def step(i, carry, side=side, tiles=tiles, base=base):
            found = []
            for u in range(UNROLL):
                slot, holder, chip = decode(info[side * LIST + i * UNROLL + u])
                at = jnp.where(chip == 16, 16, base + holder)
                value = jnp.dot(grads[jnp.minimum(chip, 15)], tiles[slot], preferred_element_type=F32)
                found.append((at, value))
            for at, value in found:
                acc[at] += value
            return carry

        lax.fori_loop(0, (info[COUNT + side] + UNROLL - 1) // UNROLL, step, 0)
    piece, width = facts_t.shape[1], grads.shape[1]
    half = piece // 2
    total = jnp.zeros((piece, width), F32)
    for chip in range(grads.shape[0]):
        total = total + lax.dot_general(
            facts_t[chip], grads[chip], (((1,), (1,)), ((), ())), preferred_element_type=F32
        )
    for q in range(4):
        weight[q] = total[:, q * 128 : (q + 1) * 128]
    for out, who, kind in ((keep, core, F32), (give, 1 - core, BF16)):
        for k in range(8):
            z = (fact_pos + k) & 7
            features = pl.ds(pl.multiple_of(who * 256 + z * 32, 32), 32)
            for at in range(16):
                out[k, at * 32 : (at + 1) * 32, :] = acc[at, features, :].astype(kind)
            rows = pl.ds(pl.multiple_of(who * half + (z & 1) * 8, 8), 8)
            mine = weight[z >> 1, rows, :]
            out[k, 512:528, :] = jnp.concatenate([mine, jnp.zeros_like(mine)], axis=0).astype(kind)


def slice_kernel(info, kept, given, from_below, from_above, from_far, *refs):
    pieces, (tab, gsum, self_piece, tacc) = refs[:9], refs[9:]
    core = info[PLACE + 2]
    total = kept[...]
    for arrived in (given, from_below, from_above, from_far):
        total = total + arrived[...].astype(F32)
    self_piece[...] = total[512:520]
    for at in range(16):
        gsum[at] = total[at * 32 : (at + 1) * 32].astype(BF16)
    tacc[...] = jnp.zeros_like(tacc)
    for array, row, side, shift in PIECES:
        h = holder_of(info, shift)
        kind = info[KIND + side * 8 + h]
        grad = gsum[8 * (core if side == 0 else 1 - core) + h]
        tacc[kind] += jnp.dot(grad, pieces[array][row], preferred_element_type=F32)
    for q in range(4):
        for t in range(3):
            at = q * 96 + t * 32
            tab[at : at + 32, :] = tacc[t, :, q * 128 : (q + 1) * 128].astype(BF16)


def pack_kernel(info, parts, gsum, self_piece, out):
    core = info[PLACE + 2]
    total = jnp.sum(parts[...].astype(F32), axis=0)
    piece = jnp.concatenate([total, self_piece[...]], axis=0).astype(BF16)
    for z in range(out.shape[0]):
        out[z, 0:32, :] = gsum[core * 8 + z]
        out[z, 32:64, :] = gsum[(1 - core) * 8 + z]
        out[z, 64:96, :] = piece


def rows_kernel(info, kept, given, w, grad_dims):
    even = info[PLACE + 2] == 0
    kind = info[KIND + info[PLACE]]
    mine, other = kept[...].astype(F32).reshape(256, 128), given[...].astype(F32).reshape(256, 128)
    turned = jnp.concatenate([jnp.where(even, mine, other), jnp.where(even, other, mine)], axis=0)
    grad_dims[...] = lax.dot_general(
        turned.T.astype(BF16), w[kind], (((1,), (1,)), ((), ())), preferred_element_type=F32
    )


def final_kernel(info, own, sib, grad_self, grad_tab):
    even = info[PLACE + 2] == 0
    scale = F32(32768.0**-0.5)
    for q in range(4):
        for group in range(2):
            tables = [[[], [], []], [[], [], []]]
            for z in range(4 * group, 4 * group + 4):
                for chip in range(16):
                    mine, other = own[chip, z].astype(F32) * scale, sib[chip, z].astype(F32) * scale
                    pair = (jnp.where(even, mine, other), jnp.where(even, other, mine))
                    for core in range(2):
                        if z // 2 == q:
                            row = (2 * chip + core) * 16 + (z % 2) * 8
                            grad_self[row : row + 8, q * 128 : (q + 1) * 128] = pair[core][24:32]
                        if chip // 4 == q:
                            first = (chip % 4) * 24
                            for t in range(3):
                                lo, hi = max(first, t * 32), min(first + 24, t * 32 + 32)
                                if lo < hi:
                                    tables[core][t].append(pair[core][lo - first : hi - first])
            for core in range(2):
                for t in range(3):
                    column = core * 256 + group * 128
                    both = jnp.concatenate(tables[core][t], axis=0)
                    grad_tab[t, q * 128 : (q + 1) * 128, column : column + 128] = both.T


def body(facts, dims, tiles, links, link_count, block_table, w_self, w_tables, cot):
    n_fact = lax.axis_size("fact")
    n_dim = lax.axis_size("dim")
    fact_pos = lax.axis_index("fact")
    dim_pos = lax.axis_index("dim")
    chips = n_dim // 2
    same = [[2 * m + core for m in range(chips)] for core in range(2)]
    pair = [(d, d ^ 1) for d in range(n_dim)]
    rows, width = dims.shape
    slots, block, _ = tiles.shape
    place = jnp.stack([fact_pos, dim_pos, dim_pos & 1, dim_pos >> 1]).astype(jnp.int32)

    def swap(x):
        return lax.ppermute(x, "dim", pair)

    def shift(x, by):
        return lax.ppermute(x, "fact", [(i, (i + by) % n_fact) for i in range(n_fact)])

    def by_chip(x):
        return lax.all_to_all(x, "dim", 0, 0, tiled=True, axis_index_groups=same)

    def by_fact(x):
        return lax.all_to_all(x, "fact", 0, 0, tiled=True)

    count = jnp.broadcast_to(link_count[None, :], (2, 1))
    links_own = jnp.concatenate([links.T, count], axis=1)
    links_sib = swap(links_own)
    info = call(
        prepare_kernel,
        jax.ShapeDtypeStruct((INFO,), jnp.int32),
        [SMEM] * 4,
        flops=1 << 31,
        moved=4096,
        out_specs=SMEM,
    )(place, links_own, links_sib, block_table)
    tiles_sib = swap(tiles)

    around = [
        (f * n_dim + d, (f + 1 - 2 * (d % 2)) % n_fact * n_dim + d) for f in range(n_fact) for d in range(n_dim)
    ]

    def along(x):
        return lax.ppermute(x, ("fact", "dim"), around)

    moving = jnp.stack([dims, swap(dims)])
    early = [moving]
    for step in range(2):
        moving = along(moving)
        early += [moving, swap(moving)]
    moving, info = lax.optimization_barrier((moving, info))
    moving = along(moving)
    late = [moving, swap(moving)]
    far = along(moving[:1])
    proj, facts_t = call(
        project_kernel,
        (jax.ShapeDtypeStruct((EARLY, rows, width), BF16), jax.ShapeDtypeStruct((width, block), BF16)),
        [SMEM] + [VMEM] * (2 + len(early)),
        flops=2 * EARLY * rows * width * width,
        moved=4 << 20,
    )(info, w_tables, facts, *early)
    far, proj = lax.optimization_barrier((far, proj))
    late += [far, swap(far)]
    partial = call(
        forward_kernel,
        jax.ShapeDtypeStruct((chips, 544, 128), BF16),
        [SMEM] + [VMEM] * (5 + len(late)),
        [pltpu.VMEM((2 * n_fact, rows, width), BF16), pltpu.VMEM((chips + 1, block, width), F32)],
        flops=2 * slots * block * block * width,
        moved=8 << 20,
    )(info, proj, *late, w_tables, facts_t, tiles, tiles_sib)
    parts = by_chip(partial)

    fact_out, spread, facts_t = call(
        middle_kernel,
        (
            jax.ShapeDtypeStruct((block, width), BF16),
            jax.ShapeDtypeStruct((chips, width, block), BF16),
            jax.ShapeDtypeStruct((chips, width // chips, block), BF16),
        ),
        [VMEM] * 4,
        flops=2 * block * width * width,
        moved=5 << 20,
    )(parts, facts, w_self, cot)
    grads = by_chip(spread)

    keep, give = call(
        backward_kernel,
        (jax.ShapeDtypeStruct((n_fact, 528, 128), F32), jax.ShapeDtypeStruct((n_fact, 528, 128), BF16)),
        [SMEM] + [VMEM] * 4,
        [pltpu.VMEM((2 * n_fact + 1, width, block), F32), pltpu.VMEM((4, width // chips, 128), F32)],
        flops=2 * slots * block * block * width,
        moved=9 << 20,
    )(info, grads, facts_t, tiles, tiles_sib)
    give = swap(give)

    def partial_sum(k, arrived):
        return (keep[k] + give[k].astype(F32) + arrived.astype(F32)).astype(BF16)

    far = shift((keep[4] + give[4].astype(F32)).astype(BF16), 4)
    up = shift((keep[3] + give[3].astype(F32)).astype(BF16), 1)
    down = shift((keep[5] + give[5].astype(F32)).astype(BF16), -1)
    for k in (2, 1):
        if k == 1:
            up, down, far = lax.optimization_barrier((up, down, far))
        up, down = shift(partial_sum(k, up), 1), shift(partial_sum(8 - k, down), -1)

    tab, gsum, self_piece = call(
        slice_kernel,
        (
            jax.ShapeDtypeStruct((384, 128), BF16),
            jax.ShapeDtypeStruct((2 * n_fact, 32, 128), BF16),
            jax.ShapeDtypeStruct((8, 128), F32),
        ),
        [SMEM] + [VMEM] * 14,
        [pltpu.VMEM((3, 32, width), F32)],
        flops=4 * n_fact * 32 * 128 * width,
        moved=3 << 20,
    )(info, keep[0], give[0], up, down, far, *early, *late)
    tab = by_chip(tab.reshape(chips, 24, 128))
    packed = call(
        pack_kernel, jax.ShapeDtypeStruct((n_fact, 96, 128), BF16), [SMEM] + [VMEM] * 3, moved=1 << 19
    )(info, tab, gsum, self_piece)
    packed = by_fact(packed)
    pieces_own = by_chip(jnp.broadcast_to(packed[None, :, 64:, :], (chips, n_fact, 32, 128)))
    given = swap(packed[:, 32:64, :])

    grad_dims = call(
        rows_kernel,
        jax.ShapeDtypeStruct((rows, width), F32),
        [SMEM] + [VMEM] * 3,
        flops=2 * rows * width * width,
        moved=2 << 20,
    )(info, packed[:, :32, :], given, w_tables)
    grad_self, grad_tab = call(
        final_kernel,
        (jax.ShapeDtypeStruct((width, width), F32), jax.ShapeDtypeStruct((3, width, width), F32)),
        [SMEM] + [VMEM] * 2,
        moved=8 << 20,
    )(info, pieces_own, swap(pieces_own))
    return (fact_out, grad_dims, grad_self, grad_tab)


def solution(mesh):
    split = P(("fact", "dim"), None)
    return jax.shard_map(
        body,
        mesh=mesh,
        in_specs=(split, split, P(("fact", "dim"), None, None), split, P(("fact", "dim")), P(), P(), P(), split),
        out_specs=(split, split, P(), P()),
        check_vma=False,
    )
```

```python
import jax
import jax.numpy as jnp
from jax import lax
from jax.experimental import pallas as pl
from jax.experimental.pallas import tpu as pltpu
from jax.sharding import PartitionSpec as P

F32 = jnp.float32
BF16 = jnp.bfloat16
VMEM = pl.BlockSpec(memory_space=pltpu.VMEM)
SMEM = pl.BlockSpec(memory_space=pltpu.SMEM)
PARAMS = pltpu.CompilerParams(vmem_limit_bytes=24 * 1024 * 1024)
UNROLL = 4


ORDER = (0, -1, 1, -2, 2, -3, 3)
EARLY = 5
LIST = 40
COUNT, KIND, PLACE, INFO = 80, 96, 112, 128


def call(kernel, out_shape, in_specs, scratch=(), flops=0, moved=0, out_specs=None):
    return pl.pallas_call(
        kernel,
        out_shape=out_shape,
        in_specs=in_specs,
        out_specs=jax.tree.map(lambda _: VMEM, out_shape) if out_specs is None else out_specs,
        scratch_shapes=list(scratch),
        compiler_params=PARAMS,
        cost_estimate=pl.CostEstimate(flops=flops, bytes_accessed=moved, transcendentals=0),
    )


def decode(code):
    return code & 31, (code >> 5) & 7, code >> 8


def prepare_kernel(place, links_own, links_sib, table, info):
    fact_pos, dim_pos, core = place[0], place[1], place[2]
    for side, links in enumerate((links_own, links_sib)):
        n = jnp.int32(0)
        for slot in range(32):
            target = links[0, slot] - fact_pos * 32
            info[side * LIST + n] = slot + ((links[1, slot] >> 5) << 5) + ((target >> 1) << 8)
            n = n + jnp.where((slot < links[0, 32]) & ((target & 1) == core), 1, 0)
        for spare in range(UNROLL - 1):
            info[side * LIST + n + spare] = 16 << 8
        info[COUNT + side] = n
    for i in range(4):
        info[PLACE + i] = place[i]
    for h in range(8):
        info[KIND + h] = table[h * 32 + dim_pos]
        info[KIND + 8 + h] = table[h * 32 + dim_pos + 1 - 2 * core]


def project_kernel(info, w, facts, *refs):
    early, (proj, facts_t) = refs[:-2], refs[-2:]
    at = 0
    for side in range(2):
        for shift in ORDER[:EARLY]:
            kind = info[KIND + side * 8 + ((info[PLACE] + shift) & 7)]
            proj[at] = jnp.dot(early[at][...], w[kind], preferred_element_type=F32).astype(BF16)
            at += 1
    facts_t[...] = facts[...].astype(F32).T.astype(BF16)


def forward_kernel(info, proj, *refs):
    late = 9 - EARLY
    sides, (w, facts_t, tiles_own, tiles_sib, out, panel, acc) = (refs[:late], refs[late : 2 * late]), refs[2 * late :]
    fact_pos = info[PLACE]
    for side, pieces in enumerate(sides):
        for at, shift in enumerate(ORDER[:EARLY]):
            panel[side * 8 + ((fact_pos + shift) & 7)] = proj[side * EARLY + at]
        blocks = [x[...] for x in pieces[:-2]] + [jnp.concatenate([pieces[-2][...], pieces[-1][...]], axis=0)]
        for shift, rows in zip(ORDER[EARLY:] + (4,), blocks):
            h = (fact_pos + shift) & 7
            value = jnp.dot(rows, w[info[KIND + side * 8 + h]], preferred_element_type=F32)
            panel[side * 8 + h] = value.astype(BF16)
    acc[...] = jnp.zeros_like(acc)
    for side, tiles in enumerate((tiles_own, tiles_sib)):

        def step(i, carry, side=side, tiles=tiles):
            found = []
            for u in range(UNROLL):
                slot, holder, chip = decode(info[side * LIST + i * UNROLL + u])
                found.append((chip, jnp.dot(tiles[slot], panel[side * 8 + holder], preferred_element_type=F32)))
            for chip, value in found:
                acc[chip] += value
            return carry

        lax.fori_loop(0, (info[COUNT + side] + UNROLL - 1) // UNROLL, step, 0)
    for chip in range(out.shape[0]):
        for q in range(4):
            out[chip, q * 128 : (q + 1) * 128, :] = acc[chip, :, q * 128 : (q + 1) * 128].astype(BF16)
        out[chip, 512:544, :] = facts_t[chip * 32 : (chip + 1) * 32, :]


def middle_kernel(parts, facts, w, cot, fact_out, spread, facts_t):
    pre = jnp.dot(facts[...], w[...], preferred_element_type=F32)
    aggs = []
    for q in range(4):
        agg = parts[0, q * 128 : (q + 1) * 128, :].astype(F32)
        for chip in range(1, parts.shape[0]):
            agg = agg + parts[chip, q * 128 : (q + 1) * 128, :].astype(F32)
        aggs.append(agg)
    pre = pre + jnp.concatenate(aggs, axis=1)
    sig = jax.nn.sigmoid(pre)
    fact_out[...] = (pre * sig).astype(BF16)
    grad = cot[...].astype(F32) * sig * (1.0 + pre * (1.0 - sig))
    turned = grad.T.astype(BF16)
    for chip in range(spread.shape[0]):
        spread[chip] = turned
        facts_t[chip] = parts[chip, 512:544, :]


def backward_kernel(info, grads, facts_t, tiles_own, tiles_sib, keep, give, acc, weight):
    fact_pos, core = info[PLACE], info[PLACE + 2]
    acc[...] = jnp.zeros_like(acc)
    for side, tiles in enumerate((tiles_own, tiles_sib)):
        base = 8 * (core if side == 0 else 1 - core)

        def step(i, carry, side=side, tiles=tiles, base=base):
            found = []
            for u in range(UNROLL):
                slot, holder, chip = decode(info[side * LIST + i * UNROLL + u])
                at = jnp.where(chip == 16, 16, base + holder)
                value = jnp.dot(grads[jnp.minimum(chip, 15)], tiles[slot], preferred_element_type=F32)
                found.append((at, value))
            for at, value in found:
                acc[at] += value
            return carry

        lax.fori_loop(0, (info[COUNT + side] + UNROLL - 1) // UNROLL, step, 0)
    piece, width = facts_t.shape[1], grads.shape[1]
    half = piece // 2
    total = jnp.zeros((piece, width), F32)
    for chip in range(grads.shape[0]):
        total = total + lax.dot_general(
            facts_t[chip], grads[chip], (((1,), (1,)), ((), ())), preferred_element_type=F32
        )
    for q in range(4):
        weight[q] = total[:, q * 128 : (q + 1) * 128]
    for out, who, kind in ((keep, core, F32), (give, 1 - core, BF16)):
        for k in range(8):
            z = (fact_pos + k) & 7
            features = pl.ds(pl.multiple_of(who * 256 + z * 32, 32), 32)
            for at in range(16):
                out[k, at * 32 : (at + 1) * 32, :] = acc[at, features, :].astype(kind)
            rows = pl.ds(pl.multiple_of(who * half + (z & 1) * 8, 8), 8)
            mine = weight[z >> 1, rows, :]
            out[k, 512:528, :] = jnp.concatenate([mine, jnp.zeros_like(mine)], axis=0).astype(kind)


def slice_kernel(info, kept, given, from_below, from_above, from_far, *refs):
    pieces, (tab, gsum, self_piece, tacc) = refs[:18], refs[18:]
    fact_pos, core = info[PLACE], info[PLACE + 2]
    total = kept[...]
    for arrived in (given, from_below, from_above, from_far):
        total = total + arrived[...].astype(F32)
    self_piece[...] = total[512:520]
    for at in range(16):
        gsum[at] = total[at * 32 : (at + 1) * 32].astype(BF16)
    tacc[...] = jnp.zeros_like(tacc)
    for side in range(2):
        column = 8 * (core if side == 0 else 1 - core)
        for at, shift in enumerate(ORDER + (4,)):
            h = (fact_pos + shift) & 7
            kind = info[KIND + side * 8 + h]
            grad = gsum[column + h]
            if shift == 4:
                low, high = pieces[side * 9 + 7], pieces[side * 9 + 8]
                rows = jnp.concatenate([low[...], high[...]], axis=0)
            else:
                rows = pieces[side * 9 + at][...]
            tacc[kind] += jnp.dot(grad, rows, preferred_element_type=F32)
    for q in range(4):
        for t in range(3):
            at = q * 96 + t * 32
            tab[at : at + 32, :] = tacc[t, :, q * 128 : (q + 1) * 128].astype(BF16)


def pack_kernel(info, parts, gsum, self_piece, out):
    core = info[PLACE + 2]
    total = jnp.sum(parts[...].astype(F32), axis=0)
    piece = jnp.concatenate([total, self_piece[...]], axis=0).astype(BF16)
    for z in range(out.shape[0]):
        out[z, 0:32, :] = gsum[core * 8 + z]
        out[z, 32:64, :] = gsum[(1 - core) * 8 + z]
        out[z, 64:96, :] = piece


def rows_kernel(info, kept, given, w, grad_dims):
    even = info[PLACE + 2] == 0
    kind = info[KIND + info[PLACE]]
    mine, other = kept[...].astype(F32).reshape(256, 128), given[...].astype(F32).reshape(256, 128)
    turned = jnp.concatenate([jnp.where(even, mine, other), jnp.where(even, other, mine)], axis=0)
    grad_dims[...] = lax.dot_general(
        turned.T.astype(BF16), w[kind], (((1,), (1,)), ((), ())), preferred_element_type=F32
    )


def final_kernel(info, own, sib, grad_self, grad_tab):
    even = info[PLACE + 2] == 0
    scale = F32(32768.0**-0.5)
    q = pl.program_id(0)

    def both_cores(chip, z):
        mine, other = own[chip, z].astype(F32) * scale, sib[chip, z].astype(F32) * scale
        return jnp.where(even, mine, other), jnp.where(even, other, mine)

    for chip in range(16):
        for half in range(2):
            for core, piece in enumerate(both_cores(chip, 2 * q + half)):
                row = (2 * chip + core) * 16 + half * 8
                grad_self[row : row + 8, :] = piece[24:32]
    for group in range(2):
        tables = [[[], [], []], [[], [], []]]
        for z in range(4 * group, 4 * group + 4):
            for i in range(4):
                first = i * 24
                for core, piece in enumerate(both_cores(4 * q + i, z)):
                    for t in range(3):
                        lo, hi = max(first, t * 32), min(first + 24, t * 32 + 32)
                        if lo < hi:
                            tables[core][t].append(piece[lo - first : hi - first])
        for core in range(2):
            for t in range(3):
                column = core * 256 + group * 128
                grad_tab[t, :, column : column + 128] = jnp.concatenate(tables[core][t], axis=0).T


def body(facts, dims, tiles, links, link_count, block_table, w_self, w_tables, cot):
    n_fact = lax.axis_size("fact")
    n_dim = lax.axis_size("dim")
    fact_pos = lax.axis_index("fact")
    dim_pos = lax.axis_index("dim")
    chips = n_dim // 2
    same = [[2 * m + core for m in range(chips)] for core in range(2)]
    pair = [(d, d ^ 1) for d in range(n_dim)]
    rows, width = dims.shape
    slots, block, _ = tiles.shape
    place = jnp.stack([fact_pos, dim_pos, dim_pos & 1, dim_pos >> 1]).astype(jnp.int32)

    def swap(x):
        return lax.ppermute(x, "dim", pair)

    def shift(x, by):
        return lax.ppermute(x, "fact", [(i, (i + by) % n_fact) for i in range(n_fact)])

    def by_chip(x):
        return lax.all_to_all(x, "dim", 0, 0, tiled=True, axis_index_groups=same)

    def by_fact(x):
        return lax.all_to_all(x, "fact", 0, 0, tiled=True)

    count = jnp.broadcast_to(link_count[None, :], (2, 1))
    links_own = jnp.concatenate([links.T, count], axis=1)
    links_sib = swap(links_own)
    info = call(
        prepare_kernel,
        jax.ShapeDtypeStruct((INFO,), jnp.int32),
        [SMEM] * 4,
        flops=1 << 31,
        moved=4096,
        out_specs=SMEM,
    )(place, links_own, links_sib, block_table)
    tiles_sib = swap(tiles)

    pieces, up, down = [dims], dims, dims
    for step in range(3):
        if step == 2:
            up, down, info = lax.optimization_barrier((up, down, info))
        up, down = shift(up, 1), shift(down, -1)
        pieces += [up, down]
    pieces_sib = [swap(x) for x in pieces]
    far = [shift(up[: rows // 2], 1), shift(down[rows // 2 :], -1)]
    early = pieces[:EARLY] + pieces_sib[:EARLY]
    proj, facts_t = call(
        project_kernel,
        (jax.ShapeDtypeStruct((len(early), rows, width), BF16), jax.ShapeDtypeStruct((width, block), BF16)),
        [SMEM] + [VMEM] * (2 + len(early)),
        flops=2 * len(early) * rows * width * width,
        moved=4 << 20,
    )(info, w_tables, facts, *early)
    *far, proj = lax.optimization_barrier((*far, proj))
    pieces, pieces_sib = pieces + far, pieces_sib + [swap(x) for x in far]
    partial = call(
        forward_kernel,
        jax.ShapeDtypeStruct((chips, 544, 128), BF16),
        [SMEM] + [VMEM] * (5 + 2 * (9 - EARLY)),
        [pltpu.VMEM((2 * n_fact, rows, width), BF16), pltpu.VMEM((chips + 1, block, width), F32)],
        flops=2 * slots * block * block * width,
        moved=8 << 20,
    )(info, proj, *pieces[EARLY:], *pieces_sib[EARLY:], w_tables, facts_t, tiles, tiles_sib)
    parts = by_chip(partial)

    fact_out, spread, facts_t = call(
        middle_kernel,
        (
            jax.ShapeDtypeStruct((block, width), BF16),
            jax.ShapeDtypeStruct((chips, width, block), BF16),
            jax.ShapeDtypeStruct((chips, width // chips, block), BF16),
        ),
        [VMEM] * 4,
        flops=2 * block * width * width,
        moved=5 << 20,
    )(parts, facts, w_self, cot)
    grads = by_chip(spread)

    keep, give = call(
        backward_kernel,
        (jax.ShapeDtypeStruct((n_fact, 528, 128), F32), jax.ShapeDtypeStruct((n_fact, 528, 128), BF16)),
        [SMEM] + [VMEM] * 4,
        [pltpu.VMEM((2 * n_fact + 1, width, block), F32), pltpu.VMEM((4, width // chips, 128), F32)],
        flops=2 * slots * block * block * width,
        moved=9 << 20,
    )(info, grads, facts_t, tiles, tiles_sib)
    give = swap(give)

    def partial_sum(k, arrived):
        return (keep[k] + give[k].astype(F32) + arrived.astype(F32)).astype(BF16)

    up = shift((keep[3] + give[3].astype(F32)).astype(BF16), 1)
    down = shift((keep[5] + give[5].astype(F32)).astype(BF16), -1)
    far, up, down = lax.optimization_barrier(((keep[4] + give[4].astype(F32)).astype(BF16), up, down))
    far = shift(far, 4)
    for k in (2, 1):
        up, down = lax.optimization_barrier((partial_sum(k, up), partial_sum(8 - k, down)))
        up, down = shift(up, 1), shift(down, -1)

    tab, gsum, self_piece = call(
        slice_kernel,
        (
            jax.ShapeDtypeStruct((384, 128), BF16),
            jax.ShapeDtypeStruct((2 * n_fact, 32, 128), BF16),
            jax.ShapeDtypeStruct((8, 128), F32),
        ),
        [SMEM] + [VMEM] * 23,
        [pltpu.VMEM((3, 32, width), F32)],
        flops=4 * n_fact * 32 * 128 * width,
        moved=3 << 20,
    )(info, keep[0], give[0], up, down, far, *pieces, *pieces_sib)
    tab = by_chip(tab.reshape(chips, 24, 128))
    packed = call(
        pack_kernel, jax.ShapeDtypeStruct((n_fact, 96, 128), BF16), [SMEM] + [VMEM] * 3, moved=1 << 19
    )(info, tab, gsum, self_piece)
    packed = by_fact(packed)
    pieces_own = by_chip(jnp.broadcast_to(packed[None, :, 64:, :], (chips, n_fact, 32, 128)))
    given = swap(packed[:, 32:64, :])

    grad_dims = call(
        rows_kernel,
        jax.ShapeDtypeStruct((rows, width), F32),
        [SMEM] + [VMEM] * 3,
        flops=2 * rows * width * width,
        moved=2 << 20,
    )(info, packed[:, :32, :], given, w_tables)
    grad_self, grad_tab = pl.pallas_call(
        final_kernel,
        out_shape=(jax.ShapeDtypeStruct((width, width), F32), jax.ShapeDtypeStruct((3, width, width), F32)),
        grid=(4,),
        in_specs=[SMEM, VMEM, VMEM],
        out_specs=(
            pl.BlockSpec((width, 128), lambda q: (0, q)),
            pl.BlockSpec((3, 128, width), lambda q: (0, q, 0)),
        ),
        compiler_params=PARAMS,
        cost_estimate=pl.CostEstimate(flops=0, bytes_accessed=8 << 20, transcendentals=0),
    )(info, pieces_own, swap(pieces_own))
    return (fact_out, grad_dims, grad_self, grad_tab)


def solution(mesh):
    split = P(("fact", "dim"), None)
    return jax.shard_map(
        body,
        mesh=mesh,
        in_specs=(split, split, P(("fact", "dim"), None, None), split, P(("fact", "dim")), P(), P(), P(), split),
        out_specs=(split, split, P(), P()),
        check_vma=False,
    )
```

```python
import jax
import jax.numpy as jnp
from jax import lax
from jax.experimental import pallas as pl
from jax.experimental.pallas import tpu as pltpu
from jax.sharding import PartitionSpec as P

F32 = jnp.float32
BF16 = jnp.bfloat16
VMEM = pl.BlockSpec(memory_space=pltpu.VMEM)
SMEM = pl.BlockSpec(memory_space=pltpu.SMEM)
PARAMS = pltpu.CompilerParams(vmem_limit_bytes=24 * 1024 * 1024)
UNROLL = 4


ORDER = (0, -1, 1, -2, 2, 4, -3, 3)
EARLY = 6
LIST = 40
COUNT, KIND, PLACE, INFO = 80, 96, 112, 128


def call(kernel, out_shape, in_specs, scratch=(), flops=0, moved=0, out_specs=None):
    return pl.pallas_call(
        kernel,
        out_shape=out_shape,
        in_specs=in_specs,
        out_specs=jax.tree.map(lambda _: VMEM, out_shape) if out_specs is None else out_specs,
        scratch_shapes=list(scratch),
        compiler_params=PARAMS,
        cost_estimate=pl.CostEstimate(flops=flops, bytes_accessed=moved, transcendentals=0),
    )


def decode(code):
    return code & 31, (code >> 5) & 7, code >> 8


def prepare_kernel(place, links_own, links_sib, table, info):
    fact_pos, dim_pos, core = place[0], place[1], place[2]
    for side, links in enumerate((links_own, links_sib)):
        n = jnp.int32(0)
        for slot in range(32):
            target = links[0, slot] - fact_pos * 32
            info[side * LIST + n] = slot + ((links[1, slot] >> 5) << 5) + ((target >> 1) << 8)
            n = n + jnp.where((slot < links[0, 32]) & ((target & 1) == core), 1, 0)
        for spare in range(UNROLL - 1):
            info[side * LIST + n + spare] = 16 << 8
        info[COUNT + side] = n
    for i in range(4):
        info[PLACE + i] = place[i]
    for h in range(8):
        info[KIND + h] = table[h * 32 + dim_pos]
        info[KIND + 8 + h] = table[h * 32 + dim_pos + 1 - 2 * core]


def project_kernel(info, w, facts, *refs):
    early, (proj, facts_t) = refs[:-2], refs[-2:]
    at = 0
    for side in range(2):
        for shift in ORDER[:EARLY]:
            kind = info[KIND + side * 8 + ((info[PLACE] + shift) & 7)]
            proj[at] = jnp.dot(early[at][...], w[kind], preferred_element_type=F32).astype(BF16)
            at += 1
    facts_t[...] = facts[...].astype(F32).T.astype(BF16)


def forward_kernel(info, proj, *refs):
    late = len(ORDER) - EARLY
    sides, (w, facts_t, tiles_own, tiles_sib, out, panel, acc) = (refs[:late], refs[late : 2 * late]), refs[2 * late :]
    fact_pos = info[PLACE]
    for side, pieces in enumerate(sides):
        for at, shift in enumerate(ORDER[:EARLY]):
            panel[side * 8 + ((fact_pos + shift) & 7)] = proj[side * EARLY + at]
        for shift, rows in zip(ORDER[EARLY:], pieces):
            h = (fact_pos + shift) & 7
            value = jnp.dot(rows[...], w[info[KIND + side * 8 + h]], preferred_element_type=F32)
            panel[side * 8 + h] = value.astype(BF16)
    acc[...] = jnp.zeros_like(acc)
    for side, tiles in enumerate((tiles_own, tiles_sib)):

        def step(i, carry, side=side, tiles=tiles):
            found = []
            for u in range(UNROLL):
                slot, holder, chip = decode(info[side * LIST + i * UNROLL + u])
                found.append((chip, jnp.dot(tiles[slot], panel[side * 8 + holder], preferred_element_type=F32)))
            for chip, value in found:
                acc[chip] += value
            return carry

        lax.fori_loop(0, (info[COUNT + side] + UNROLL - 1) // UNROLL, step, 0)
    for chip in range(out.shape[0]):
        for q in range(4):
            out[chip, q * 128 : (q + 1) * 128, :] = acc[chip, :, q * 128 : (q + 1) * 128].astype(BF16)
        out[chip, 512:544, :] = facts_t[chip * 32 : (chip + 1) * 32, :]


def middle_kernel(parts, facts, w, cot, fact_out, spread, facts_t):
    pre = jnp.dot(facts[...], w[...], preferred_element_type=F32)
    aggs = []
    for q in range(4):
        agg = parts[0, q * 128 : (q + 1) * 128, :].astype(F32)
        for chip in range(1, parts.shape[0]):
            agg = agg + parts[chip, q * 128 : (q + 1) * 128, :].astype(F32)
        aggs.append(agg)
    pre = pre + jnp.concatenate(aggs, axis=1)
    sig = jax.nn.sigmoid(pre)
    fact_out[...] = (pre * sig).astype(BF16)
    grad = cot[...].astype(F32) * sig * (1.0 + pre * (1.0 - sig))
    turned = grad.T.astype(BF16)
    for chip in range(spread.shape[0]):
        spread[chip] = turned
        facts_t[chip] = parts[chip, 512:544, :]


def backward_kernel(info, grads, facts_t, tiles_own, tiles_sib, keep, give, acc, weight):
    fact_pos, core = info[PLACE], info[PLACE + 2]
    acc[...] = jnp.zeros_like(acc)
    for side, tiles in enumerate((tiles_own, tiles_sib)):
        base = 8 * (core if side == 0 else 1 - core)

        def step(i, carry, side=side, tiles=tiles, base=base):
            found = []
            for u in range(UNROLL):
                slot, holder, chip = decode(info[side * LIST + i * UNROLL + u])
                at = jnp.where(chip == 16, 16, base + holder)
                value = jnp.dot(grads[jnp.minimum(chip, 15)], tiles[slot], preferred_element_type=F32)
                found.append((at, value))
            for at, value in found:
                acc[at] += value
            return carry

        lax.fori_loop(0, (info[COUNT + side] + UNROLL - 1) // UNROLL, step, 0)
    piece, width = facts_t.shape[1], grads.shape[1]
    half = piece // 2
    total = jnp.zeros((piece, width), F32)
    for chip in range(grads.shape[0]):
        total = total + lax.dot_general(
            facts_t[chip], grads[chip], (((1,), (1,)), ((), ())), preferred_element_type=F32
        )
    for q in range(4):
        weight[q] = total[:, q * 128 : (q + 1) * 128]
    for out, who, kind in ((keep, core, F32), (give, 1 - core, BF16)):
        for k in range(8):
            z = (fact_pos + k) & 7
            features = pl.ds(pl.multiple_of(who * 256 + z * 32, 32), 32)
            for at in range(16):
                out[k, at * 32 : (at + 1) * 32, :] = acc[at, features, :].astype(kind)
            rows = pl.ds(pl.multiple_of(who * half + (z & 1) * 8, 8), 8)
            mine = weight[z >> 1, rows, :]
            out[k, 512:528, :] = jnp.concatenate([mine, jnp.zeros_like(mine)], axis=0).astype(kind)


def slice_kernel(info, kept, given, from_below, from_above, from_far, *refs):
    pieces, (tab, gsum_own, gsum_sib, self_piece, tacc, gsum) = refs[:16], refs[16:]
    fact_pos, core = info[PLACE], info[PLACE + 2]
    total = kept[...]
    for arrived in (given, from_below, from_above, from_far):
        total = total + arrived[...].astype(F32)
    self_piece[...] = total[512:520]
    for at in range(16):
        gsum[at] = total[at * 32 : (at + 1) * 32].astype(BF16)
    tacc[...] = jnp.zeros_like(tacc)
    for side in range(2):
        column = 8 * (core if side == 0 else 1 - core)
        for at, shift in enumerate(ORDER):
            h = (fact_pos + shift) & 7
            kind = info[KIND + side * 8 + h]
            rows = pieces[side * 8 + at][...]
            tacc[kind] += jnp.dot(gsum[column + h], rows, preferred_element_type=F32)
    for h in range(8):
        gsum_own[h] = gsum[core * 8 + h]
        gsum_sib[h] = gsum[(1 - core) * 8 + h]
    for q in range(4):
        for t in range(3):
            at = q * 96 + t * 32
            tab[at : at + 32, :] = tacc[t, :, q * 128 : (q + 1) * 128].astype(BF16)


def pack_kernel(parts, gsum, gsum_arrived, self_piece, out):
    total = jnp.sum(parts[...].astype(F32), axis=0)
    piece = jnp.concatenate([total, self_piece[...]], axis=0).astype(BF16)
    for z in range(out.shape[0]):
        out[z, 0:32, :] = gsum[z]
        out[z, 32:64, :] = gsum_arrived[z]
        out[z, 64:96, :] = piece


def rows_kernel(info, packed, w, grad_dims):
    even = info[PLACE + 2] == 0
    kind = info[KIND + info[PLACE]]
    mine = packed[:, 0:32, :].astype(F32).reshape(256, 128)
    other = packed[:, 32:64, :].astype(F32).reshape(256, 128)
    turned = jnp.concatenate([jnp.where(even, mine, other), jnp.where(even, other, mine)], axis=0)
    grad_dims[...] = lax.dot_general(
        turned.T.astype(BF16), w[kind], (((1,), (1,)), ((), ())), preferred_element_type=F32
    )


def final_kernel(info, own, sib, grad_self, grad_tab):
    even = info[PLACE + 2] == 0
    scale = F32(32768.0**-0.5)
    q = pl.program_id(0)

    def both_cores(chip, z):
        mine, other = own[chip, z].astype(F32) * scale, sib[chip, z].astype(F32) * scale
        return jnp.where(even, mine, other), jnp.where(even, other, mine)

    for chip in range(16):
        for half in range(2):
            for core, piece in enumerate(both_cores(chip, 2 * q + half)):
                row = (2 * chip + core) * 16 + half * 8
                grad_self[row : row + 8, :] = piece[24:32]
    for group in range(2):
        tables = [[[], [], []], [[], [], []]]
        for z in range(4 * group, 4 * group + 4):
            for i in range(4):
                first = i * 24
                for core, piece in enumerate(both_cores(4 * q + i, z)):
                    for t in range(3):
                        lo, hi = max(first, t * 32), min(first + 24, t * 32 + 32)
                        if lo < hi:
                            tables[core][t].append(piece[lo - first : hi - first])
        for core in range(2):
            for t in range(3):
                column = core * 256 + group * 128
                grad_tab[t, :, column : column + 128] = jnp.concatenate(tables[core][t], axis=0).T


def body(facts, dims, tiles, links, link_count, block_table, w_self, w_tables, cot):
    n_fact = lax.axis_size("fact")
    n_dim = lax.axis_size("dim")
    fact_pos = lax.axis_index("fact")
    dim_pos = lax.axis_index("dim")
    chips = n_dim // 2
    same = [[2 * m + core for m in range(chips)] for core in range(2)]
    pair = [(d, d ^ 1) for d in range(n_dim)]
    rows, width = dims.shape
    slots, block, _ = tiles.shape
    place = jnp.stack([fact_pos, dim_pos, dim_pos & 1, dim_pos >> 1]).astype(jnp.int32)

    def swap(x):
        return lax.ppermute(x, "dim", pair)

    def shift(x, by):
        return lax.ppermute(x, "fact", [(i, (i + by) % n_fact) for i in range(n_fact)])

    def by_chip(x):
        return lax.all_to_all(x, "dim", 0, 0, tiled=True, axis_index_groups=same)

    def by_fact(x):
        return lax.all_to_all(x, "fact", 0, 0, tiled=True)

    count = jnp.broadcast_to(link_count[None, :], (2, 1))
    links_own = jnp.concatenate([links.T, count], axis=1)
    links_sib = swap(links_own)
    info = call(
        prepare_kernel,
        jax.ShapeDtypeStruct((INFO,), jnp.int32),
        [SMEM] * 4,
        flops=1 << 31,
        moved=4096,
        out_specs=SMEM,
    )(place, links_own, links_sib, block_table)
    tiles_sib = swap(tiles)

    up, down = shift(dims, 1), shift(dims, -1)
    far, up, down = lax.optimization_barrier((dims, up, down))
    far = shift(far, 4)
    pieces = [dims, up, down]
    up, down = shift(up, 1), shift(down, -1)
    up, down, far, info = lax.optimization_barrier((up, down, far, info))
    pieces += [up, down, far]
    late = [shift(up, 1), shift(down, -1)]
    pieces_sib = [swap(x) for x in pieces]
    early = pieces + pieces_sib
    proj, facts_t = call(
        project_kernel,
        (jax.ShapeDtypeStruct((len(early), rows, width), BF16), jax.ShapeDtypeStruct((width, block), BF16)),
        [SMEM] + [VMEM] * (2 + len(early)),
        flops=2 * len(early) * rows * width * width,
        moved=4 << 20,
    )(info, w_tables, facts, *early)
    *late, proj = lax.optimization_barrier((*late, proj))
    late_sib = [swap(x) for x in late]
    partial = call(
        forward_kernel,
        jax.ShapeDtypeStruct((chips, 544, 128), BF16),
        [SMEM] + [VMEM] * (5 + 2 * len(late)),
        [pltpu.VMEM((2 * n_fact, rows, width), BF16), pltpu.VMEM((chips + 1, block, width), F32)],
        flops=2 * slots * block * block * width,
        moved=8 << 20,
    )(info, proj, *late, *late_sib, w_tables, facts_t, tiles, tiles_sib)
    parts = by_chip(partial)

    fact_out, spread, facts_t = call(
        middle_kernel,
        (
            jax.ShapeDtypeStruct((block, width), BF16),
            jax.ShapeDtypeStruct((chips, width, block), BF16),
            jax.ShapeDtypeStruct((chips, width // chips, block), BF16),
        ),
        [VMEM] * 4,
        flops=2 * block * width * width,
        moved=5 << 20,
    )(parts, facts, w_self, cot)
    grads = by_chip(spread)

    keep, give = call(
        backward_kernel,
        (jax.ShapeDtypeStruct((n_fact, 528, 128), F32), jax.ShapeDtypeStruct((n_fact, 528, 128), BF16)),
        [SMEM] + [VMEM] * 4,
        [pltpu.VMEM((2 * n_fact + 1, width, block), F32), pltpu.VMEM((4, width // chips, 128), F32)],
        flops=2 * slots * block * block * width,
        moved=9 << 20,
    )(info, grads, facts_t, tiles, tiles_sib)
    give = swap(give)

    def partial_sum(k, arrived):
        return (keep[k] + give[k].astype(F32) + arrived.astype(F32)).astype(BF16)

    up = shift((keep[3] + give[3].astype(F32)).astype(BF16), 1)
    down = shift((keep[5] + give[5].astype(F32)).astype(BF16), -1)
    far_sum, up, down = lax.optimization_barrier(((keep[4] + give[4].astype(F32)).astype(BF16), up, down))
    far_sum = shift(far_sum, 4)
    for k in (2, 1):
        up, down = lax.optimization_barrier((partial_sum(k, up), partial_sum(8 - k, down)))
        up, down = shift(up, 1), shift(down, -1)

    tab, gsum_own, gsum_sib, self_piece = call(
        slice_kernel,
        (
            jax.ShapeDtypeStruct((384, 128), BF16),
            jax.ShapeDtypeStruct((n_fact, 32, 128), BF16),
            jax.ShapeDtypeStruct((n_fact, 32, 128), BF16),
            jax.ShapeDtypeStruct((8, 128), F32),
        ),
        [SMEM] + [VMEM] * 21,
        [pltpu.VMEM((3, 32, width), F32), pltpu.VMEM((2 * n_fact, 32, 128), BF16)],
        flops=4 * n_fact * 32 * 128 * width,
        moved=3 << 20,
    )(info, keep[0], give[0], up, down, far_sum, *pieces, *late, *pieces_sib, *late_sib)
    gsum_arrived = swap(gsum_sib)
    tab = by_chip(tab.reshape(chips, 24, 128))
    packed = call(
        pack_kernel, jax.ShapeDtypeStruct((n_fact, 96, 128), BF16), [VMEM] * 4, moved=1 << 19
    )(tab, gsum_own, gsum_arrived, self_piece)
    packed = by_fact(packed)
    pieces_own = by_chip(jnp.broadcast_to(packed[None, :, 64:, :], (chips, n_fact, 32, 128)))

    grad_dims = call(
        rows_kernel,
        jax.ShapeDtypeStruct((rows, width), F32),
        [SMEM] + [VMEM] * 2,
        flops=2 * rows * width * width,
        moved=2 << 20,
    )(info, packed, w_tables)
    grad_self, grad_tab = pl.pallas_call(
        final_kernel,
        out_shape=(jax.ShapeDtypeStruct((width, width), F32), jax.ShapeDtypeStruct((3, width, width), F32)),
        grid=(4,),
        in_specs=[SMEM, VMEM, VMEM],
        out_specs=(
            pl.BlockSpec((width, 128), lambda q: (0, q)),
            pl.BlockSpec((3, 128, width), lambda q: (0, q, 0)),
        ),
        compiler_params=PARAMS,
        cost_estimate=pl.CostEstimate(flops=0, bytes_accessed=8 << 20, transcendentals=0),
    )(info, pieces_own, swap(pieces_own))
    return (fact_out, grad_dims, grad_self, grad_tab)


def solution(mesh):
    split = P(("fact", "dim"), None)
    return jax.shard_map(
        body,
        mesh=mesh,
        in_specs=(split, split, P(("fact", "dim"), None, None), split, P(("fact", "dim")), P(), P(), P(), split),
        out_specs=(split, split, P(), P()),
        check_vma=False,
    )
```

```python
import jax
import jax.numpy as jnp
from jax import lax
from jax.experimental import pallas as pl
from jax.experimental.pallas import tpu as pltpu
from jax.sharding import PartitionSpec as P

F32 = jnp.float32
BF16 = jnp.bfloat16
VMEM = pl.BlockSpec(memory_space=pltpu.VMEM)
SMEM = pl.BlockSpec(memory_space=pltpu.SMEM)
PARAMS = pltpu.CompilerParams(vmem_limit_bytes=24 * 1024 * 1024)
UNROLL = 4


ORDER = (0, -1, 1, -2, 2, -3, 3)
EARLY = 5
FIRST, REST = (3, 5), (0, 1, 2, 4, 6, 7)
LIST = 40
COUNT, KIND, PLACE, INFO = 80, 96, 112, 128


def call(kernel, out_shape, in_specs, scratch=(), flops=0, moved=0, out_specs=None):
    return pl.pallas_call(
        kernel,
        out_shape=out_shape,
        in_specs=in_specs,
        out_specs=jax.tree.map(lambda _: VMEM, out_shape) if out_specs is None else out_specs,
        scratch_shapes=list(scratch),
        compiler_params=PARAMS,
        cost_estimate=pl.CostEstimate(flops=flops, bytes_accessed=moved, transcendentals=0),
    )


def decode(code):
    return code & 31, (code >> 5) & 7, code >> 8


def prepare_kernel(place, links_own, links_sib, table, info):
    fact_pos, dim_pos, core = place[0], place[1], place[2]
    for side, links in enumerate((links_own, links_sib)):
        n = jnp.int32(0)
        for slot in range(32):
            target = links[0, slot] - fact_pos * 32
            info[side * LIST + n] = slot + ((links[1, slot] >> 5) << 5) + ((target >> 1) << 8)
            n = n + jnp.where((slot < links[0, 32]) & ((target & 1) == core), 1, 0)
        for spare in range(UNROLL - 1):
            info[side * LIST + n + spare] = 16 << 8
        info[COUNT + side] = n
    for i in range(4):
        info[PLACE + i] = place[i]
    for h in range(8):
        info[KIND + h] = table[h * 32 + dim_pos]
        info[KIND + 8 + h] = table[h * 32 + dim_pos + 1 - 2 * core]


def project_kernel(info, w, facts, *refs):
    early, (proj, facts_t) = refs[:-2], refs[-2:]
    at = 0
    for side in range(2):
        for shift in ORDER[:EARLY]:
            kind = info[KIND + side * 8 + ((info[PLACE] + shift) & 7)]
            proj[at] = jnp.dot(early[at][...], w[kind], preferred_element_type=F32).astype(BF16)
            at += 1
    facts_t[...] = facts[...].astype(F32).T.astype(BF16)


def forward_kernel(info, proj, *refs):
    late = 9 - EARLY
    sides, (w, facts_t, tiles_own, tiles_sib, out, panel, acc) = (refs[:late], refs[late : 2 * late]), refs[2 * late :]
    fact_pos = info[PLACE]
    for side, pieces in enumerate(sides):
        for at, shift in enumerate(ORDER[:EARLY]):
            panel[side * 8 + ((fact_pos + shift) & 7)] = proj[side * EARLY + at]
        blocks = [x[...] for x in pieces[:-2]] + [jnp.concatenate([pieces[-2][...], pieces[-1][...]], axis=0)]
        for shift, rows in zip(ORDER[EARLY:] + (4,), blocks):
            h = (fact_pos + shift) & 7
            value = jnp.dot(rows, w[info[KIND + side * 8 + h]], preferred_element_type=F32)
            panel[side * 8 + h] = value.astype(BF16)
    acc[...] = jnp.zeros_like(acc)
    for side, tiles in enumerate((tiles_own, tiles_sib)):

        def step(i, carry, side=side, tiles=tiles):
            found = []
            for u in range(UNROLL):
                slot, holder, chip = decode(info[side * LIST + i * UNROLL + u])
                found.append((chip, jnp.dot(tiles[slot], panel[side * 8 + holder], preferred_element_type=F32)))
            for chip, value in found:
                acc[chip] += value
            return carry

        lax.fori_loop(0, (info[COUNT + side] + UNROLL - 1) // UNROLL, step, 0)
    for chip in range(out.shape[0]):
        for q in range(4):
            out[chip, q * 128 : (q + 1) * 128, :] = acc[chip, :, q * 128 : (q + 1) * 128].astype(BF16)
        out[chip, 512:544, :] = facts_t[chip * 32 : (chip + 1) * 32, :]


def middle_kernel(parts, facts, w, cot, fact_out, spread, facts_t):
    pre = jnp.dot(facts[...], w[...], preferred_element_type=F32)
    aggs = []
    for q in range(4):
        agg = parts[0, q * 128 : (q + 1) * 128, :].astype(F32)
        for chip in range(1, parts.shape[0]):
            agg = agg + parts[chip, q * 128 : (q + 1) * 128, :].astype(F32)
        aggs.append(agg)
    pre = pre + jnp.concatenate(aggs, axis=1)
    sig = jax.nn.sigmoid(pre)
    fact_out[...] = (pre * sig).astype(BF16)
    grad = cot[...].astype(F32) * sig * (1.0 + pre * (1.0 - sig))
    turned = grad.T.astype(BF16)
    for chip in range(spread.shape[0]):
        spread[chip] = turned
        facts_t[chip] = parts[chip, 512:544, :]


def backward_kernel(info, grads, facts_t, tiles_own, tiles_sib, keep, give_first, give_rest, acc, weight):
    fact_pos, core = info[PLACE], info[PLACE + 2]
    acc[...] = jnp.zeros_like(acc)
    for side, tiles in enumerate((tiles_own, tiles_sib)):
        base = 8 * (core if side == 0 else 1 - core)

        def step(i, carry, side=side, tiles=tiles, base=base):
            found = []
            for u in range(UNROLL):
                slot, holder, chip = decode(info[side * LIST + i * UNROLL + u])
                at = jnp.where(chip == 16, 16, base + holder)
                value = jnp.dot(grads[jnp.minimum(chip, 15)], tiles[slot], preferred_element_type=F32)
                found.append((at, value))
            for at, value in found:
                acc[at] += value
            return carry

        lax.fori_loop(0, (info[COUNT + side] + UNROLL - 1) // UNROLL, step, 0)
    piece, width = facts_t.shape[1], grads.shape[1]
    half = piece // 2
    total = jnp.zeros((piece, width), F32)
    for chip in range(grads.shape[0]):
        total = total + lax.dot_general(
            facts_t[chip], grads[chip], (((1,), (1,)), ((), ())), preferred_element_type=F32
        )
    for q in range(4):
        weight[q] = total[:, q * 128 : (q + 1) * 128]
    given = [(give_first, at, k) for at, k in enumerate(FIRST)] + [(give_rest, at, k) for at, k in enumerate(REST)]
    for who, kind, slices in ((core, F32, [(keep, k, k) for k in range(8)]), (1 - core, BF16, given)):
        for out, at, k in slices:
            z = (fact_pos + k) & 7
            features = pl.ds(pl.multiple_of(who * 256 + z * 32, 32), 32)
            for block in range(16):
                out[at, block * 32 : (block + 1) * 32, :] = acc[block, features, :].astype(kind)
            rows = pl.ds(pl.multiple_of(who * half + (z & 1) * 8, 8), 8)
            mine = weight[z >> 1, rows, :]
            out[at, 512:528, :] = jnp.concatenate([mine, jnp.zeros_like(mine)], axis=0).astype(kind)


def slice_kernel(info, kept, given, from_below, from_above, from_far, *refs):
    pieces, (tab, gsum, self_piece, tacc) = refs[:18], refs[18:]
    fact_pos, core = info[PLACE], info[PLACE + 2]
    total = kept[...]
    for arrived in (given, from_below, from_above, from_far):
        total = total + arrived[...].astype(F32)
    self_piece[...] = total[512:520]
    for at in range(16):
        gsum[at] = total[at * 32 : (at + 1) * 32].astype(BF16)
    tacc[...] = jnp.zeros_like(tacc)
    for side in range(2):
        column = 8 * (core if side == 0 else 1 - core)
        for at, shift in enumerate(ORDER + (4,)):
            h = (fact_pos + shift) & 7
            kind = info[KIND + side * 8 + h]
            grad = gsum[column + h]
            if shift == 4:
                low, high = pieces[side * 9 + 7], pieces[side * 9 + 8]
                rows = jnp.concatenate([low[...], high[...]], axis=0)
            else:
                rows = pieces[side * 9 + at][...]
            tacc[kind] += jnp.dot(grad, rows, preferred_element_type=F32)
    for q in range(4):
        for t in range(3):
            at = q * 96 + t * 32
            tab[at : at + 32, :] = tacc[t, :, q * 128 : (q + 1) * 128].astype(BF16)


def pack_kernel(info, parts, gsum, self_piece, out):
    core = info[PLACE + 2]
    total = jnp.sum(parts[...].astype(F32), axis=0)
    piece = jnp.concatenate([total, self_piece[...]], axis=0).astype(BF16)
    for z in range(out.shape[0]):
        out[z, 0:32, :] = gsum[core * 8 + z]
        out[z, 32:64, :] = gsum[(1 - core) * 8 + z]
        out[z, 64:96, :] = piece


def rows_kernel(info, kept, given, w, grad_dims):
    even = info[PLACE + 2] == 0
    kind = info[KIND + info[PLACE]]
    mine, other = kept[...].astype(F32).reshape(256, 128), given[...].astype(F32).reshape(256, 128)
    turned = jnp.concatenate([jnp.where(even, mine, other), jnp.where(even, other, mine)], axis=0)
    grad_dims[...] = lax.dot_general(
        turned.T.astype(BF16), w[kind], (((1,), (1,)), ((), ())), preferred_element_type=F32
    )


def final_kernel(info, own, sib, grad_self, grad_tab):
    even = info[PLACE + 2] == 0
    scale = F32(32768.0**-0.5)
    q = pl.program_id(0)

    def both_cores(chip, z):
        mine, other = own[chip, z].astype(F32) * scale, sib[chip, z].astype(F32) * scale
        return jnp.where(even, mine, other), jnp.where(even, other, mine)

    for chip in range(16):
        for half in range(2):
            for core, piece in enumerate(both_cores(chip, 2 * q + half)):
                row = (2 * chip + core) * 16 + half * 8
                grad_self[row : row + 8, :] = piece[24:32]
    for group in range(2):
        tables = [[[], [], []], [[], [], []]]
        for z in range(4 * group, 4 * group + 4):
            for i in range(4):
                first = i * 24
                for core, piece in enumerate(both_cores(4 * q + i, z)):
                    for t in range(3):
                        lo, hi = max(first, t * 32), min(first + 24, t * 32 + 32)
                        if lo < hi:
                            tables[core][t].append(piece[lo - first : hi - first])
        for core in range(2):
            for t in range(3):
                column = core * 256 + group * 128
                grad_tab[t, :, column : column + 128] = jnp.concatenate(tables[core][t], axis=0).T


def body(facts, dims, tiles, links, link_count, block_table, w_self, w_tables, cot):
    n_fact = lax.axis_size("fact")
    n_dim = lax.axis_size("dim")
    fact_pos = lax.axis_index("fact")
    dim_pos = lax.axis_index("dim")
    chips = n_dim // 2
    same = [[2 * m + core for m in range(chips)] for core in range(2)]
    pair = [(d, d ^ 1) for d in range(n_dim)]
    rows, width = dims.shape
    slots, block, _ = tiles.shape
    place = jnp.stack([fact_pos, dim_pos, dim_pos & 1, dim_pos >> 1]).astype(jnp.int32)

    def swap(x):
        return lax.ppermute(x, "dim", pair)

    def shift(x, by):
        return lax.ppermute(x, "fact", [(i, (i + by) % n_fact) for i in range(n_fact)])

    def by_chip(x):
        return lax.all_to_all(x, "dim", 0, 0, tiled=True, axis_index_groups=same)

    def by_fact(x):
        return lax.all_to_all(x, "fact", 0, 0, tiled=True)

    count = jnp.broadcast_to(link_count[None, :], (2, 1))
    links_own = jnp.concatenate([links.T, count], axis=1)
    links_sib = swap(links_own)
    info = call(
        prepare_kernel,
        jax.ShapeDtypeStruct((INFO,), jnp.int32),
        [SMEM] * 4,
        flops=1 << 31,
        moved=4096,
        out_specs=SMEM,
    )(place, links_own, links_sib, block_table)
    tiles_sib = swap(tiles)

    pieces, up, down = [dims], dims, dims
    for step in range(3):
        if step == 1:
            up, down, info = lax.optimization_barrier((up, down, info))
        up, down = shift(up, 1), shift(down, -1)
        pieces += [up, down]
    pieces_sib = [swap(x) for x in pieces]
    far = [shift(up[: rows // 2], 1), shift(down[rows // 2 :], -1)]
    early = pieces[:EARLY] + pieces_sib[:EARLY]
    proj, facts_t = call(
        project_kernel,
        (jax.ShapeDtypeStruct((len(early), rows, width), BF16), jax.ShapeDtypeStruct((width, block), BF16)),
        [SMEM] + [VMEM] * (2 + len(early)),
        flops=2 * len(early) * rows * width * width,
        moved=4 << 20,
    )(info, w_tables, facts, *early)
    *far, proj = lax.optimization_barrier((*far, proj))
    pieces, pieces_sib = pieces + far, pieces_sib + [swap(x) for x in far]
    partial = call(
        forward_kernel,
        jax.ShapeDtypeStruct((chips, 544, 128), BF16),
        [SMEM] + [VMEM] * (5 + 2 * (9 - EARLY)),
        [pltpu.VMEM((2 * n_fact, rows, width), BF16), pltpu.VMEM((chips + 1, block, width), F32)],
        flops=2 * slots * block * block * width,
        moved=8 << 20,
    )(info, proj, *pieces[EARLY:], *pieces_sib[EARLY:], w_tables, facts_t, tiles, tiles_sib)
    parts = by_chip(partial)

    fact_out, spread, facts_t = call(
        middle_kernel,
        (
            jax.ShapeDtypeStruct((block, width), BF16),
            jax.ShapeDtypeStruct((chips, width, block), BF16),
            jax.ShapeDtypeStruct((chips, width // chips, block), BF16),
        ),
        [VMEM] * 4,
        flops=2 * block * width * width,
        moved=5 << 20,
    )(parts, facts, w_self, cot)
    grads = by_chip(spread)

    keep, give_first, give_rest = call(
        backward_kernel,
        (
            jax.ShapeDtypeStruct((n_fact, 528, 128), F32),
            jax.ShapeDtypeStruct((len(FIRST), 528, 128), BF16),
            jax.ShapeDtypeStruct((len(REST), 528, 128), BF16),
        ),
        [SMEM] + [VMEM] * 4,
        [pltpu.VMEM((2 * n_fact + 1, width, block), F32), pltpu.VMEM((4, width // chips, 128), F32)],
        flops=2 * slots * block * block * width,
        moved=9 << 20,
    )(info, grads, facts_t, tiles, tiles_sib)
    give_first, give_rest = lax.optimization_barrier((swap(give_first), give_rest))
    give_rest = swap(give_rest)
    give = {k: give_first[at] for at, k in enumerate(FIRST)}

    def partial_sum(k, arrived):
        return (keep[k] + give[k].astype(F32) + arrived.astype(F32)).astype(BF16)

    up = shift((keep[3] + give[3].astype(F32)).astype(BF16), 1)
    down = shift((keep[5] + give[5].astype(F32)).astype(BF16), -1)
    give_rest, up, down = lax.optimization_barrier((give_rest, up, down))
    give |= {k: give_rest[at] for at, k in enumerate(REST)}
    far = shift((keep[4] + give[4].astype(F32)).astype(BF16), 4)
    for k in (2, 1):
        up, down = lax.optimization_barrier((partial_sum(k, up), partial_sum(8 - k, down)))
        up, down = shift(up, 1), shift(down, -1)

    tab, gsum, self_piece = call(
        slice_kernel,
        (
            jax.ShapeDtypeStruct((384, 128), BF16),
            jax.ShapeDtypeStruct((2 * n_fact, 32, 128), BF16),
            jax.ShapeDtypeStruct((8, 128), F32),
        ),
        [SMEM] + [VMEM] * 23,
        [pltpu.VMEM((3, 32, width), F32)],
        flops=4 * n_fact * 32 * 128 * width,
        moved=3 << 20,
    )(info, keep[0], give[0], up, down, far, *pieces, *pieces_sib)
    tab = by_chip(tab.reshape(chips, 24, 128))
    packed = call(
        pack_kernel, jax.ShapeDtypeStruct((n_fact, 96, 128), BF16), [SMEM] + [VMEM] * 3, moved=1 << 19
    )(info, tab, gsum, self_piece)
    packed = by_fact(packed)
    pieces_own = by_chip(jnp.broadcast_to(packed[None, :, 64:, :], (chips, n_fact, 32, 128)))
    given = swap(packed[:, 32:64, :])

    grad_dims = call(
        rows_kernel,
        jax.ShapeDtypeStruct((rows, width), F32),
        [SMEM] + [VMEM] * 3,
        flops=2 * rows * width * width,
        moved=2 << 20,
    )(info, packed[:, :32, :], given, w_tables)
    grad_self, grad_tab = pl.pallas_call(
        final_kernel,
        out_shape=(jax.ShapeDtypeStruct((width, width), F32), jax.ShapeDtypeStruct((3, width, width), F32)),
        grid=(4,),
        in_specs=[SMEM, VMEM, VMEM],
        out_specs=(
            pl.BlockSpec((width, 128), lambda q: (0, q)),
            pl.BlockSpec((3, 128, width), lambda q: (0, q, 0)),
        ),
        compiler_params=PARAMS,
        cost_estimate=pl.CostEstimate(flops=0, bytes_accessed=8 << 20, transcendentals=0),
    )(info, pieces_own, swap(pieces_own))
    return (fact_out, grad_dims, grad_self, grad_tab)


def solution(mesh):
    split = P(("fact", "dim"), None)
    return jax.shard_map(
        body,
        mesh=mesh,
        in_specs=(split, split, P(("fact", "dim"), None, None), split, P(("fact", "dim")), P(), P(), P(), split),
        out_specs=(split, split, P(), P()),
        check_vma=False,
    )
```

```python
import jax
import jax.numpy as jnp
from jax import lax
from jax.experimental import pallas as pl
from jax.experimental.pallas import tpu as pltpu
from jax.sharding import PartitionSpec as P

F32 = jnp.float32
BF16 = jnp.bfloat16
VMEM = pl.BlockSpec(memory_space=pltpu.VMEM)
SMEM = pl.BlockSpec(memory_space=pltpu.SMEM)
PARAMS = pltpu.CompilerParams(vmem_limit_bytes=24 * 1024 * 1024)
UNROLL = 4


ORDER = (0, -1, 1, -2, 2, 4, -3, 3)
EARLY = 5
FIRST, REST = (3, 5), (0, 1, 2, 4, 6, 7)
LIST = 40
COUNT, KIND, PLACE, INFO = 80, 96, 112, 128


def call(kernel, out_shape, in_specs, scratch=(), flops=0, moved=0, out_specs=None):
    return pl.pallas_call(
        kernel,
        out_shape=out_shape,
        in_specs=in_specs,
        out_specs=jax.tree.map(lambda _: VMEM, out_shape) if out_specs is None else out_specs,
        scratch_shapes=list(scratch),
        compiler_params=PARAMS,
        cost_estimate=pl.CostEstimate(flops=flops, bytes_accessed=moved, transcendentals=0),
    )


def decode(code):
    return code & 31, (code >> 5) & 7, code >> 8


def prepare_kernel(place, links_own, links_sib, table, info):
    fact_pos, dim_pos, core = place[0], place[1], place[2]
    for side, links in enumerate((links_own, links_sib)):
        n = jnp.int32(0)
        for slot in range(32):
            target = links[0, slot] - fact_pos * 32
            info[side * LIST + n] = slot + ((links[1, slot] >> 5) << 5) + ((target >> 1) << 8)
            n = n + jnp.where((slot < links[0, 32]) & ((target & 1) == core), 1, 0)
        for spare in range(UNROLL - 1):
            info[side * LIST + n + spare] = 16 << 8
        info[COUNT + side] = n
    for i in range(4):
        info[PLACE + i] = place[i]
    for h in range(8):
        info[KIND + h] = table[h * 32 + dim_pos]
        info[KIND + 8 + h] = table[h * 32 + dim_pos + 1 - 2 * core]


def project_kernel(info, w, facts, *refs):
    early, (proj, facts_t) = refs[:-2], refs[-2:]
    at = 0
    for side in range(2):
        for shift in ORDER[:EARLY]:
            kind = info[KIND + side * 8 + ((info[PLACE] + shift) & 7)]
            proj[at] = jnp.dot(early[at][...], w[kind], preferred_element_type=F32).astype(BF16)
            at += 1
    facts_t[...] = facts[...].astype(F32).T.astype(BF16)


def forward_kernel(info, proj, *refs):
    late = len(ORDER) - EARLY
    sides, (w, facts_t, tiles_own, tiles_sib, out, panel, acc) = (refs[:late], refs[late : 2 * late]), refs[2 * late :]
    fact_pos = info[PLACE]
    for side, pieces in enumerate(sides):
        for at, shift in enumerate(ORDER[:EARLY]):
            panel[side * 8 + ((fact_pos + shift) & 7)] = proj[side * EARLY + at]
        for shift, rows in zip(ORDER[EARLY:], pieces):
            h = (fact_pos + shift) & 7
            value = jnp.dot(rows[...], w[info[KIND + side * 8 + h]], preferred_element_type=F32)
            panel[side * 8 + h] = value.astype(BF16)
    acc[...] = jnp.zeros_like(acc)
    for side, tiles in enumerate((tiles_own, tiles_sib)):

        def step(i, carry, side=side, tiles=tiles):
            found = []
            for u in range(UNROLL):
                slot, holder, chip = decode(info[side * LIST + i * UNROLL + u])
                found.append((chip, jnp.dot(tiles[slot], panel[side * 8 + holder], preferred_element_type=F32)))
            for chip, value in found:
                acc[chip] += value
            return carry

        lax.fori_loop(0, (info[COUNT + side] + UNROLL - 1) // UNROLL, step, 0)
    for chip in range(out.shape[0]):
        for q in range(4):
            out[chip, q * 128 : (q + 1) * 128, :] = acc[chip, :, q * 128 : (q + 1) * 128].astype(BF16)
        out[chip, 512:544, :] = facts_t[chip * 32 : (chip + 1) * 32, :]


def middle_kernel(parts, facts, w, cot, fact_out, spread, facts_t):
    pre = jnp.dot(facts[...], w[...], preferred_element_type=F32)
    aggs = []
    for q in range(4):
        agg = parts[0, q * 128 : (q + 1) * 128, :].astype(F32)
        for chip in range(1, parts.shape[0]):
            agg = agg + parts[chip, q * 128 : (q + 1) * 128, :].astype(F32)
        aggs.append(agg)
    pre = pre + jnp.concatenate(aggs, axis=1)
    sig = jax.nn.sigmoid(pre)
    fact_out[...] = (pre * sig).astype(BF16)
    grad = cot[...].astype(F32) * sig * (1.0 + pre * (1.0 - sig))
    turned = grad.T.astype(BF16)
    for chip in range(spread.shape[0]):
        spread[chip] = turned
        facts_t[chip] = parts[chip, 512:544, :]


def backward_kernel(info, grads, facts_t, tiles_own, tiles_sib, keep, give_first, give_rest, acc, weight):
    fact_pos, core = info[PLACE], info[PLACE + 2]
    acc[...] = jnp.zeros_like(acc)
    for side, tiles in enumerate((tiles_own, tiles_sib)):
        base = 8 * (core if side == 0 else 1 - core)

        def step(i, carry, side=side, tiles=tiles, base=base):
            found = []
            for u in range(UNROLL):
                slot, holder, chip = decode(info[side * LIST + i * UNROLL + u])
                at = jnp.where(chip == 16, 16, base + holder)
                value = jnp.dot(grads[jnp.minimum(chip, 15)], tiles[slot], preferred_element_type=F32)
                found.append((at, value))
            for at, value in found:
                acc[at] += value
            return carry

        lax.fori_loop(0, (info[COUNT + side] + UNROLL - 1) // UNROLL, step, 0)
    piece, width = facts_t.shape[1], grads.shape[1]
    half = piece // 2
    total = jnp.zeros((piece, width), F32)
    for chip in range(grads.shape[0]):
        total = total + lax.dot_general(
            facts_t[chip], grads[chip], (((1,), (1,)), ((), ())), preferred_element_type=F32
        )
    for q in range(4):
        weight[q] = total[:, q * 128 : (q + 1) * 128]
    given = [(give_first, at, k) for at, k in enumerate(FIRST)] + [(give_rest, at, k) for at, k in enumerate(REST)]
    for who, kind, slices in ((core, F32, [(keep, k, k) for k in range(8)]), (1 - core, BF16, given)):
        for out, at, k in slices:
            z = (fact_pos + k) & 7
            features = pl.ds(pl.multiple_of(who * 256 + z * 32, 32), 32)
            for block in range(16):
                out[at, block * 32 : (block + 1) * 32, :] = acc[block, features, :].astype(kind)
            rows = pl.ds(pl.multiple_of(who * half + (z & 1) * 8, 8), 8)
            mine = weight[z >> 1, rows, :]
            out[at, 512:528, :] = jnp.concatenate([mine, jnp.zeros_like(mine)], axis=0).astype(kind)


def slice_kernel(info, kept, given, from_below, from_above, from_far, *refs):
    pieces, (tab, gsum, self_piece, tacc) = refs[:16], refs[16:]
    fact_pos, core = info[PLACE], info[PLACE + 2]
    total = kept[...]
    for arrived in (given, from_below, from_above, from_far):
        total = total + arrived[...].astype(F32)
    self_piece[...] = total[512:520]
    for at in range(16):
        gsum[at] = total[at * 32 : (at + 1) * 32].astype(BF16)
    tacc[...] = jnp.zeros_like(tacc)
    for side in range(2):
        column = 8 * (core if side == 0 else 1 - core)
        for at, shift in enumerate(ORDER):
            h = (fact_pos + shift) & 7
            kind = info[KIND + side * 8 + h]
            rows = pieces[side * 8 + at][...]
            tacc[kind] += jnp.dot(gsum[column + h], rows, preferred_element_type=F32)
    for q in range(4):
        for t in range(3):
            at = q * 96 + t * 32
            tab[at : at + 32, :] = tacc[t, :, q * 128 : (q + 1) * 128].astype(BF16)


def pack_kernel(info, parts, gsum, self_piece, out):
    core = info[PLACE + 2]
    total = jnp.sum(parts[...].astype(F32), axis=0)
    piece = jnp.concatenate([total, self_piece[...]], axis=0).astype(BF16)
    for z in range(out.shape[0]):
        out[z, 0:32, :] = gsum[core * 8 + z]
        out[z, 32:64, :] = gsum[(1 - core) * 8 + z]
        out[z, 64:96, :] = piece


def final_kernel(info, own, sib, kept, given, w, grad_dims, grad_self, grad_tab):
    even = info[PLACE + 2] == 0
    scale = F32(32768.0**-0.5)
    q = pl.program_id(0)

    @pl.when(q == 0)
    def _():
        mine, other = kept[...].astype(F32).reshape(256, 128), given[...].astype(F32).reshape(256, 128)
        turned = jnp.concatenate([jnp.where(even, mine, other), jnp.where(even, other, mine)], axis=0)
        weight = w[info[KIND + info[PLACE]]]
        grad_dims[...] = lax.dot_general(
            turned.T.astype(BF16), weight, (((1,), (1,)), ((), ())), preferred_element_type=F32
        )

    def both_cores(chip, z):
        mine, other = own[chip, z].astype(F32) * scale, sib[chip, z].astype(F32) * scale
        return jnp.where(even, mine, other), jnp.where(even, other, mine)

    for chip in range(16):
        for half in range(2):
            for core, piece in enumerate(both_cores(chip, 2 * q + half)):
                row = (2 * chip + core) * 16 + half * 8
                grad_self[row : row + 8, :] = piece[24:32]
    for group in range(2):
        tables = [[[], [], []], [[], [], []]]
        for z in range(4 * group, 4 * group + 4):
            for i in range(4):
                first = i * 24
                for core, piece in enumerate(both_cores(4 * q + i, z)):
                    for t in range(3):
                        lo, hi = max(first, t * 32), min(first + 24, t * 32 + 32)
                        if lo < hi:
                            tables[core][t].append(piece[lo - first : hi - first])
        for core in range(2):
            for t in range(3):
                column = core * 256 + group * 128
                grad_tab[t, :, column : column + 128] = jnp.concatenate(tables[core][t], axis=0).T


def body(facts, dims, tiles, links, link_count, block_table, w_self, w_tables, cot):
    n_fact = lax.axis_size("fact")
    n_dim = lax.axis_size("dim")
    fact_pos = lax.axis_index("fact")
    dim_pos = lax.axis_index("dim")
    chips = n_dim // 2
    same = [[2 * m + core for m in range(chips)] for core in range(2)]
    pair = [(d, d ^ 1) for d in range(n_dim)]
    rows, width = dims.shape
    slots, block, _ = tiles.shape
    place = jnp.stack([fact_pos, dim_pos, dim_pos & 1, dim_pos >> 1]).astype(jnp.int32)

    def swap(x):
        return lax.ppermute(x, "dim", pair)

    def shift(x, by):
        return lax.ppermute(x, "fact", [(i, (i + by) % n_fact) for i in range(n_fact)])

    def by_chip(x):
        return lax.all_to_all(x, "dim", 0, 0, tiled=True, axis_index_groups=same)

    def by_fact(x):
        return lax.all_to_all(x, "fact", 0, 0, tiled=True)

    count = jnp.broadcast_to(link_count[None, :], (2, 1))
    links_own = jnp.concatenate([links.T, count], axis=1)
    links_sib = swap(links_own)
    info = call(
        prepare_kernel,
        jax.ShapeDtypeStruct((INFO,), jnp.int32),
        [SMEM] * 4,
        flops=1 << 31,
        moved=4096,
        out_specs=SMEM,
    )(place, links_own, links_sib, block_table)
    tiles_sib = swap(tiles)

    up, down = shift(dims, 1), shift(dims, -1)
    far, up, down, info = lax.optimization_barrier((dims, up, down, info))
    far = shift(far, 4)
    pieces = [dims, up, down]
    up, down = shift(up, 1), shift(down, -1)
    pieces += [up, down]
    up, down = lax.optimization_barrier((up, down))
    late = [far, shift(up, 1), shift(down, -1)]
    pieces_sib = [swap(x) for x in pieces]
    early = pieces + pieces_sib
    proj, facts_t = call(
        project_kernel,
        (jax.ShapeDtypeStruct((len(early), rows, width), BF16), jax.ShapeDtypeStruct((width, block), BF16)),
        [SMEM] + [VMEM] * (2 + len(early)),
        flops=2 * len(early) * rows * width * width,
        moved=4 << 20,
    )(info, w_tables, facts, *early)
    *late, proj = lax.optimization_barrier((*late, proj))
    late_sib = [swap(x) for x in late]
    partial = call(
        forward_kernel,
        jax.ShapeDtypeStruct((chips, 544, 128), BF16),
        [SMEM] + [VMEM] * (5 + 2 * len(late)),
        [pltpu.VMEM((2 * n_fact, rows, width), BF16), pltpu.VMEM((chips + 1, block, width), F32)],
        flops=2 * slots * block * block * width,
        moved=8 << 20,
    )(info, proj, *late, *late_sib, w_tables, facts_t, tiles, tiles_sib)
    parts = by_chip(partial)

    fact_out, spread, facts_t = call(
        middle_kernel,
        (
            jax.ShapeDtypeStruct((block, width), BF16),
            jax.ShapeDtypeStruct((chips, width, block), BF16),
            jax.ShapeDtypeStruct((chips, width // chips, block), BF16),
        ),
        [VMEM] * 4,
        flops=2 * block * width * width,
        moved=5 << 20,
    )(parts, facts, w_self, cot)
    grads = by_chip(spread)

    keep, give_first, give_rest = call(
        backward_kernel,
        (
            jax.ShapeDtypeStruct((n_fact, 528, 128), F32),
            jax.ShapeDtypeStruct((len(FIRST), 528, 128), BF16),
            jax.ShapeDtypeStruct((len(REST), 528, 128), BF16),
        ),
        [SMEM] + [VMEM] * 4,
        [pltpu.VMEM((2 * n_fact + 1, width, block), F32), pltpu.VMEM((4, width // chips, 128), F32)],
        flops=2 * slots * block * block * width,
        moved=9 << 20,
    )(info, grads, facts_t, tiles, tiles_sib)
    give_first, give_rest = lax.optimization_barrier((swap(give_first), give_rest))
    give_rest = swap(give_rest)
    give = {k: give_first[at] for at, k in enumerate(FIRST)}

    def partial_sum(k, arrived):
        return (keep[k] + give[k].astype(F32) + arrived.astype(F32)).astype(BF16)

    up = shift((keep[3] + give[3].astype(F32)).astype(BF16), 1)
    down = shift((keep[5] + give[5].astype(F32)).astype(BF16), -1)
    give_rest, up, down = lax.optimization_barrier((give_rest, up, down))
    give |= {k: give_rest[at] for at, k in enumerate(REST)}
    far_sum = shift((keep[4] + give[4].astype(F32)).astype(BF16), 4)
    for k in (2, 1):
        up, down = lax.optimization_barrier((partial_sum(k, up), partial_sum(8 - k, down)))
        up, down = shift(up, 1), shift(down, -1)

    tab, gsum, self_piece = call(
        slice_kernel,
        (
            jax.ShapeDtypeStruct((384, 128), BF16),
            jax.ShapeDtypeStruct((2 * n_fact, 32, 128), BF16),
            jax.ShapeDtypeStruct((8, 128), F32),
        ),
        [SMEM] + [VMEM] * 21,
        [pltpu.VMEM((3, 32, width), F32)],
        flops=4 * n_fact * 32 * 128 * width,
        moved=3 << 20,
    )(info, keep[0], give[0], up, down, far_sum, *pieces, *late, *pieces_sib, *late_sib)
    tab = by_chip(tab.reshape(chips, 24, 128))
    packed = call(
        pack_kernel, jax.ShapeDtypeStruct((n_fact, 96, 128), BF16), [SMEM] + [VMEM] * 3, moved=1 << 19
    )(info, tab, gsum, self_piece)
    packed = by_fact(packed)
    pieces_own = by_chip(jnp.broadcast_to(packed[None, :, 64:, :], (chips, n_fact, 32, 128)))
    given = swap(packed[:, 32:64, :])

    grad_dims, grad_self, grad_tab = pl.pallas_call(
        final_kernel,
        out_shape=(
            jax.ShapeDtypeStruct((rows, width), F32),
            jax.ShapeDtypeStruct((width, width), F32),
            jax.ShapeDtypeStruct((3, width, width), F32),
        ),
        grid=(4,),
        in_specs=[SMEM] + [VMEM] * 5,
        out_specs=(
            pl.BlockSpec((rows, width), lambda q: (0, 0)),
            pl.BlockSpec((width, 128), lambda q: (0, q)),
            pl.BlockSpec((3, 128, width), lambda q: (0, q, 0)),
        ),
        compiler_params=PARAMS,
        cost_estimate=pl.CostEstimate(flops=2 * rows * width * width, bytes_accessed=8 << 20, transcendentals=0),
    )(info, pieces_own, swap(pieces_own), packed[:, :32, :], given, w_tables)
    return (fact_out, grad_dims, grad_self, grad_tab)


def solution(mesh):
    split = P(("fact", "dim"), None)
    return jax.shard_map(
        body,
        mesh=mesh,
        in_specs=(split, split, P(("fact", "dim"), None, None), split, P(("fact", "dim")), P(), P(), P(), split),
        out_specs=(split, split, P(), P()),
        check_vma=False,
    )
```

```python
import jax
import jax.numpy as jnp
from jax import lax
from jax.experimental import pallas as pl
from jax.experimental.pallas import tpu as pltpu
from jax.sharding import PartitionSpec as P

F32 = jnp.float32
BF16 = jnp.bfloat16
VMEM = pl.BlockSpec(memory_space=pltpu.VMEM)
SMEM = pl.BlockSpec(memory_space=pltpu.SMEM)
PARAMS = pltpu.CompilerParams(vmem_limit_bytes=24 * 1024 * 1024)
UNROLL = 4


ORDER = (0, -1, 1, -2, 2, -3, 3)
EARLY = 5
FIRST, REST = (3, 5), (0, 1, 2, 4, 6, 7)
LIST = 40
COUNT, KIND, PLACE, INFO = 80, 96, 112, 128


def call(kernel, out_shape, in_specs, scratch=(), flops=0, moved=0, out_specs=None):
    return pl.pallas_call(
        kernel,
        out_shape=out_shape,
        in_specs=in_specs,
        out_specs=jax.tree.map(lambda _: VMEM, out_shape) if out_specs is None else out_specs,
        scratch_shapes=list(scratch),
        compiler_params=PARAMS,
        cost_estimate=pl.CostEstimate(flops=flops, bytes_accessed=moved, transcendentals=0),
    )


def decode(code):
    return code & 31, (code >> 5) & 7, code >> 8


def prepare_kernel(place, links_own, links_sib, table, info):
    fact_pos, dim_pos, core = place[0], place[1], place[2]
    for side, links in enumerate((links_own, links_sib)):
        n = jnp.int32(0)
        for slot in range(32):
            target = links[0, slot] - fact_pos * 32
            info[side * LIST + n] = slot + ((links[1, slot] >> 5) << 5) + ((target >> 1) << 8)
            n = n + jnp.where((slot < links[0, 32]) & ((target & 1) == core), 1, 0)
        for spare in range(UNROLL - 1):
            info[side * LIST + n + spare] = 16 << 8
        info[COUNT + side] = n
    for i in range(4):
        info[PLACE + i] = place[i]
    for h in range(8):
        info[KIND + h] = table[h * 32 + dim_pos]
        info[KIND + 8 + h] = table[h * 32 + dim_pos + 1 - 2 * core]


def project_kernel(info, w, facts, *refs):
    early, (proj, facts_t) = refs[:-2], refs[-2:]
    at = 0
    for side in range(2):
        for shift in ORDER[:EARLY]:
            kind = info[KIND + side * 8 + ((info[PLACE] + shift) & 7)]
            proj[at] = jnp.dot(early[at][...], w[kind], preferred_element_type=F32).astype(BF16)
            at += 1
    facts_t[...] = facts[...].astype(F32).T.astype(BF16)


def forward_kernel(info, proj, *refs):
    late = 9 - EARLY
    sides, (w, facts_t, tiles_own, tiles_sib, out, panel, acc) = (refs[:late], refs[late : 2 * late]), refs[2 * late :]
    fact_pos = info[PLACE]
    for side, pieces in enumerate(sides):
        for at, shift in enumerate(ORDER[:EARLY]):
            panel[side * 8 + ((fact_pos + shift) & 7)] = proj[side * EARLY + at]
        blocks = [x[...] for x in pieces[:-2]] + [jnp.concatenate([pieces[-2][...], pieces[-1][...]], axis=0)]
        for shift, rows in zip(ORDER[EARLY:] + (4,), blocks):
            h = (fact_pos + shift) & 7
            value = jnp.dot(rows, w[info[KIND + side * 8 + h]], preferred_element_type=F32)
            panel[side * 8 + h] = value.astype(BF16)
    acc[...] = jnp.zeros_like(acc)
    for side, tiles in enumerate((tiles_own, tiles_sib)):

        def step(i, carry, side=side, tiles=tiles):
            found = []
            for u in range(UNROLL):
                slot, holder, chip = decode(info[side * LIST + i * UNROLL + u])
                found.append((chip, jnp.dot(tiles[slot], panel[side * 8 + holder], preferred_element_type=F32)))
            for chip, value in found:
                acc[chip] += value
            return carry

        lax.fori_loop(0, (info[COUNT + side] + UNROLL - 1) // UNROLL, step, 0)
    for chip in range(out.shape[0]):
        for q in range(4):
            out[chip, q * 128 : (q + 1) * 128, :] = acc[chip, :, q * 128 : (q + 1) * 128].astype(BF16)
        out[chip, 512:544, :] = facts_t[chip * 32 : (chip + 1) * 32, :]


def middle_kernel(parts, facts, w, cot, fact_out, spread, facts_t):
    pre = jnp.dot(facts[...], w[...], preferred_element_type=F32)
    aggs = []
    for q in range(4):
        agg = parts[0, q * 128 : (q + 1) * 128, :].astype(F32)
        for chip in range(1, parts.shape[0]):
            agg = agg + parts[chip, q * 128 : (q + 1) * 128, :].astype(F32)
        aggs.append(agg)
    pre = pre + jnp.concatenate(aggs, axis=1)
    sig = jax.nn.sigmoid(pre)
    fact_out[...] = (pre * sig).astype(BF16)
    grad = cot[...].astype(F32) * sig * (1.0 + pre * (1.0 - sig))
    turned = grad.T.astype(BF16)
    for chip in range(spread.shape[0]):
        spread[chip] = turned
        facts_t[chip] = parts[chip, 512:544, :]


def backward_kernel(info, grads, facts_t, tiles_own, tiles_sib, keep, give_first, give_rest, acc, weight):
    fact_pos, core = info[PLACE], info[PLACE + 2]
    acc[...] = jnp.zeros_like(acc)
    for side, tiles in enumerate((tiles_own, tiles_sib)):
        base = 8 * (core if side == 0 else 1 - core)

        def step(i, carry, side=side, tiles=tiles, base=base):
            found = []
            for u in range(UNROLL):
                slot, holder, chip = decode(info[side * LIST + i * UNROLL + u])
                at = jnp.where(chip == 16, 16, base + holder)
                value = jnp.dot(grads[jnp.minimum(chip, 15)], tiles[slot], preferred_element_type=F32)
                found.append((at, value))
            for at, value in found:
                acc[at] += value
            return carry

        lax.fori_loop(0, (info[COUNT + side] + UNROLL - 1) // UNROLL, step, 0)
    piece, width = facts_t.shape[1], grads.shape[1]
    half = piece // 2
    total = jnp.zeros((piece, width), F32)
    for chip in range(grads.shape[0]):
        total = total + lax.dot_general(
            facts_t[chip], grads[chip], (((1,), (1,)), ((), ())), preferred_element_type=F32
        )
    for q in range(4):
        weight[q] = total[:, q * 128 : (q + 1) * 128]
    given = [(give_first, at, k) for at, k in enumerate(FIRST)] + [(give_rest, at, k) for at, k in enumerate(REST)]
    for who, kind, slices in ((core, F32, [(keep, k, k) for k in range(8)]), (1 - core, BF16, given)):
        for out, at, k in slices:
            z = (fact_pos + k) & 7
            features = pl.ds(pl.multiple_of(who * 256 + z * 32, 32), 32)
            for block in range(16):
                out[at, block * 32 : (block + 1) * 32, :] = acc[block, features, :].astype(kind)
            rows = pl.ds(pl.multiple_of(who * half + (z & 1) * 8, 8), 8)
            mine = weight[z >> 1, rows, :]
            out[at, 512:528, :] = jnp.concatenate([mine, jnp.zeros_like(mine)], axis=0).astype(kind)


def slice_kernel(info, kept, given, from_below, from_above, from_far, *refs):
    pieces, (tab, gsum, self_piece, tacc) = refs[:18], refs[18:]
    fact_pos, core = info[PLACE], info[PLACE + 2]
    total = kept[...]
    for arrived in (given, from_below, from_above, from_far):
        total = total + arrived[...].astype(F32)
    self_piece[...] = total[512:520]
    for at in range(16):
        gsum[at] = total[at * 32 : (at + 1) * 32].astype(BF16)
    tacc[...] = jnp.zeros_like(tacc)
    for side in range(2):
        column = 8 * (core if side == 0 else 1 - core)
        for at, shift in enumerate(ORDER + (4,)):
            h = (fact_pos + shift) & 7
            kind = info[KIND + side * 8 + h]
            grad = gsum[column + h]
            if shift == 4:
                low, high = pieces[side * 9 + 7], pieces[side * 9 + 8]
                rows = jnp.concatenate([low[...], high[...]], axis=0)
            else:
                rows = pieces[side * 9 + at][...]
            tacc[kind] += jnp.dot(grad, rows, preferred_element_type=F32)
    for q in range(4):
        for t in range(3):
            at = q * 96 + t * 32
            tab[at : at + 32, :] = tacc[t, :, q * 128 : (q + 1) * 128].astype(BF16)


def pack_kernel(info, parts, gsum, self_piece, out):
    core = info[PLACE + 2]
    total = jnp.sum(parts[...].astype(F32), axis=0)
    piece = jnp.concatenate([total, self_piece[...]], axis=0).astype(BF16)
    for z in range(out.shape[0]):
        out[z, 0:32, :] = gsum[core * 8 + z]
        out[z, 32:64, :] = gsum[(1 - core) * 8 + z]
        out[z, 64:96, :] = piece


def final_kernel(info, own, sib, kept, given, w, grad_dims, grad_self, grad_tab):
    even = info[PLACE + 2] == 0
    scale = F32(32768.0**-0.5)
    q = pl.program_id(0)

    @pl.when(q == 0)
    def _():
        mine, other = kept[...].astype(F32).reshape(256, 128), given[...].astype(F32).reshape(256, 128)
        turned = jnp.concatenate([jnp.where(even, mine, other), jnp.where(even, other, mine)], axis=0)
        weight = w[info[KIND + info[PLACE]]]
        grad_dims[...] = lax.dot_general(
            turned.T.astype(BF16), weight, (((1,), (1,)), ((), ())), preferred_element_type=F32
        )

    def both_cores(chip, z):
        mine, other = own[chip, z].astype(F32) * scale, sib[chip, z].astype(F32) * scale
        return jnp.where(even, mine, other), jnp.where(even, other, mine)

    for chip in range(16):
        for half in range(2):
            for core, piece in enumerate(both_cores(chip, 2 * q + half)):
                row = (2 * chip + core) * 16 + half * 8
                grad_self[row : row + 8, :] = piece[24:32]
    for group in range(2):
        tables = [[[], [], []], [[], [], []]]
        for z in range(4 * group, 4 * group + 4):
            for i in range(4):
                first = i * 24
                for core, piece in enumerate(both_cores(4 * q + i, z)):
                    for t in range(3):
                        lo, hi = max(first, t * 32), min(first + 24, t * 32 + 32)
                        if lo < hi:
                            tables[core][t].append(piece[lo - first : hi - first])
        for core in range(2):
            for t in range(3):
                column = core * 256 + group * 128
                grad_tab[t, :, column : column + 128] = jnp.concatenate(tables[core][t], axis=0).T


def body(facts, dims, tiles, links, link_count, block_table, w_self, w_tables, cot):
    n_fact = lax.axis_size("fact")
    n_dim = lax.axis_size("dim")
    fact_pos = lax.axis_index("fact")
    dim_pos = lax.axis_index("dim")
    chips = n_dim // 2
    same = [[2 * m + core for m in range(chips)] for core in range(2)]
    pair = [(d, d ^ 1) for d in range(n_dim)]
    rows, width = dims.shape
    slots, block, _ = tiles.shape
    place = jnp.stack([fact_pos, dim_pos, dim_pos & 1, dim_pos >> 1]).astype(jnp.int32)

    def swap(x):
        return lax.ppermute(x, "dim", pair)

    def shift(x, by):
        return lax.ppermute(x, "fact", [(i, (i + by) % n_fact) for i in range(n_fact)])

    def by_chip(x):
        return lax.all_to_all(x, "dim", 0, 0, tiled=True, axis_index_groups=same)

    def by_fact(x):
        return lax.all_to_all(x, "fact", 0, 0, tiled=True)

    count = jnp.broadcast_to(link_count[None, :], (2, 1))
    links_own = jnp.concatenate([links.T, count], axis=1)
    links_sib = swap(links_own)
    info = call(
        prepare_kernel,
        jax.ShapeDtypeStruct((INFO,), jnp.int32),
        [SMEM] * 4,
        flops=1 << 31,
        moved=4096,
        out_specs=SMEM,
    )(place, links_own, links_sib, block_table)
    tiles_sib = swap(tiles)

    pieces, up, down = [dims], dims, dims
    for step in range(3):
        if step == 1:
            up, down, info = lax.optimization_barrier((up, down, info))
        up, down = shift(up, 1), shift(down, -1)
        pieces += [up, down]
    pieces_sib = [swap(x) for x in pieces]
    far = [shift(up[: rows // 2], 1), shift(down[rows // 2 :], -1)]
    early = pieces[:EARLY] + pieces_sib[:EARLY]
    proj, facts_t = call(
        project_kernel,
        (jax.ShapeDtypeStruct((len(early), rows, width), BF16), jax.ShapeDtypeStruct((width, block), BF16)),
        [SMEM] + [VMEM] * (2 + len(early)),
        flops=2 * len(early) * rows * width * width,
        moved=4 << 20,
    )(info, w_tables, facts, *early)
    *far, proj = lax.optimization_barrier((*far, proj))
    pieces, pieces_sib = pieces + far, pieces_sib + [swap(x) for x in far]
    partial = call(
        forward_kernel,
        jax.ShapeDtypeStruct((chips, 544, 128), BF16),
        [SMEM] + [VMEM] * (5 + 2 * (9 - EARLY)),
        [pltpu.VMEM((2 * n_fact, rows, width), BF16), pltpu.VMEM((chips + 1, block, width), F32)],
        flops=2 * slots * block * block * width,
        moved=8 << 20,
    )(info, proj, *pieces[EARLY:], *pieces_sib[EARLY:], w_tables, facts_t, tiles, tiles_sib)
    parts = by_chip(partial)

    fact_out, spread, facts_t = call(
        middle_kernel,
        (
            jax.ShapeDtypeStruct((block, width), BF16),
            jax.ShapeDtypeStruct((chips, width, block), BF16),
            jax.ShapeDtypeStruct((chips, width // chips, block), BF16),
        ),
        [VMEM] * 4,
        flops=2 * block * width * width,
        moved=5 << 20,
    )(parts, facts, w_self, cot)
    grads = by_chip(spread)

    keep, give_first, give_rest = call(
        backward_kernel,
        (
            jax.ShapeDtypeStruct((n_fact, 528, 128), F32),
            jax.ShapeDtypeStruct((len(FIRST), 528, 128), BF16),
            jax.ShapeDtypeStruct((len(REST), 528, 128), BF16),
        ),
        [SMEM] + [VMEM] * 4,
        [pltpu.VMEM((2 * n_fact + 1, width, block), F32), pltpu.VMEM((4, width // chips, 128), F32)],
        flops=2 * slots * block * block * width,
        moved=9 << 20,
    )(info, grads, facts_t, tiles, tiles_sib)
    give_first, give_rest = lax.optimization_barrier((swap(give_first), give_rest))
    give_rest = swap(give_rest)
    give = {k: give_first[at] for at, k in enumerate(FIRST)}

    def partial_sum(k, arrived):
        return (keep[k] + give[k].astype(F32) + arrived.astype(F32)).astype(BF16)

    up = shift((keep[3] + give[3].astype(F32)).astype(BF16), 1)
    down = shift((keep[5] + give[5].astype(F32)).astype(BF16), -1)
    give_rest, up, down = lax.optimization_barrier((give_rest, up, down))
    give |= {k: give_rest[at] for at, k in enumerate(REST)}
    far = shift((keep[4] + give[4].astype(F32)).astype(BF16), 4)
    for k in (2, 1):
        up, down = lax.optimization_barrier((partial_sum(k, up), partial_sum(8 - k, down)))
        up, down = shift(up, 1), shift(down, -1)

    tab, gsum, self_piece = call(
        slice_kernel,
        (
            jax.ShapeDtypeStruct((384, 128), BF16),
            jax.ShapeDtypeStruct((2 * n_fact, 32, 128), BF16),
            jax.ShapeDtypeStruct((8, 128), F32),
        ),
        [SMEM] + [VMEM] * 23,
        [pltpu.VMEM((3, 32, width), F32)],
        flops=4 * n_fact * 32 * 128 * width,
        moved=3 << 20,
    )(info, keep[0], give[0], up, down, far, *pieces, *pieces_sib)
    tab = by_chip(tab.reshape(chips, 24, 128))
    packed = call(
        pack_kernel, jax.ShapeDtypeStruct((n_fact, 96, 128), BF16), [SMEM] + [VMEM] * 3, moved=1 << 19
    )(info, tab, gsum, self_piece)
    packed = by_fact(packed)
    pieces_own = by_chip(jnp.broadcast_to(packed[None, :, 64:, :], (chips, n_fact, 32, 128)))
    given = swap(packed[:, 32:64, :])

    grad_dims, grad_self, grad_tab = pl.pallas_call(
        final_kernel,
        out_shape=(
            jax.ShapeDtypeStruct((rows, width), F32),
            jax.ShapeDtypeStruct((width, width), F32),
            jax.ShapeDtypeStruct((3, width, width), F32),
        ),
        grid=(4,),
        in_specs=[SMEM] + [VMEM] * 5,
        out_specs=(
            pl.BlockSpec((rows, width), lambda q: (0, 0)),
            pl.BlockSpec((width, 128), lambda q: (0, q)),
            pl.BlockSpec((3, 128, width), lambda q: (0, q, 0)),
        ),
        compiler_params=PARAMS,
        cost_estimate=pl.CostEstimate(flops=2 * rows * width * width, bytes_accessed=8 << 20, transcendentals=0),
    )(info, pieces_own, swap(pieces_own), packed[:, :32, :], given, w_tables)
    return (fact_out, grad_dims, grad_self, grad_tab)


def solution(mesh):
    split = P(("fact", "dim"), None)
    return jax.shard_map(
        body,
        mesh=mesh,
        in_specs=(split, split, P(("fact", "dim"), None, None), split, P(("fact", "dim")), P(), P(), P(), split),
        out_specs=(split, split, P(), P()),
        check_vma=False,
    )
```

```python
import jax
import jax.numpy as jnp
from jax import lax
from jax.experimental import pallas as pl
from jax.experimental.pallas import tpu as pltpu
from jax.sharding import PartitionSpec as P

F32 = jnp.float32
BF16 = jnp.bfloat16
VMEM = pl.BlockSpec(memory_space=pltpu.VMEM)
SMEM = pl.BlockSpec(memory_space=pltpu.SMEM)
PARAMS = pltpu.CompilerParams(vmem_limit_bytes=24 * 1024 * 1024)
UNROLL = 8


ORDER = (0, -1, 1, -2, 2, -3, 3)
EARLY = 5
FIRST, REST = (3, 5), (0, 1, 2, 4, 6, 7)
LIST = 40
COUNT, KIND, PLACE, INFO = 80, 96, 112, 128


def call(kernel, out_shape, in_specs, scratch=(), flops=0, moved=0, out_specs=None):
    return pl.pallas_call(
        kernel,
        out_shape=out_shape,
        in_specs=in_specs,
        out_specs=jax.tree.map(lambda _: VMEM, out_shape) if out_specs is None else out_specs,
        scratch_shapes=list(scratch),
        compiler_params=PARAMS,
        cost_estimate=pl.CostEstimate(flops=flops, bytes_accessed=moved, transcendentals=0),
    )


def decode(code):
    return code & 31, (code >> 5) & 7, code >> 8


def prepare_kernel(place, links_own, links_sib, table, info):
    fact_pos, dim_pos, core = place[0], place[1], place[2]
    for side, links in enumerate((links_own, links_sib)):
        n = jnp.int32(0)
        for slot in range(32):
            target = links[0, slot] - fact_pos * 32
            info[side * LIST + n] = slot + ((links[1, slot] >> 5) << 5) + ((target >> 1) << 8)
            n = n + jnp.where((slot < links[0, 32]) & ((target & 1) == core), 1, 0)
        for spare in range(UNROLL - 1):
            info[side * LIST + n + spare] = 16 << 8
        info[COUNT + side] = n
    for i in range(4):
        info[PLACE + i] = place[i]
    for h in range(8):
        info[KIND + h] = table[h * 32 + dim_pos]
        info[KIND + 8 + h] = table[h * 32 + dim_pos + 1 - 2 * core]


def project_kernel(info, w, facts, *refs):
    early, (proj, facts_t) = refs[:-2], refs[-2:]
    at = 0
    for side in range(2):
        for shift in ORDER[:EARLY]:
            kind = info[KIND + side * 8 + ((info[PLACE] + shift) & 7)]
            proj[at] = jnp.dot(early[at][...], w[kind], preferred_element_type=F32).astype(BF16)
            at += 1
    facts_t[...] = facts[...].astype(F32).T.astype(BF16)


def forward_kernel(info, proj, *refs):
    late = 9 - EARLY
    sides, (w, facts_t, tiles_own, tiles_sib, out, panel, acc) = (refs[:late], refs[late : 2 * late]), refs[2 * late :]
    fact_pos = info[PLACE]
    for side, pieces in enumerate(sides):
        for at, shift in enumerate(ORDER[:EARLY]):
            panel[side * 8 + ((fact_pos + shift) & 7)] = proj[side * EARLY + at]
        blocks = [x[...] for x in pieces[:-2]] + [jnp.concatenate([pieces[-2][...], pieces[-1][...]], axis=0)]
        for shift, rows in zip(ORDER[EARLY:] + (4,), blocks):
            h = (fact_pos + shift) & 7
            value = jnp.dot(rows, w[info[KIND + side * 8 + h]], preferred_element_type=F32)
            panel[side * 8 + h] = value.astype(BF16)
    acc[...] = jnp.zeros_like(acc)
    for side, tiles in enumerate((tiles_own, tiles_sib)):

        def step(i, carry, side=side, tiles=tiles):
            found = []
            for u in range(UNROLL):
                slot, holder, chip = decode(info[side * LIST + i * UNROLL + u])
                found.append((chip, jnp.dot(tiles[slot], panel[side * 8 + holder], preferred_element_type=F32)))
            for chip, value in found:
                acc[chip] += value
            return carry

        lax.fori_loop(0, (info[COUNT + side] + UNROLL - 1) // UNROLL, step, 0)
    for chip in range(out.shape[0]):
        for q in range(4):
            out[chip, q * 128 : (q + 1) * 128, :] = acc[chip, :, q * 128 : (q + 1) * 128].astype(BF16)
        out[chip, 512:544, :] = facts_t[chip * 32 : (chip + 1) * 32, :]


def middle_kernel(parts, facts, w, cot, fact_out, spread, facts_t):
    pre = jnp.dot(facts[...], w[...], preferred_element_type=F32)
    aggs = []
    for q in range(4):
        agg = parts[0, q * 128 : (q + 1) * 128, :].astype(F32)
        for chip in range(1, parts.shape[0]):
            agg = agg + parts[chip, q * 128 : (q + 1) * 128, :].astype(F32)
        aggs.append(agg)
    pre = pre + jnp.concatenate(aggs, axis=1)
    sig = jax.nn.sigmoid(pre)
    fact_out[...] = (pre * sig).astype(BF16)
    grad = cot[...].astype(F32) * sig * (1.0 + pre * (1.0 - sig))
    turned = grad.T.astype(BF16)
    for chip in range(spread.shape[0]):
        spread[chip] = turned
        facts_t[chip] = parts[chip, 512:544, :]


def backward_kernel(info, grads, facts_t, tiles_own, tiles_sib, keep, give_first, give_rest, acc, weight):
    fact_pos, core = info[PLACE], info[PLACE + 2]
    acc[...] = jnp.zeros_like(acc)
    for side, tiles in enumerate((tiles_own, tiles_sib)):
        base = 8 * (core if side == 0 else 1 - core)

        def step(i, carry, side=side, tiles=tiles, base=base):
            found = []
            for u in range(UNROLL):
                slot, holder, chip = decode(info[side * LIST + i * UNROLL + u])
                at = jnp.where(chip == 16, 16, base + holder)
                value = jnp.dot(grads[jnp.minimum(chip, 15)], tiles[slot], preferred_element_type=F32)
                found.append((at, value))
            for at, value in found:
                acc[at] += value
            return carry

        lax.fori_loop(0, (info[COUNT + side] + UNROLL - 1) // UNROLL, step, 0)
    piece, width = facts_t.shape[1], grads.shape[1]
    half = piece // 2
    total = jnp.zeros((piece, width), F32)
    for chip in range(grads.shape[0]):
        total = total + lax.dot_general(
            facts_t[chip], grads[chip], (((1,), (1,)), ((), ())), preferred_element_type=F32
        )
    for q in range(4):
        weight[q] = total[:, q * 128 : (q + 1) * 128]
    given = [(give_first, at, k) for at, k in enumerate(FIRST)] + [(give_rest, at, k) for at, k in enumerate(REST)]
    for who, kind, slices in ((core, F32, [(keep, k, k) for k in range(8)]), (1 - core, BF16, given)):
        for out, at, k in slices:
            z = (fact_pos + k) & 7
            features = pl.ds(pl.multiple_of(who * 256 + z * 32, 32), 32)
            for block in range(16):
                out[at, block * 32 : (block + 1) * 32, :] = acc[block, features, :].astype(kind)
            rows = pl.ds(pl.multiple_of(who * half + (z & 1) * 8, 8), 8)
            mine = weight[z >> 1, rows, :]
            out[at, 512:528, :] = jnp.concatenate([mine, jnp.zeros_like(mine)], axis=0).astype(kind)


def slice_kernel(info, kept, given, from_below, from_above, from_far, *refs):
    pieces, (tab, gsum, self_piece, tacc) = refs[:18], refs[18:]
    fact_pos, core = info[PLACE], info[PLACE + 2]
    total = kept[...]
    for arrived in (given, from_below, from_above, from_far):
        total = total + arrived[...].astype(F32)
    self_piece[...] = total[512:520]
    for at in range(16):
        gsum[at] = total[at * 32 : (at + 1) * 32].astype(BF16)
    tacc[...] = jnp.zeros_like(tacc)
    for side in range(2):
        column = 8 * (core if side == 0 else 1 - core)
        for at, shift in enumerate(ORDER + (4,)):
            h = (fact_pos + shift) & 7
            kind = info[KIND + side * 8 + h]
            grad = gsum[column + h]
            if shift == 4:
                low, high = pieces[side * 9 + 7], pieces[side * 9 + 8]
                rows = jnp.concatenate([low[...], high[...]], axis=0)
            else:
                rows = pieces[side * 9 + at][...]
            tacc[kind] += jnp.dot(grad, rows, preferred_element_type=F32)
    for q in range(4):
        for t in range(3):
            at = q * 96 + t * 32
            tab[at : at + 32, :] = tacc[t, :, q * 128 : (q + 1) * 128].astype(BF16)


def pack_kernel(info, parts, gsum, self_piece, out):
    core = info[PLACE + 2]
    total = jnp.sum(parts[...].astype(F32), axis=0)
    piece = jnp.concatenate([total, self_piece[...]], axis=0).astype(BF16)
    for z in range(out.shape[0]):
        out[z, 0:32, :] = gsum[core * 8 + z]
        out[z, 32:64, :] = gsum[(1 - core) * 8 + z]
        out[z, 64:96, :] = piece


def final_kernel(info, own, sib, kept, given, w, grad_dims, grad_self, grad_tab):
    even = info[PLACE + 2] == 0
    scale = F32(32768.0**-0.5)
    q = pl.program_id(0)

    @pl.when(q == 0)
    def _():
        mine, other = kept[...].astype(F32).reshape(256, 128), given[...].astype(F32).reshape(256, 128)
        turned = jnp.concatenate([jnp.where(even, mine, other), jnp.where(even, other, mine)], axis=0)
        weight = w[info[KIND + info[PLACE]]]
        grad_dims[...] = lax.dot_general(
            turned.T.astype(BF16), weight, (((1,), (1,)), ((), ())), preferred_element_type=F32
        )

    def both_cores(chip, z):
        mine, other = own[chip, z].astype(F32) * scale, sib[chip, z].astype(F32) * scale
        return jnp.where(even, mine, other), jnp.where(even, other, mine)

    for chip in range(16):
        for half in range(2):
            for core, piece in enumerate(both_cores(chip, 2 * q + half)):
                row = (2 * chip + core) * 16 + half * 8
                grad_self[row : row + 8, :] = piece[24:32]
    for group in range(2):
        tables = [[[], [], []], [[], [], []]]
        for z in range(4 * group, 4 * group + 4):
            for i in range(4):
                first = i * 24
                for core, piece in enumerate(both_cores(4 * q + i, z)):
                    for t in range(3):
                        lo, hi = max(first, t * 32), min(first + 24, t * 32 + 32)
                        if lo < hi:
                            tables[core][t].append(piece[lo - first : hi - first])
        for core in range(2):
            for t in range(3):
                column = core * 256 + group * 128
                grad_tab[t, :, column : column + 128] = jnp.concatenate(tables[core][t], axis=0).T


def body(facts, dims, tiles, links, link_count, block_table, w_self, w_tables, cot):
    n_fact = lax.axis_size("fact")
    n_dim = lax.axis_size("dim")
    fact_pos = lax.axis_index("fact")
    dim_pos = lax.axis_index("dim")
    chips = n_dim // 2
    same = [[2 * m + core for m in range(chips)] for core in range(2)]
    pair = [(d, d ^ 1) for d in range(n_dim)]
    rows, width = dims.shape
    slots, block, _ = tiles.shape
    place = jnp.stack([fact_pos, dim_pos, dim_pos & 1, dim_pos >> 1]).astype(jnp.int32)

    def swap(x):
        return lax.ppermute(x, "dim", pair)

    def shift(x, by):
        return lax.ppermute(x, "fact", [(i, (i + by) % n_fact) for i in range(n_fact)])

    def by_chip(x):
        return lax.all_to_all(x, "dim", 0, 0, tiled=True, axis_index_groups=same)

    def by_fact(x):
        return lax.all_to_all(x, "fact", 0, 0, tiled=True)

    count = jnp.broadcast_to(link_count[None, :], (2, 1))
    links_own = jnp.concatenate([links.T, count], axis=1)
    links_sib = swap(links_own)
    info = call(
        prepare_kernel,
        jax.ShapeDtypeStruct((INFO,), jnp.int32),
        [SMEM] * 4,
        flops=1 << 31,
        moved=4096,
        out_specs=SMEM,
    )(place, links_own, links_sib, block_table)
    tiles_sib = swap(tiles)

    pieces, up, down = [dims], dims, dims
    for step in range(3):
        if step == 1:
            up, down, info = lax.optimization_barrier((up, down, info))
        up, down = shift(up, 1), shift(down, -1)
        pieces += [up, down]
    pieces_sib = [swap(x) for x in pieces]
    far = [shift(up[: rows // 2], 1), shift(down[rows // 2 :], -1)]
    early = pieces[:EARLY] + pieces_sib[:EARLY]
    proj, facts_t = call(
        project_kernel,
        (jax.ShapeDtypeStruct((len(early), rows, width), BF16), jax.ShapeDtypeStruct((width, block), BF16)),
        [SMEM] + [VMEM] * (2 + len(early)),
        flops=2 * len(early) * rows * width * width,
        moved=4 << 20,
    )(info, w_tables, facts, *early)
    *far, proj = lax.optimization_barrier((*far, proj))
    pieces, pieces_sib = pieces + far, pieces_sib + [swap(x) for x in far]
    partial = call(
        forward_kernel,
        jax.ShapeDtypeStruct((chips, 544, 128), BF16),
        [SMEM] + [VMEM] * (5 + 2 * (9 - EARLY)),
        [pltpu.VMEM((2 * n_fact, rows, width), BF16), pltpu.VMEM((chips + 1, block, width), F32)],
        flops=2 * slots * block * block * width,
        moved=8 << 20,
    )(info, proj, *pieces[EARLY:], *pieces_sib[EARLY:], w_tables, facts_t, tiles, tiles_sib)
    parts = by_chip(partial)

    fact_out, spread, facts_t = call(
        middle_kernel,
        (
            jax.ShapeDtypeStruct((block, width), BF16),
            jax.ShapeDtypeStruct((chips, width, block), BF16),
            jax.ShapeDtypeStruct((chips, width // chips, block), BF16),
        ),
        [VMEM] * 4,
        flops=2 * block * width * width,
        moved=5 << 20,
    )(parts, facts, w_self, cot)
    grads = by_chip(spread)

    keep, give_first, give_rest = call(
        backward_kernel,
        (
            jax.ShapeDtypeStruct((n_fact, 528, 128), F32),
            jax.ShapeDtypeStruct((len(FIRST), 528, 128), BF16),
            jax.ShapeDtypeStruct((len(REST), 528, 128), BF16),
        ),
        [SMEM] + [VMEM] * 4,
        [pltpu.VMEM((2 * n_fact + 1, width, block), F32), pltpu.VMEM((4, width // chips, 128), F32)],
        flops=2 * slots * block * block * width,
        moved=9 << 20,
    )(info, grads, facts_t, tiles, tiles_sib)
    give_first, give_rest = lax.optimization_barrier((swap(give_first), give_rest))
    give_rest = swap(give_rest)
    give = {k: give_first[at] for at, k in enumerate(FIRST)}

    def partial_sum(k, arrived):
        return (keep[k] + give[k].astype(F32) + arrived.astype(F32)).astype(BF16)

    up = shift((keep[3] + give[3].astype(F32)).astype(BF16), 1)
    down = shift((keep[5] + give[5].astype(F32)).astype(BF16), -1)
    give_rest, up, down = lax.optimization_barrier((give_rest, up, down))
    give |= {k: give_rest[at] for at, k in enumerate(REST)}
    far = shift((keep[4] + give[4].astype(F32)).astype(BF16), 4)
    for k in (2, 1):
        up, down = lax.optimization_barrier((partial_sum(k, up), partial_sum(8 - k, down)))
        up, down = shift(up, 1), shift(down, -1)

    tab, gsum, self_piece = call(
        slice_kernel,
        (
            jax.ShapeDtypeStruct((384, 128), BF16),
            jax.ShapeDtypeStruct((2 * n_fact, 32, 128), BF16),
            jax.ShapeDtypeStruct((8, 128), F32),
        ),
        [SMEM] + [VMEM] * 23,
        [pltpu.VMEM((3, 32, width), F32)],
        flops=4 * n_fact * 32 * 128 * width,
        moved=3 << 20,
    )(info, keep[0], give[0], up, down, far, *pieces, *pieces_sib)
    tab = by_chip(tab.reshape(chips, 24, 128))
    packed = call(
        pack_kernel, jax.ShapeDtypeStruct((n_fact, 96, 128), BF16), [SMEM] + [VMEM] * 3, moved=1 << 19
    )(info, tab, gsum, self_piece)
    packed = by_fact(packed)
    pieces_own = by_chip(jnp.broadcast_to(packed[None, :, 64:, :], (chips, n_fact, 32, 128)))
    given = swap(packed[:, 32:64, :])

    grad_dims, grad_self, grad_tab = pl.pallas_call(
        final_kernel,
        out_shape=(
            jax.ShapeDtypeStruct((rows, width), F32),
            jax.ShapeDtypeStruct((width, width), F32),
            jax.ShapeDtypeStruct((3, width, width), F32),
        ),
        grid=(4,),
        in_specs=[SMEM] + [VMEM] * 5,
        out_specs=(
            pl.BlockSpec((rows, width), lambda q: (0, 0)),
            pl.BlockSpec((width, 128), lambda q: (0, q)),
            pl.BlockSpec((3, 128, width), lambda q: (0, q, 0)),
        ),
        compiler_params=PARAMS,
        cost_estimate=pl.CostEstimate(flops=2 * rows * width * width, bytes_accessed=8 << 20, transcendentals=0),
    )(info, pieces_own, swap(pieces_own), packed[:, :32, :], given, w_tables)
    return (fact_out, grad_dims, grad_self, grad_tab)


def solution(mesh):
    split = P(("fact", "dim"), None)
    return jax.shard_map(
        body,
        mesh=mesh,
        in_specs=(split, split, P(("fact", "dim"), None, None), split, P(("fact", "dim")), P(), P(), P(), split),
        out_specs=(split, split, P(), P()),
        check_vma=False,
    )
```
